128 devices in a mesh: dp: 16 (over y_hi, z, core), seq: 8 (over x, y_lo).
Axes of the slice: x: 4, y: 4 (y_hi: 2, y_lo: 2; y = y_hi * 2 + y_lo), z: 4, core: 2. Of those that a mesh axis runs over, the one named last changes fastest.
Arguments:
- hidden_in: bfloat16 [32, 1024, 1024], P('dp', 'seq'), may hold values from -6 to 6
- out_cotangent: bfloat16 [32, 1024, 1024], P('dp', 'seq'), may hold values from -6 to 6
- slot_lengths: int32 [32], P('dp'), may hold values from 512 to 1024, as said below
- position_ids: int32 [32, 1024], P('dp', 'seq'), may hold values from 0 to 1534, as said below
- attn_gain: bfloat16 [1024], P('dp'), may hold values from 0.25 to 1.75
- w_query: bfloat16 [1024, 2048], P('dp'), may hold values from -0.1875 to 0.1875
- key_weight: bfloat16 [1024, 1024], P('dp'), may hold values from -0.1875 to 0.1875
- value_weight: bfloat16 [1024, 1024], P('dp'), may hold values from -0.1875 to 0.1875
- query_gain: bfloat16 [128], P('dp'), may hold values from 0.25 to 1.75
- key_gain: bfloat16 [128], P('dp'), may hold values from 0.25 to 1.75
- w_output: bfloat16 [2048, 1024], P('dp'), may hold values from -0.375 to 0.375
- ffn_gain: bfloat16 [1024], P('dp'), may hold values from 0.25 to 1.75
- w_gate: bfloat16 [1024, 3072], P('dp'), may hold values from -0.1875 to 0.1875
- w_up: bfloat16 [1024, 3072], P('dp'), may hold values from -0.1875 to 0.1875
- w_down: bfloat16 [3072, 1024], P('dp'), may hold values from -0.109375 to 0.109375
Outputs:
- layer_out: bfloat16 [32, 1024, 1024], P('dp', 'seq')
- input_grad: float32 [32, 1024, 1024], P('dp', 'seq')
- grad_attn_gain: float32 [1024], P('dp')
- grad_query: float32 [1024, 2048], P('dp')
- grad_key: float32 [1024, 1024], P('dp')
- grad_value: float32 [1024, 1024], P('dp')
- grad_query_gain: float32 [128], P('dp')
- grad_key_gain: float32 [128], P('dp')
- grad_output: float32 [2048, 1024], P('dp')
- grad_ffn_gain: float32 [1024], P('dp')
- grad_gate: float32 [1024, 3072], P('dp')
- grad_up: float32 [1024, 3072], P('dp')
- grad_down: float32 [3072, 1024], P('dp')
The draws below stay inside these ranges and needn't reach their ends.
Inputs may be any that keep to these rules, and one draw needn't show every extreme that they name: `slot_lengths`: in the 2 slots that one index of dp holds, one slot, which one drawn from the seed, is full. `position_ids`: in each slot positions start at 0 and rise by 1 or 2 from token to token; the last is 1534.
All inputs are finite; a program needn't handle non-finite values.
Results may differ from the reference program's by a relative error of at most 0.03.
Values may be sent and summed in bfloat16 or wider, within the bound.
A program may use at most 320 MiB of HBM per device.

```python
import math
import jax
import jax.numpy as jnp
from jax import lax

MODEL_WIDTH = 1024
HQ = 16
KEY_VALUE_HEADS = 8
HEAD_SIZE = 128
FF = 3072
SLOT = 1024
MB = 2
SLOTS = 32


def draw_slot_lengths(key, part):
    key = jax.random.fold_in(key, 11)
    first_key, second_key = jax.random.split(key)
    groups = SLOTS // MB
    drawn = jax.random.randint(first_key, (groups, MB), SLOT // 2, SLOT + 1)
    chosen = jax.random.randint(second_key, (groups, 1), 0, MB)
    drawn = jnp.where(jnp.arange(MB)[None, :] == chosen, SLOT, drawn)
    return drawn.reshape(SLOTS).astype(jnp.int32)


def draw_position_ids(key, part):
    key = jax.random.fold_in(key, 23)
    increments = jnp.where(jnp.arange(SLOT - 1) < SLOT // 2, 1, 2).astype(jnp.int32)
    slot_keys = jax.random.split(key, SLOTS)
    shuffled = jax.vmap(lambda one_key: jax.random.permutation(one_key, increments))(slot_keys)
    starts = jnp.zeros((SLOTS, 1), jnp.int32)
    return jnp.concatenate([starts, jnp.cumsum(shuffled, axis=1)], axis=1).astype(jnp.int32)


def level_of(stream_key, extent, cuts, smallest, largest):
    loudness, own = 1.0, jax.random.fold_in(stream_key, 6)
    for axis_at, parts in cuts:
        heights = jnp.exp(jax.random.uniform(jax.random.fold_in(own, axis_at), (parts,), jnp.float32, smallest / len(cuts), largest / len(cuts)))
        loudness = loudness * jnp.repeat(heights, extent[axis_at] // parts).reshape([-1 if axis == axis_at else 1 for axis in range(len(extent))])
    return loudness


def bell_draw(own_key, extent, width, limit, shards=(), held_as=jnp.bfloat16):
    values = width * jax.random.normal(own_key, extent, jnp.float32)
    if shards:
        values = values * level_of(own_key, extent, shards, -0.22, 0.18)
    return jnp.clip(values, -limit, limit).astype(held_as)


def setup_inputs(seed: int = 0) -> dict:
    keys = jax.random.split(jax.random.key(seed), 16)
    hidden_in = bell_draw(keys[0], (SLOTS, SLOT, MODEL_WIDTH), 1.0, 6.0, ((0, 16), (1, 8)))
    out_cotangent = bell_draw(keys[1], (SLOTS, SLOT, MODEL_WIDTH), 1.0, 6.0, ((0, 16), (1, 8)))
    slot_lengths = draw_slot_lengths(jax.random.fold_in(keys[15], 71), 0)
    position_ids = draw_position_ids(jax.random.fold_in(keys[15], 71), 0)
    attn_gain = jnp.clip(1.0 + 0.15 * jax.random.normal(keys[4], (MODEL_WIDTH,), jnp.float32), 0.25, 1.75).astype(jnp.bfloat16)
    w_query = bell_draw(keys[5], (MODEL_WIDTH, HQ * HEAD_SIZE), MODEL_WIDTH ** -0.5, 0.1875, ((0, 16),))
    key_weight = bell_draw(keys[6], (MODEL_WIDTH, KEY_VALUE_HEADS * HEAD_SIZE), MODEL_WIDTH ** -0.5, 0.1875, ((0, 16),))
    value_weight = bell_draw(keys[7], (MODEL_WIDTH, KEY_VALUE_HEADS * HEAD_SIZE), MODEL_WIDTH ** -0.5, 0.1875, ((0, 16),))
    query_gain = jnp.clip(1.0 + 0.15 * jax.random.normal(keys[8], (HEAD_SIZE,), jnp.float32), 0.25, 1.75).astype(jnp.bfloat16)
    key_gain = jnp.clip(1.0 + 0.15 * jax.random.normal(keys[9], (HEAD_SIZE,), jnp.float32), 0.25, 1.75).astype(jnp.bfloat16)
    w_output = bell_draw(keys[10], (HQ * HEAD_SIZE, MODEL_WIDTH), (HQ * HEAD_SIZE // 8) ** -0.5, 0.375, ((0, 16),))
    ffn_gain = jnp.clip(1.0 + 0.15 * jax.random.normal(keys[11], (MODEL_WIDTH,), jnp.float32), 0.25, 1.75).astype(jnp.bfloat16)
    w_gate = bell_draw(keys[12], (MODEL_WIDTH, FF), MODEL_WIDTH ** -0.5, 0.1875, ((0, 16),))
    w_up = bell_draw(keys[13], (MODEL_WIDTH, FF), MODEL_WIDTH ** -0.5, 0.1875, ((0, 16),))
    w_down = bell_draw(keys[14], (FF, MODEL_WIDTH), FF ** -0.5, 0.109375, ((0, 16),))
    return {"hidden_in": hidden_in, "out_cotangent": out_cotangent, "slot_lengths": slot_lengths, "position_ids": position_ids, "attn_gain": attn_gain, "w_query": w_query, "key_weight": key_weight, "value_weight": value_weight, "query_gain": query_gain, "key_gain": key_gain, "w_output": w_output, "ffn_gain": ffn_gain, "w_gate": w_gate, "w_up": w_up, "w_down": w_down}


epsilon = 1e-06
rope_base = 1000000.0

@jax.custom_vjp
def low(v):
    return lax.optimization_barrier(v.astype(jnp.bfloat16)).astype(jnp.float32)

@jax.custom_vjp
def low_back(v):
    return v

def low_keep(v):
    return (low(v), None)

def low_pass(kept, grad):
    return (grad,)

def back_keep(v):
    return (v, None)

def back_low(kept, grad):
    return (low(grad),)
low.defvjp(low_keep, low_pass)
low_back.defvjp(back_keep, back_low)

def rms_scale(values, gain_vec):
    return values * lax.rsqrt(lax.optimization_barrier(jnp.mean(values * values, axis=-1, keepdims=True)) + epsilon) * gain_vec

def rotary_tables(position_vector, head_width):
    half_width = head_width // 2
    frequency = jnp.exp(jnp.arange(half_width, dtype=jnp.float32) * (-2.0 * math.log(rope_base) / head_width))
    angles = position_vector.astype(jnp.float32)[:, None] * frequency[None, :]
    cos_half = jnp.cos(angles)
    sin_half = jnp.sin(angles)
    return (jnp.concatenate([cos_half, cos_half], axis=-1), jnp.concatenate([sin_half, sin_half], axis=-1))

def rotate_heads(values, cos_tab, sin_tab):
    half_width = values.shape[-1] // 2
    turned = jnp.concatenate([-values[..., half_width:], values[..., :half_width]], axis=-1)
    return values * cos_tab[:, None, :] + turned * sin_tab[:, None, :]

def head_norm_rope(flat_rows, gain_vec, cos_tab, sin_tab, head_count):
    shaped = flat_rows.reshape(flat_rows.shape[0], head_count, -1)
    return rotate_heads(rms_scale(shaped, gain_vec), cos_tab, sin_tab)

def gated_unit(gate_proj, up_proj):
    return jax.nn.silu(gate_proj) * up_proj

def matmul(left, right):
    return jnp.dot(left, right, precision=lax.Precision.HIGHEST, preferred_element_type=jnp.float32)

def attention(queries, keys_in, values_in):
    slot_len, q_count, head_width = queries.shape
    key_value_count = keys_in.shape[1]
    group_size = q_count // key_value_count
    block_len = min(512, slot_len)
    block_count = slot_len // block_len
    score_scale = head_width ** (-0.5)
    query_blocks = queries.reshape(block_count, block_len, key_value_count, group_size, head_width)
    block_starts = jnp.arange(block_count, dtype=jnp.int32) * block_len
    key_order = jnp.arange(slot_len, dtype=jnp.int32)

    def one_block(block_args):
        query_part, first_row = block_args
        raw_scores = jnp.einsum('qkgd,skd->kgqs', query_part, keys_in, precision=lax.Precision.HIGHEST)
        scores = low_back(raw_scores) * score_scale
        query_order = first_row + jnp.arange(block_len, dtype=jnp.int32)
        allowed = key_order[None, :] <= query_order[:, None]
        scores = jnp.where(allowed, scores, -1e+30)
        row_max = lax.optimization_barrier(jnp.max(scores, axis=-1, keepdims=True))
        shifted = jnp.exp(scores - row_max)
        prob_tab = shifted / lax.optimization_barrier(jnp.sum(shifted, axis=-1, keepdims=True))
        return jnp.einsum('kgqs,skd->qkgd', low(prob_tab), values_in, precision=lax.Precision.HIGHEST)
    attended = lax.map(jax.checkpoint(one_block), (query_blocks, block_starts))
    return attended.reshape(slot_len, q_count, head_width)

def layer_forward(params, x_rows, cos_tab, sin_tab, is_valid):
    g_attn, w_query, key_weight, value_weight, g_query, g_key, w_output, g_ffn, w_gate, w_up, w_down = params
    head_width = g_query.shape[0]
    q_count = w_query.shape[1] // head_width
    key_value_count = key_weight.shape[1] // head_width
    slot_len = x_rows.shape[0]
    x_in = low(rms_scale(x_rows, g_attn))
    query_flat = low_back(matmul(x_in, w_query))
    queries = low(low_back(head_norm_rope(query_flat, g_query, cos_tab, sin_tab, q_count)))
    key_flat = low_back(matmul(x_in, key_weight))
    keys_in = low(low_back(head_norm_rope(key_flat, g_key, cos_tab, sin_tab, key_value_count)))
    values_in = low(low_back(matmul(x_in, value_weight))).reshape(slot_len, key_value_count, head_width)
    attended = low(low_back(attention(queries, keys_in, values_in)))
    residual = x_rows + low_back(matmul(attended.reshape(slot_len, q_count * head_width), w_output))
    mid_in = low(rms_scale(residual, g_ffn))
    gate_proj = low_back(matmul(mid_in, w_gate))
    up_proj = low_back(matmul(mid_in, w_up))
    unit_in = low(gated_unit(gate_proj, up_proj))
    result = residual + low_back(matmul(unit_in, w_down))
    return jnp.where(is_valid[:, None], result, 0.0)

def reference(hidden_in, out_cotangent, slot_lengths, position_ids, attn_gain, w_query, key_weight, value_weight, query_gain, key_gain, w_output, ffn_gain, w_gate, w_up, w_down):
    params = tuple((weight_arr.astype(jnp.float32) for weight_arr in (attn_gain, w_query, key_weight, value_weight, query_gain, key_gain, w_output, ffn_gain, w_gate, w_up, w_down)))

    def slot_turn(totals, slot_args):
        x_slot, cot_slot, length_now, pos_slot = slot_args
        cos_tab, sin_tab = rotary_tables(pos_slot, HEAD_SIZE)
        is_valid = jnp.arange(SLOT, dtype=jnp.int32) < length_now
        result, pull_back = jax.vjp(lambda weights_in, rows_in: layer_forward(weights_in, rows_in, cos_tab, sin_tab, is_valid), params, x_slot.astype(jnp.float32))
        grad_params, grad_rows = pull_back(cot_slot.astype(jnp.float32))
        totals = jax.tree.map(jnp.add, totals, grad_params)
        return (totals, (result.astype(jnp.bfloat16), grad_rows))
    zero_grads = tuple((jnp.zeros(weight_arr.shape, jnp.float32) for weight_arr in params))
    totals, (out_rows, input_grad) = lax.scan(slot_turn, zero_grads, (hidden_in, out_cotangent, slot_lengths, position_ids))
    return (out_rows, input_grad, totals[0], totals[1], totals[2], totals[3], totals[4], totals[5], totals[6], totals[7], totals[8], totals[9], totals[10])
```

```python
import math

import jax
import jax.numpy as jnp
from jax import lax
from jax.sharding import PartitionSpec as P

epsilon = 1e-06
rope_base = 1000000.0
bf16 = jnp.bfloat16
f32 = jnp.float32


def product(left, right):
    return jnp.dot(left, right, preferred_element_type=f32)


def cross_rows(left, right):
    return lax.dot_general(left, right, (((0,), (0,)), ((), ())), preferred_element_type=f32)


def times_trans(left, right):
    return lax.dot_general(left, right, (((1,), (1,)), ((), ())), preferred_element_type=f32)


def rotary_tables(positions, width):
    half = width // 2
    frequency = jnp.exp(jnp.arange(half, dtype=f32) * (-2.0 * math.log(rope_base) / width))
    angles = positions.astype(f32)[:, None] * frequency[None, :]
    cos_half, sin_half = jnp.cos(angles), jnp.sin(angles)
    return (
        jnp.concatenate([cos_half, cos_half], axis=-1),
        jnp.concatenate([sin_half, sin_half], axis=-1),
    )


def turn(v):
    half = v.shape[-1] // 2
    return jnp.concatenate([-v[..., half:], v[..., :half]], axis=-1)


def turn_back(v):
    half = v.shape[-1] // 2
    return jnp.concatenate([v[..., half:], -v[..., :half]], axis=-1)


def inverse_rms(v):
    return lax.rsqrt(jnp.mean(v * v, axis=-1, keepdims=True) + epsilon)


def rms_back(v, gain, grad):
    r = inverse_rms(v)
    ge = gain * grad
    dv = r * ge - v * (r * r * r) * jnp.mean(v * ge, axis=-1, keepdims=True)
    return dv, grad * v * r


def attend_forward(q, k, v):
    rows, heads, width = q.shape
    kv = k.shape[1]
    q = q.reshape(rows, kv, heads // kv, width)
    scores = jnp.einsum("qkgd,skd->kgqs", q, k, preferred_element_type=f32) * width ** (-0.5)
    order = jnp.arange(rows, dtype=jnp.int32)
    scores = jnp.where(order[None, :] <= order[:, None], scores, -1e30)
    top = jnp.max(scores, axis=-1, keepdims=True)
    shifted = jnp.exp(scores - top)
    total = jnp.sum(shifted, axis=-1, keepdims=True)
    prob = (shifted / total).astype(bf16)
    out = jnp.einsum("kgqs,skd->qkgd", prob, v, preferred_element_type=f32)
    return out.astype(bf16).reshape(rows, heads, width), top + jnp.log(total)


def attend_backward(q, k, v, grad, lse):
    rows, heads, width = q.shape
    kv = k.shape[1]
    scale = width ** (-0.5)
    q = q.reshape(rows, kv, heads // kv, width)
    grad = grad.reshape(rows, kv, heads // kv, width)
    scores = jnp.einsum("qkgd,skd->kgqs", q, k, preferred_element_type=f32) * scale
    order = jnp.arange(rows, dtype=jnp.int32)
    scores = jnp.where(order[None, :] <= order[:, None], scores, -1e30)
    prob = jnp.exp(scores - lse)
    d_prob = jnp.einsum("qkgd,skd->kgqs", grad, v, preferred_element_type=f32)
    row_dot = jnp.sum(prob * d_prob, axis=-1, keepdims=True)
    d_score = (prob * (d_prob - row_dot) * scale).astype(bf16)
    dq = jnp.einsum("kgqs,skd->qkgd", d_score, k, preferred_element_type=f32)
    dk = jnp.einsum("kgqs,qkgd->skd", d_score, q, preferred_element_type=f32)
    dv = jnp.einsum("kgqs,qkgd->skd", prob.astype(bf16), grad, preferred_element_type=f32)
    return dq.astype(bf16).reshape(rows, heads, width), dk.astype(bf16), dv.astype(bf16)


def to_heads(rows_in, slots):
    parts = rows_in.reshape(slots, -1, rows_in.shape[1] // 128, 128)
    return lax.all_to_all(parts, "seq", split_axis=2, concat_axis=1, tiled=True)


def to_rows(heads_in):
    out = lax.all_to_all(heads_in, "seq", split_axis=1, concat_axis=2, tiled=True)
    return out.reshape(out.shape[0] * out.shape[1], -1)


def layer(hidden, cotangent, lengths, positions, gains, weights):
    g_attn, g_query, g_key, g_ffn = [g.astype(f32) for g in gains]
    w_query, w_key, w_value, w_output, w_gate, w_up, w_down = weights
    slots, tokens, width = hidden.shape
    rows = slots * tokens
    head = g_query.shape[0]
    hq, hkv = w_query.shape[1] // head, w_key.shape[1] // head
    index = lax.axis_index("seq") * tokens + jnp.arange(tokens, dtype=jnp.int32)
    valid = (index[None, :] < lengths[:, None]).reshape(rows, 1)
    cos, sin = rotary_tables(positions.reshape(rows), head)
    cos, sin = cos[:, None, :], sin[:, None, :]
    x = hidden.reshape(rows, width).astype(f32)
    x_in = (x * inverse_rms(x) * g_attn).astype(bf16)
    q_flat = product(x_in, w_query).reshape(rows, hq, head)
    k_flat = product(x_in, w_key).reshape(rows, hkv, head)
    v_rows = product(x_in, w_value).astype(bf16)

    def rope(v):
        return v * cos + turn(v) * sin

    q_rows = rope(q_flat * inverse_rms(q_flat) * g_query).astype(bf16).reshape(rows, -1)
    k_rows = rope(k_flat * inverse_rms(k_flat) * g_key).astype(bf16).reshape(rows, -1)
    q, k, v = to_heads(q_rows, slots), to_heads(k_rows, slots), to_heads(v_rows, slots)
    attended, lse = zip(*[attend_forward(q[i], k[i], v[i]) for i in range(slots)])
    context = to_rows(jnp.stack(attended))
    residual = x + product(context, w_output)
    mid_in = (residual * inverse_rms(residual) * g_ffn).astype(bf16)
    gate, up = product(mid_in, w_gate), product(mid_in, w_up)
    sig = 1.0 / (1.0 + jnp.exp(-gate))
    silu = gate * sig
    unit = (silu * up).astype(bf16)
    result = residual + product(unit, w_down)
    out = jnp.where(valid, result, 0.0).astype(bf16)
    d_result = jnp.where(valid, cotangent.reshape(rows, width).astype(f32), 0.0)
    d_branch = d_result.astype(bf16)
    grad_down = cross_rows(unit, d_branch)
    d_unit = times_trans(d_branch, w_down)
    d_gate = (d_unit * up * sig * (1.0 + gate * (1.0 - sig))).astype(bf16)
    d_up = (d_unit * silu).astype(bf16)
    grad_gate, grad_up = cross_rows(mid_in, d_gate), cross_rows(mid_in, d_up)
    d_mid = times_trans(d_gate, w_gate) + times_trans(d_up, w_up)
    dv_mid, dg_ffn = rms_back(residual, g_ffn, d_mid)
    d_residual = d_result + dv_mid
    d_attn = d_residual.astype(bf16)
    grad_output = cross_rows(context, d_attn)
    d_attended = times_trans(d_attn, w_output).astype(bf16)
    grad_heads = to_heads(d_attended, slots)
    back = [attend_backward(q[i], k[i], v[i], grad_heads[i], lse[i]) for i in range(slots)]
    dq, dk, dv = [to_rows(jnp.stack(part)) for part in zip(*back)]

    def head_back(flat, gain, grad):
        grad = grad.reshape(flat.shape).astype(f32)
        grad = grad * cos + turn_back(grad * sin)
        d_flat, dg = rms_back(flat, gain, grad)
        return d_flat.astype(bf16).reshape(rows, -1), jnp.sum(dg, axis=(0, 1))

    d_query, dg_query = head_back(q_flat, g_query, dq)
    d_key, dg_key = head_back(k_flat, g_key, dk)
    grad_query, grad_key, grad_value = (
        cross_rows(x_in, d_query),
        cross_rows(x_in, d_key),
        cross_rows(x_in, dv),
    )
    d_x_in = (
        times_trans(d_query, w_query) + times_trans(d_key, w_key) + times_trans(dv, w_value)
    )
    dv_x, dg_attn = rms_back(x, g_attn, d_x_in)
    d_input = d_residual + dv_x
    gain_grads = (jnp.sum(dg_attn, axis=0), dg_query, dg_key, jnp.sum(dg_ffn, axis=0))
    weight_grads = (
        grad_query,
        grad_key,
        grad_value,
        grad_output,
        grad_gate,
        grad_up,
        grad_down,
    )
    shape = (slots, tokens, width)
    return out.reshape(shape), d_input.reshape(shape), gain_grads, weight_grads


def per_device(
    hidden_in,
    out_cotangent,
    slot_lengths,
    position_ids,
    attn_gain,
    w_query,
    key_weight,
    value_weight,
    query_gain,
    key_gain,
    w_output,
    ffn_gain,
    w_gate,
    w_up,
    w_down,
):
    def gather(shard):
        return lax.all_gather(shard, "dp", axis=0, tiled=True)

    gains = [gather(g) for g in (attn_gain, query_gain, key_gain, ffn_gain)]
    shards = (w_query, key_weight, value_weight, w_output, w_gate, w_up, w_down)
    weights = [gather(w) for w in shards]
    out, d_input, gain_grads, weight_grads = layer(
        hidden_in, out_cotangent, slot_lengths, position_ids, gains, weights
    )

    def owned(part):
        part = lax.psum_scatter(part.astype(bf16), "dp", scatter_dimension=0, tiled=True)
        return lax.psum(part, "seq").astype(f32)

    dg_attn, dg_query, dg_key, dg_ffn = [owned(g) for g in gain_grads]
    gq, gk, gv, go, gg, gu, gd = [owned(g) for g in weight_grads]
    return (out, d_input, dg_attn, gq, gk, gv, dg_query, dg_key, go, dg_ffn, gg, gu, gd)


def solution(mesh):
    slots, rows, vector, matrix = P("dp", "seq", None), P("dp", "seq"), P("dp"), P("dp", None)
    in_specs = (
        slots,
        slots,
        vector,
        rows,
        vector,
        matrix,
        matrix,
        matrix,
        vector,
        vector,
        matrix,
        vector,
        matrix,
        matrix,
        matrix,
    )
    out_specs = (
        slots,
        slots,
        vector,
        matrix,
        matrix,
        matrix,
        vector,
        vector,
        matrix,
        vector,
        matrix,
        matrix,
        matrix,
    )
    return jax.shard_map(
        per_device, mesh=mesh, in_specs=in_specs, out_specs=out_specs, check_vma=False
    )
```

```python
import functools
import math

import jax
import jax.numpy as jnp
from jax import lax
from jax.experimental import pallas as pl
from jax.experimental.pallas import tpu as pltpu
from jax.sharding import PartitionSpec as P

epsilon = 1e-06
rope_base = 1000000.0
bf16 = jnp.bfloat16
f32 = jnp.float32


MESH = pl.DeviceIdType.MESH
SHARD_ROWS = (64, 128, 64, 192)
COLUMNS = (4096, 1024, 6144, 1024)
THIRDS = ((640, 640, 768), (256, 128, 128), (1024, 1024, 1024), (128, 256, 128))


class Place:
    def __init__(self):
        dp, seq = lax.axis_index("dp"), lax.axis_index("seq")
        x, y_lo = seq // 2, seq % 2
        y_hi, z, core = dp // 8, (dp // 2) % 4, dp % 2
        self.dp, self.seq, self.x, self.y_lo = dp, seq, x, y_lo
        self.y_hi, self.z, self.core = y_hi, z, core
        self.z_up, self.z_down, self.z_far = (z + 1) % 4, (z + 3) % 4, (z + 2) % 4
        self.color = (x + y_lo + y_hi) % 2
        self.to_z_up = (y_hi * 8 + self.z_up * 2 + core, seq)
        self.to_z_down = (y_hi * 8 + self.z_down * 2 + core, seq)
        self.to_x_up = (dp, ((x + 1) % 4) * 2 + y_lo)
        self.to_x_down = (dp, ((x + 3) % 4) * 2 + y_lo)
        self.to_pair = (dp, x * 2 + 1 - y_lo)
        self.to_cross = ((1 - y_hi) * 8 + z * 2 + core, x * 2 + 1 - y_lo)
        self.to_core = (y_hi * 8 + z * 2 + 1 - core, seq)

    def torus(self):
        return (
            self.to_z_up,
            self.to_z_down,
            self.to_x_up,
            self.to_x_down,
            self.to_pair,
            self.to_cross,
            self.to_core,
        )


def greet(peers):
    barrier = pltpu.get_barrier_semaphore()
    for peer in peers:
        pl.semaphore_signal(barrier, inc=1, device_id=peer, device_id_type=MESH)
    pl.semaphore_wait(barrier, len(peers))


GATHER_KINDS = (
    "own_up",
    "own_down",
    "on_up",
    "on_down",
    "cross_own",
    "cross_up",
    "cross_down",
    "cross_far",
    "other_up",
    "other_down",
    "other_on_up",
    "other_on_down",
) + tuple(f"share_{n}_{s}" for n in range(3) for s in ("up", "down", "far", "other"))
GATHER_KINDS += tuple(f"core_{s}" for s in ("own", "up", "down", "far", "other"))
KIND_AT = {kind: at for at, kind in enumerate(GATHER_KINDS)}
KINDS = len(GATHER_KINDS)


class Gather:
    def __init__(self, place, buffers, send_sem, recv_sem):
        self.place, self.buffers, self.send_sem, self.recv_sem = place, buffers, send_sem, recv_sem
        self.sent = []

    def region(self, g, kind, receiving):
        p = self.place
        rows, cols = SHARD_ROWS[g], COLUMNS[g]
        half = cols // 2
        here, there = p.y_hi, 1 - p.y_hi
        whole, top, low = pl.ds(0, rows), pl.ds(0, rows // 2), pl.ds(rows // 2, rows // 2)
        low_first = pl.ds(rows // 2, rows // 4)
        low_last = pl.ds(rows // 2 + rows // 4, rows // 4)
        color = p.color
        if kind.startswith("share") and receiving:
            color = 1 - color
        first = color * half
        mine = pl.ds(pl.multiple_of(first, 128), half)
        below, above = p.z_down, p.z_up
        z, far = p.z, p.z_far
        buf = self.buffers[g]

        def at(y, zz, r, c):
            return buf.at[y, zz, p.core, r, c]

        if kind == "own_up":
            return at(here, below if receiving else z, whole, mine), p.to_z_up
        if kind == "own_down":
            return at(here, above if receiving else z, whole, mine), p.to_z_down
        if kind == "on_up":
            return at(here, far if receiving else below, top, mine), p.to_z_up
        if kind == "on_down":
            return at(here, far if receiving else above, low, mine), p.to_z_down
        if kind.startswith("cross"):
            y = there if receiving else here
            which = kind[6:]
            if which == "own":
                return at(y, z, whole, mine), p.to_cross
            return at(y, {"up": above, "down": below, "far": far}[which], top, mine), p.to_cross
        if kind == "other_up":
            return at(there, below if receiving else z, low, mine), p.to_z_up
        if kind == "other_down":
            return at(there, above if receiving else z, low, mine), p.to_z_down
        if kind == "other_on_up":
            return at(there, far if receiving else below, low_first, mine), p.to_z_up
        if kind == "other_on_down":
            return at(there, far if receiving else above, low_last, mine), p.to_z_down
        if kind.startswith("share"):
            _, n, which = kind.split("_")
            n = int(n)
            start = sum(THIRDS[g][:n])
            part = pl.ds(pl.multiple_of(first + start, 128), THIRDS[g][n])
            to = (p.to_x_up, p.to_x_down, p.to_pair)[n]
            if which == "other":
                return buf.at[there, :, p.core, :, part], to
            return at(here, {"up": above, "down": below, "far": far}[which], whole, part), to
        which = kind[5:]
        core = 1 - p.core if receiving else p.core
        if which == "other":
            return buf.at[there, :, core], p.to_core
        return buf.at[here, {"own": z, "up": above, "down": below, "far": far}[which], core], p.to_core

    def copy(self, g, kind, receiving=False):
        region, to = self.region(g, kind, receiving)
        at = KIND_AT[kind]
        return pltpu.make_async_remote_copy(
            src_ref=region,
            dst_ref=region,
            send_sem=self.send_sem.at[g, at],
            recv_sem=self.recv_sem.at[g, at],
            device_id=to,
            device_id_type=MESH,
        )

    def send(self, g, *kinds):
        for kind in kinds:
            self.copy(g, kind).start()
            self.sent.append((g, kind))

    def take(self, g, *kinds):
        for kind in kinds:
            self.copy(g, kind, True).wait_recv()

    def share(self, g, which):
        self.send(g, *(f"share_{n}_{which}" for n in range(3)))

    def taken(self, g, which):
        self.take(g, *(f"share_{n}_{which}" for n in range(3)))

    def phase(self, number, g):
        if number == 0:
            self.send(g, "own_up", "own_down", "cross_own", "core_own")
        elif number == 1:
            self.take(g, "own_up", "own_down")
            self.send(g, "on_up", "on_down", "cross_up", "cross_down")
            self.share(g, "up")
            self.share(g, "down")
        elif number == 2:
            self.take(g, "cross_own")
            self.send(g, "other_up", "other_down")
            self.take(g, "on_up", "on_down")
            self.send(g, "cross_far")
            self.share(g, "far")
        elif number == 3:
            self.take(g, "other_up", "other_down")
            self.send(g, "other_on_up", "other_on_down")
        elif number == 4:
            self.take(g, "cross_up", "cross_down", "cross_far", "other_on_up", "other_on_down")
            self.share(g, "other")
        elif number == 5:
            for which in ("up", "down", "far"):
                self.taken(g, which)
                self.send(g, f"core_{which}")
        elif number == 6:
            self.taken(g, "other")
            self.send(g, "core_other")
        else:
            self.take(g, "core_own", "core_up", "core_down", "core_far", "core_other")

    def finish(self):
        for g, kind in self.sent:
            self.copy(g, kind).wait_send()
        self.sent = []


def own_places(place, buffers):
    mine = [buf.at[place.y_hi, place.z, place.core] for buf in buffers]
    return (
        mine[0].at[:, pl.ds(0, 2048)],
        mine[0].at[:, pl.ds(2048, 1024)],
        mine[0].at[:, pl.ds(3072, 1024)],
        mine[1],
        mine[2].at[:, pl.ds(0, 3072)],
        mine[2].at[:, pl.ds(3072, 3072)],
        mine[3],
    )


class GatherSmall:
    def __init__(self, place, buffer, send_sem, recv_sem):
        self.place, self.buffer, self.send_sem, self.recv_sem = place, buffer, send_sem, recv_sem

    def copy(self, step, receiving=False):
        p, buf = self.place, self.buffer
        if step == 0:
            region, to = buf.at[p.y_hi, p.z, 1 - p.core if receiving else p.core], p.to_core
        elif step == 1:
            region, to = buf.at[1 - p.y_hi if receiving else p.y_hi, p.z], p.to_cross
        elif step == 2:
            region, to = buf.at[:, p.z_down if receiving else p.z], p.to_z_up
        elif step == 3:
            region, to = buf.at[:, p.z_up if receiving else p.z], p.to_z_down
        else:
            region, to = buf.at[:, p.z_far if receiving else p.z_down], p.to_z_up
        return pltpu.make_async_remote_copy(
            src_ref=region,
            dst_ref=region,
            send_sem=self.send_sem.at[step],
            recv_sem=self.recv_sem.at[step],
            device_id=to,
            device_id_type=MESH,
        )

    def start(self, step):
        self.copy(step).start()

    def take(self, step):
        self.copy(step, True).wait_recv()

    def finish(self):
        for step in range(5):
            self.copy(step).wait_send()


ORDER = (
    (0, 0),
    (0, 1),
    (1, 0),
    (2, 0),
    (0, 2),
    (3, 0),
    (1, 1),
    (4, 0),
    (2, 1),
    (5, 0),
    (3, 1),
    (0, 3),
    (1, 2),
    (4, 1),
    (6, 0),
    (2, 2),
    (5, 1),
    (3, 2),
    (1, 3),
    (4, 2),
    (6, 1),
    (2, 3),
    (5, 2),
    (3, 3),
    (4, 3),
    (6, 2),
    (5, 3),
    (6, 3),
    (7, 0),
    (7, 1),
    (7, 2),
    (7, 3),
)


def gather_kernel(*refs):
    shards, small = refs[:7], refs[7]
    buffers, small_all = refs[8:12], refs[12]
    send_sem, recv_sem, small_send, small_recv, local_sem = refs[13:]
    place = Place()
    copies = [
        pltpu.make_async_copy(shard, there, local_sem.at[at])
        for at, (shard, there) in enumerate(
            zip(shards + (small,), own_places(place, buffers) + (small_all.at[place.y_hi, place.z, place.core],))
        )
    ]
    for copy in copies:
        copy.start()
    greet(place.torus())
    for copy in copies:
        copy.wait()
    gather = Gather(place, buffers, send_sem, recv_sem)
    little = GatherSmall(place, small_all, small_send, small_recv)
    little.start(0)
    gather.phase(0, 0)
    little.take(0)
    little.start(1)
    gather.phase(0, 1)
    little.take(1)
    little.start(2)
    little.start(3)
    little.take(2)
    little.take(3)
    little.start(4)
    for number, g in ORDER[2:]:
        gather.phase(number, g)
    little.take(4)
    gather.finish()
    little.finish()


def gather_all(shards, small):
    shapes = [
        jax.ShapeDtypeStruct((2, 4, 2, rows, cols), bf16) for rows, cols in zip(SHARD_ROWS, COLUMNS)
    ] + [jax.ShapeDtypeStruct((2, 4, 2, 16, 128), bf16)]
    return pl.pallas_call(
        functools.partial(gather_kernel),
        out_shape=shapes,
        in_specs=[pl.BlockSpec(memory_space=pltpu.VMEM)] * 8,
        out_specs=[pl.BlockSpec(memory_space=pl.ANY)] * 5,
        scratch_shapes=[
            pltpu.SemaphoreType.DMA((4, KINDS)),
            pltpu.SemaphoreType.DMA((4, KINDS)),
            pltpu.SemaphoreType.DMA((5,)),
            pltpu.SemaphoreType.DMA((5,)),
            pltpu.SemaphoreType.DMA((8,)),
        ],
        compiler_params=pltpu.CompilerParams(collective_id=1, has_side_effects=True),
        name="gather_weights",
    )(*shards, small)


PART_ORDER = ("xyz", "yzx", "zxy")
FREE = ((("yl", "yh", "z"), ("z",), ()), (("z", "x"), ("x",), ()), (("yl", "yh", "x"), ("yl", "yh"), ()))
EXTENT = {"yl": 2, "yh": 2, "z": 4, "x": 4}


def half_shape(part, step):
    free = FREE[part][step]
    first = EXTENT[free[0]] // 2
    return ((first,) if first > 1 else ()) + tuple(EXTENT[d] for d in free[1:])


def near_shape(part, step):
    return tuple(EXTENT[d] for d in FREE[part][step])


def reduce_scratch():
    shapes = []
    for g in range(4):
        rows, half = SHARD_ROWS[g] // 4, COLUMNS[g] // 2
        shapes.append(pltpu.VMEM((2, 2, 4, 4, rows, half), bf16))
        shapes.append(pltpu.VMEM((2, 2, 4, 4, rows, half), bf16))
        shapes.append(pltpu.VMEM((2, 4, rows, half), bf16))
        for part in range(3):
            tail = (rows, THIRDS[g][part])
            for step in range(3):
                if step < 2:
                    shapes.append(pltpu.VMEM((2,) + half_shape(part, step) + tail, bf16))
                else:
                    shapes.append(pltpu.VMEM((1,) + tail, bf16))
                shapes.append(pltpu.VMEM((2,) + near_shape(part, step) + tail, bf16))
    return shapes


SCRATCH_PER_GROUP = 3 + 18
REDUCE_SEMS = 3 * 12 + 1 + 1 + 2 + 2


def accumulate(dst, src):
    lead = dst.shape[:-2]
    count = 1
    for n in lead:
        count *= n
    if not lead:
        dst[...] = dst[...] + src[...]
        return

    def body(i, carry):
        at, rest = [], i
        for n in reversed(lead):
            at.append(rest % n)
            rest = rest // n
        at = tuple(reversed(at))
        dst.at[at][...] = dst.at[at][...] + src.at[at][...]
        return carry

    lax.fori_loop(0, count, body, 0)


class Reduce:
    def __init__(self, place, grads, scratch, send_sem, recv_sem, load_sem):
        self.place, self.grads = place, grads
        self.send_sem, self.recv_sem, self.load_sem = send_sem, recv_sem, load_sem
        self.sent = []
        self.groups = [scratch[g * SCRATCH_PER_GROUP : (g + 1) * SCRATCH_PER_GROUP] for g in range(4)]

    def total(self, g):
        return self.groups[g][0]

    def from_core(self, g):
        return self.groups[g][1]

    def result(self, g):
        return self.groups[g][2]

    def halves(self, g, part, step):
        return self.groups[g][3 + (part * 3 + step) * 2]

    def nears(self, g, part, step):
        return self.groups[g][4 + (part * 3 + step) * 2]

    def cols(self, g, part):
        return pl.ds(sum(THIRDS[g][:part]), THIRDS[g][part])

    def moved(self, dim, by):
        p = self.place
        if dim == "x":
            x = (p.x + by) % 4
            return {"x": x}, (p.dp, x * 2 + p.y_lo)
        if dim == "z":
            z = (p.z + by) % 4
            return {"z": z}, (p.y_hi * 8 + z * 2 + p.core, p.seq)
        y = (p.y_hi * 2 + p.y_lo + by) % 4
        return {"yl": y % 2, "yh": y // 2}, ((y // 2) * 8 + p.z * 2 + p.core, p.x * 2 + y % 2)

    def chunk(self, g, part, step, by, half=None):
        at = {}
        for earlier in range(step):
            at.update(self.moved(PART_ORDER[part][earlier], 0)[0])
        at.update(self.moved(PART_ORDER[part][step], by)[0])
        if half is not None:
            cut = FREE[part][step][0]
            size = EXTENT[cut] // 2
            at[cut] = half if size == 1 else pl.ds(half * size, size)
        index = tuple(at.get(name, slice(None)) for name in ("yl", "yh", "z", "x"))
        return self.total(g).at[index + (slice(None), self.cols(g, part))]

    def remote(self, g, sem, src, dst, to):
        return pltpu.make_async_remote_copy(
            src_ref=src,
            dst_ref=dst,
            send_sem=self.send_sem.at[g, sem],
            recv_sem=self.recv_sem.at[g, sem],
            device_id=to,
            device_id_type=MESH,
        )

    def send(self, g, sem, src, dst, to):
        copy = self.remote(g, sem, src, dst, to)
        copy.start()
        self.sent.append(copy)

    def take(self, g, sem, dst):
        self.remote(g, sem, dst, dst, self.place.to_core).wait_recv()

    def begin(self, g):
        p = self.place
        self.send(g, 36, self.grads[g].at[:, :, :, 1 - p.core], self.from_core(g), p.to_core)
        self.load(g).start()

    def load(self, g):
        return pltpu.make_async_copy(self.grads[g].at[:, :, :, self.place.core], self.total(g), self.load_sem.at[g])

    def join_cores(self, g):
        self.load(g).wait()
        self.take(g, 36, self.from_core(g))
        accumulate(self.total(g), self.from_core(g))

    def send_far(self, g, step):
        for part in range(3):
            sem, dim = part * 12 + step * 4, PART_ORDER[part][step]
            buf = self.halves(g, part, step)
            up, down = self.moved(dim, 1)[1], self.moved(dim, 3)[1]
            if step < 2:
                self.send(g, sem, self.chunk(g, part, step, 2, 0), buf.at[0], up)
                self.send(g, sem + 1, self.chunk(g, part, step, 2, 1), buf.at[1], down)
            else:
                self.send(g, sem, self.chunk(g, part, step, 2), buf.at[0], up)

    def send_near(self, g, step):
        for part in range(3):
            sem, dim = part * 12 + step * 4, PART_ORDER[part][step]
            buf, near = self.halves(g, part, step), self.nears(g, part, step)
            up, down = self.moved(dim, 1)[1], self.moved(dim, 3)[1]
            self.take(g, sem, buf.at[0])
            accumulate(self.chunk(g, part, step, 1, 0 if step < 2 else None), buf.at[0])
            self.send(g, sem + 2, self.chunk(g, part, step, 1), near.at[0], up)
            if step < 2:
                self.take(g, sem + 1, buf.at[1])
                accumulate(self.chunk(g, part, step, 3, 1), buf.at[1])
            self.send(g, sem + 3, self.chunk(g, part, step, 3), near.at[1], down)

    def join_near(self, g, step):
        for part in range(3):
            sem, near = part * 12 + step * 4, self.nears(g, part, step)
            for way in range(2):
                self.take(g, sem + 2 + way, near.at[way])
                accumulate(self.chunk(g, part, step, 0), near.at[way])

    def stage(self, number, g):
        p = self.place
        result = self.result(g)
        if number == 0:
            self.join_cores(g)
            self.send_far(g, 0)
        elif number in (1, 3, 5):
            self.send_near(g, number // 2)
        elif number in (2, 4):
            self.join_near(g, number // 2 - 1)
            self.send_far(g, number // 2)
        elif number == 6:
            self.join_near(g, 2)
            result.at[p.y_lo, p.x][...] = self.total(g).at[p.y_lo, p.y_hi, p.z, p.x][...]
            mine = result.at[p.y_lo, p.x]
            self.send(g, 37, mine, mine, p.to_pair)
        elif number == 7:
            self.take(g, 37, result.at[1 - p.y_lo, p.x])
            mine = result.at[:, p.x]
            self.send(g, 38, mine, mine, p.to_x_up)
            self.send(g, 39, mine, mine, p.to_x_down)
        elif number == 8:
            below, above = (p.x + 3) % 4, (p.x + 1) % 4
            self.take(g, 38, result.at[:, below])
            self.send(g, 40, result.at[0, below], result.at[0, below], p.to_x_up)
            self.take(g, 39, result.at[:, above])
            self.send(g, 41, result.at[1, above], result.at[1, above], p.to_x_down)
        else:
            far = (p.x + 2) % 4
            self.take(g, 40, result.at[0, far])
            self.take(g, 41, result.at[1, far])

    def finish(self):
        for copy in self.sent:
            copy.wait_send()
        self.sent = []


class ReduceSmall:
    STEPS = (("core", 2), ("pair", 2), ("cross", 2), ("x", 4), ("z", 4))

    def __init__(self, place, slots, send_sem, recv_sem):
        self.place, self.slots, self.send_sem, self.recv_sem = place, slots, send_sem, recv_sem

    def peers(self, step):
        p = self.place
        name, count = self.STEPS[step]
        if count == 2:
            mine, to = {
                "core": (p.core, p.to_core),
                "pair": (p.y_lo, p.to_pair),
                "cross": (p.y_hi, p.to_cross),
            }[name]
            return mine, [(1 - mine, to)]
        if name == "x":
            return p.x, [((p.x + by) % 4, (p.dp, (p.x + by) % 4 * 2 + p.y_lo)) for by in (1, 2, 3)]
        return p.z, [
            ((p.z + by) % 4, (p.y_hi * 8 + (p.z + by) % 4 * 2 + p.core, p.seq)) for by in (1, 2, 3)
        ]

    def copies(self, step, receiving):
        mine, peers = self.peers(step)
        if receiving:
            peers = peers[::-1]
        for at, (place, to) in enumerate(peers):
            slot = self.slots.at[step, place if receiving else mine]
            yield pltpu.make_async_remote_copy(
                src_ref=slot,
                dst_ref=slot,
                send_sem=self.send_sem.at[step, at],
                recv_sem=self.recv_sem.at[step, at],
                device_id=to,
                device_id_type=MESH,
            )

    def put(self, step, values):
        mine, _ = self.peers(step)
        self.slots.at[step, mine][...] = values
        for copy in self.copies(step, False):
            copy.start()

    def sum(self, step):
        for copy in self.copies(step, True):
            copy.wait_recv()
        for copy in self.copies(step, False):
            copy.wait_send()
        total = self.slots[step, 0]
        for at in range(1, self.STEPS[step][1]):
            total = total + self.slots[step, at]
        return total


REDUCE_ORDER = (3, 2, 1, 0)


def reduce_kernel(*refs):
    grads, small = refs[:4], refs[4]
    outs, small_out = refs[5:9], refs[9]
    scratch = refs[10 : 10 + 4 * SCRATCH_PER_GROUP]
    slots, send_sem, recv_sem, load_sem, small_send, small_recv, out_sem = refs[10 + 4 * SCRATCH_PER_GROUP :]
    place = Place()
    greet(
        place.torus()
        + (
            (place.dp, (place.x + 2) % 4 * 2 + place.y_lo),
            (place.y_hi * 8 + place.z_far * 2 + place.core, place.seq),
        )
    )
    reduce = Reduce(place, grads, scratch, send_sem, recv_sem, load_sem)
    little = ReduceSmall(place, slots, small_send, small_recv)
    for g in REDUCE_ORDER:
        reduce.begin(g)
    little.put(0, small[...])
    for slot in range(4 + 9):
        for stage in range(10):
            if 0 <= slot - stage < 4:
                reduce.stage(stage, REDUCE_ORDER[slot - stage])
                if stage == 9:
                    g = REDUCE_ORDER[slot - stage]
                    pltpu.make_async_copy(reduce.result(g), outs[g], out_sem.at[g]).start()
        if slot < 4:
            little.put(slot + 1, little.sum(slot))
        elif slot == 4:
            small_out[...] = little.sum(4)
    reduce.finish()
    for g in range(4):
        pltpu.make_async_copy(reduce.result(g), outs[g], out_sem.at[g]).wait()


def reduce_all(grads, small):
    shapes = [
        jax.ShapeDtypeStruct((2, 4, rows // 4, cols // 2), bf16) for rows, cols in zip(SHARD_ROWS, COLUMNS)
    ] + [jax.ShapeDtypeStruct((24, 128), f32)]
    vmem = pl.BlockSpec(memory_space=pltpu.VMEM)
    hbm = pl.BlockSpec(memory_space=pl.ANY)
    return pl.pallas_call(
        functools.partial(reduce_kernel),
        out_shape=shapes,
        in_specs=[hbm] * 4 + [vmem],
        out_specs=[hbm] * 4 + [vmem],
        scratch_shapes=reduce_scratch()
        + [
            pltpu.VMEM((5, 4, 24, 128), f32),
            pltpu.SemaphoreType.DMA((4, REDUCE_SEMS)),
            pltpu.SemaphoreType.DMA((4, REDUCE_SEMS)),
            pltpu.SemaphoreType.DMA((4,)),
            pltpu.SemaphoreType.DMA((5, 3)),
            pltpu.SemaphoreType.DMA((5, 3)),
            pltpu.SemaphoreType.DMA((4,)),
        ],
        compiler_params=pltpu.CompilerParams(
            collective_id=2, has_side_effects=True, vmem_limit_bytes=60 * 1024 * 1024
        ),
        name="reduce_grads",
    )(*grads, small)


def product(left, right):
    return jnp.dot(left, right, preferred_element_type=f32)


def cross_rows(left, right):
    return lax.dot_general(left, right, (((0,), (0,)), ((), ())), preferred_element_type=f32)


def times_trans(left, right):
    return lax.dot_general(left, right, (((1,), (1,)), ((), ())), preferred_element_type=f32)


def rotary_tables(positions, width):
    half = width // 2
    frequency = jnp.exp(jnp.arange(half, dtype=f32) * (-2.0 * math.log(rope_base) / width))
    angles = positions.astype(f32)[:, None] * frequency[None, :]
    cos_half, sin_half = jnp.cos(angles), jnp.sin(angles)
    return (
        jnp.concatenate([cos_half, cos_half], axis=-1),
        jnp.concatenate([sin_half, sin_half], axis=-1),
    )


def turn(v):
    half = v.shape[-1] // 2
    return jnp.concatenate([-v[..., half:], v[..., :half]], axis=-1)


def turn_back(v):
    half = v.shape[-1] // 2
    return jnp.concatenate([v[..., half:], -v[..., :half]], axis=-1)


def inverse_rms(v):
    return lax.rsqrt(jnp.mean(v * v, axis=-1, keepdims=True) + epsilon)


def rms_back(v, gain, grad):
    r = inverse_rms(v)
    ge = gain * grad
    dv = r * ge - v * (r * r * r) * jnp.mean(v * ge, axis=-1, keepdims=True)
    return dv, grad * v * r


def attend_forward(q, k, v):
    rows, heads, width = q.shape
    kv = k.shape[1]
    q = q.reshape(rows, kv, heads // kv, width)
    scores = jnp.einsum("qkgd,skd->kgqs", q, k, preferred_element_type=f32) * width ** (-0.5)
    order = jnp.arange(rows, dtype=jnp.int32)
    scores = jnp.where(order[None, :] <= order[:, None], scores, -1e30)
    top = jnp.max(scores, axis=-1, keepdims=True)
    shifted = jnp.exp(scores - top)
    total = jnp.sum(shifted, axis=-1, keepdims=True)
    prob = (shifted / total).astype(bf16)
    out = jnp.einsum("kgqs,skd->qkgd", prob, v, preferred_element_type=f32)
    return out.astype(bf16).reshape(rows, heads, width), top + jnp.log(total)


def attend_backward(q, k, v, grad, lse):
    rows, heads, width = q.shape
    kv = k.shape[1]
    scale = width ** (-0.5)
    q = q.reshape(rows, kv, heads // kv, width)
    grad = grad.reshape(rows, kv, heads // kv, width)
    scores = jnp.einsum("qkgd,skd->kgqs", q, k, preferred_element_type=f32) * scale
    order = jnp.arange(rows, dtype=jnp.int32)
    scores = jnp.where(order[None, :] <= order[:, None], scores, -1e30)
    prob = jnp.exp(scores - lse)
    d_prob = jnp.einsum("qkgd,skd->kgqs", grad, v, preferred_element_type=f32)
    row_dot = jnp.sum(prob * d_prob, axis=-1, keepdims=True)
    d_score = (prob * (d_prob - row_dot) * scale).astype(bf16)
    dq = jnp.einsum("kgqs,skd->qkgd", d_score, k, preferred_element_type=f32)
    dk = jnp.einsum("kgqs,qkgd->skd", d_score, q, preferred_element_type=f32)
    dv = jnp.einsum("kgqs,qkgd->skd", prob.astype(bf16), grad, preferred_element_type=f32)
    return dq.astype(bf16).reshape(rows, heads, width), dk.astype(bf16), dv.astype(bf16)


def to_heads(rows_in, slots):
    parts = rows_in.reshape(slots, -1, rows_in.shape[1] // 128, 128)
    return lax.all_to_all(parts, "seq", split_axis=2, concat_axis=1, tiled=True)


def to_rows(heads_in):
    out = lax.all_to_all(heads_in, "seq", split_axis=1, concat_axis=2, tiled=True)
    return out.reshape(out.shape[0] * out.shape[1], -1)


def layer(hidden, cotangent, lengths, positions, gains, weights):
    g_attn, g_query, g_key, g_ffn = [g.astype(f32) for g in gains]
    w_query, w_key, w_value, w_output, w_gate, w_up, w_down = weights
    slots, tokens, width = hidden.shape
    rows = slots * tokens
    head = g_query.shape[0]
    hq, hkv = w_query.shape[1] // head, w_key.shape[1] // head
    index = lax.axis_index("seq") * tokens + jnp.arange(tokens, dtype=jnp.int32)
    valid = (index[None, :] < lengths[:, None]).reshape(rows, 1)
    cos, sin = rotary_tables(positions.reshape(rows), head)
    cos, sin = cos[:, None, :], sin[:, None, :]
    x = hidden.reshape(rows, width).astype(f32)
    x_in = (x * inverse_rms(x) * g_attn).astype(bf16)
    q_flat = product(x_in, w_query).reshape(rows, hq, head)
    k_flat = product(x_in, w_key).reshape(rows, hkv, head)
    v_rows = product(x_in, w_value).astype(bf16)

    def rope(v):
        return v * cos + turn(v) * sin

    q_rows = rope(q_flat * inverse_rms(q_flat) * g_query).astype(bf16).reshape(rows, -1)
    k_rows = rope(k_flat * inverse_rms(k_flat) * g_key).astype(bf16).reshape(rows, -1)
    q, k, v = to_heads(q_rows, slots), to_heads(k_rows, slots), to_heads(v_rows, slots)
    attended, lse = zip(*[attend_forward(q[i], k[i], v[i]) for i in range(slots)])
    context = to_rows(jnp.stack(attended))
    residual = x + product(context, w_output)
    mid_in = (residual * inverse_rms(residual) * g_ffn).astype(bf16)
    gate, up = product(mid_in, w_gate), product(mid_in, w_up)
    sig = 1.0 / (1.0 + jnp.exp(-gate))
    silu = gate * sig
    unit = (silu * up).astype(bf16)
    result = residual + product(unit, w_down)
    out = jnp.where(valid, result, 0.0).astype(bf16)
    d_result = jnp.where(valid, cotangent.reshape(rows, width).astype(f32), 0.0)
    d_branch = d_result.astype(bf16)
    grad_down = cross_rows(unit, d_branch)
    d_unit = times_trans(d_branch, w_down)
    d_gate = (d_unit * up * sig * (1.0 + gate * (1.0 - sig))).astype(bf16)
    d_up = (d_unit * silu).astype(bf16)
    grad_gate, grad_up = cross_rows(mid_in, d_gate), cross_rows(mid_in, d_up)
    d_mid = times_trans(d_gate, w_gate) + times_trans(d_up, w_up)
    dv_mid, dg_ffn = rms_back(residual, g_ffn, d_mid)
    d_residual = d_result + dv_mid
    d_attn = d_residual.astype(bf16)
    grad_output = cross_rows(context, d_attn)
    d_attended = times_trans(d_attn, w_output).astype(bf16)
    grad_heads = to_heads(d_attended, slots)
    back = [attend_backward(q[i], k[i], v[i], grad_heads[i], lse[i]) for i in range(slots)]
    dq, dk, dv = [to_rows(jnp.stack(part)) for part in zip(*back)]

    def head_back(flat, gain, grad):
        grad = grad.reshape(flat.shape).astype(f32)
        grad = grad * cos + turn_back(grad * sin)
        d_flat, dg = rms_back(flat, gain, grad)
        return d_flat.astype(bf16).reshape(rows, -1), jnp.sum(dg, axis=(0, 1))

    d_query, dg_query = head_back(q_flat, g_query, dq)
    d_key, dg_key = head_back(k_flat, g_key, dk)
    grad_query, grad_key, grad_value = (
        cross_rows(x_in, d_query),
        cross_rows(x_in, d_key),
        cross_rows(x_in, dv),
    )
    d_x_in = (
        times_trans(d_query, w_query) + times_trans(d_key, w_key) + times_trans(dv, w_value)
    )
    dv_x, dg_attn = rms_back(x, g_attn, d_x_in)
    d_input = d_residual + dv_x
    gain_grads = (jnp.sum(dg_attn, axis=0), dg_query, dg_key, jnp.sum(dg_ffn, axis=0))
    weight_grads = (
        grad_query,
        grad_key,
        grad_value,
        grad_output,
        grad_gate,
        grad_up,
        grad_down,
    )
    shape = (slots, tokens, width)
    return out.reshape(shape), d_input.reshape(shape), gain_grads, weight_grads


def per_device(
    hidden_in,
    out_cotangent,
    slot_lengths,
    position_ids,
    attn_gain,
    w_query,
    key_weight,
    value_weight,
    query_gain,
    key_gain,
    w_output,
    ffn_gain,
    w_gate,
    w_up,
    w_down,
):
    dp = lax.axis_index("dp")
    tile = jnp.zeros((16, 128), bf16)
    for row, (gain, lane) in enumerate(
        ((attn_gain, dp % 2 * 64), (query_gain, dp * 8), (key_gain, dp * 8), (ffn_gain, dp % 2 * 64))
    ):
        tile = lax.dynamic_update_slice(tile, gain[None, :], (row, lane))
    shards = (w_query, key_weight, value_weight, w_output, w_gate, w_up, w_down)
    qkv, output, gate_up, down, small = gather_all(shards, tile)
    qkv, gate_up = qkv.reshape(1024, 4096), gate_up.reshape(1024, 6144)
    weights = (
        qkv[:, :2048],
        qkv[:, 2048:3072],
        qkv[:, 3072:],
        output.reshape(2048, 1024),
        gate_up[:, :3072],
        gate_up[:, 3072:],
        down.reshape(3072, 1024),
    )
    small = small.astype(f32).reshape(8, 2, 16, 128)
    gains = (
        jnp.sum(small[:, :, 0], axis=1).reshape(1024),
        jnp.sum(small[:, :, 1], axis=(0, 1)),
        jnp.sum(small[:, :, 2], axis=(0, 1)),
        jnp.sum(small[:, :, 3], axis=1).reshape(1024),
    )
    out, d_input, gain_grads, weight_grads = layer(
        hidden_in, out_cotangent, slot_lengths, position_ids, gains, weights
    )

    gq, gk, gv, go, gg, gu, gd = [part.astype(bf16) for part in weight_grads]
    halves = (
        (gq, jnp.concatenate([gk, gv], axis=1)),
        (go[:, :512], go[:, 512:]),
        (gg, gu),
        (gd[:, :512], gd[:, 512:]),
    )
    grads = [
        jnp.stack(pair).reshape(2, 2, 4, 2, 4, rows // 4, cols // 2)
        for pair, rows, cols in zip(halves, SHARD_ROWS, COLUMNS)
    ]
    flat = jnp.concatenate(gain_grads)
    flat = jnp.pad(flat, (0, 24 * 128 - flat.shape[0])).reshape(24, 128)
    *sums, gains_sum = reduce_all(grads, flat)
    qkv, output, gate_up, down = [
        part.reshape(2, rows, cols // 2).astype(f32)
        for part, rows, cols in zip(sums, SHARD_ROWS, COLUMNS)
    ]
    gq, gk, gv, gg, gu = qkv[0], qkv[1, :, :1024], qkv[1, :, 1024:], gate_up[0], gate_up[1]
    go, gd = jnp.concatenate([output[0], output[1]], 1), jnp.concatenate([down[0], down[1]], 1)
    gains_sum = gains_sum.reshape(-1)
    dg_attn, dg_query, dg_key, dg_ffn = [
        lax.dynamic_slice(gains_sum, (start + dp * size,), (size,))
        for start, size in ((0, 64), (1024, 8), (1152, 8), (1280, 64))
    ]
    return (out, d_input, dg_attn, gq, gk, gv, dg_query, dg_key, go, dg_ffn, gg, gu, gd)


def solution(mesh):
    slots, rows, vector, matrix = P("dp", "seq", None), P("dp", "seq"), P("dp"), P("dp", None)
    in_specs = (
        slots,
        slots,
        vector,
        rows,
        vector,
        matrix,
        matrix,
        matrix,
        vector,
        vector,
        matrix,
        vector,
        matrix,
        matrix,
        matrix,
    )
    out_specs = (
        slots,
        slots,
        vector,
        matrix,
        matrix,
        matrix,
        vector,
        vector,
        matrix,
        vector,
        matrix,
        matrix,
        matrix,
    )
    return jax.shard_map(
        per_device, mesh=mesh, in_specs=in_specs, out_specs=out_specs, check_vma=False
    )
```

```python
import functools
import math

import jax
import jax.numpy as jnp
from jax import lax
from jax.experimental import pallas as pl
from jax.experimental.pallas import tpu as pltpu
from jax.sharding import PartitionSpec as P

epsilon = 1e-06
rope_base = 1000000.0
bf16 = jnp.bfloat16
f32 = jnp.float32


MESH = pl.DeviceIdType.MESH
SHARD_ROWS = (64, 128, 64, 192)
COLUMNS = (4096, 1024, 6144, 1024)
THIRDS = ((640, 640, 768), (256, 128, 128), (1024, 1024, 1024), (128, 256, 128))


class Place:
    def __init__(self):
        dp, seq = lax.axis_index("dp"), lax.axis_index("seq")
        x, y_lo = seq // 2, seq % 2
        y_hi, z, core = dp // 8, (dp // 2) % 4, dp % 2
        self.dp, self.seq, self.x, self.y_lo = dp, seq, x, y_lo
        self.y_hi, self.z, self.core = y_hi, z, core
        self.z_up, self.z_down, self.z_far = (z + 1) % 4, (z + 3) % 4, (z + 2) % 4
        self.color = (x + y_lo + y_hi) % 2
        self.to_z_up = (y_hi * 8 + self.z_up * 2 + core, seq)
        self.to_z_down = (y_hi * 8 + self.z_down * 2 + core, seq)
        self.to_x_up = (dp, ((x + 1) % 4) * 2 + y_lo)
        self.to_x_down = (dp, ((x + 3) % 4) * 2 + y_lo)
        self.to_pair = (dp, x * 2 + 1 - y_lo)
        self.to_cross = ((1 - y_hi) * 8 + z * 2 + core, x * 2 + 1 - y_lo)
        self.to_core = (y_hi * 8 + z * 2 + 1 - core, seq)

    def torus(self):
        return (
            self.to_z_up,
            self.to_z_down,
            self.to_x_up,
            self.to_x_down,
            self.to_pair,
            self.to_cross,
            self.to_core,
        )


def greet(peers):
    barrier = pltpu.get_barrier_semaphore()
    for peer in peers:
        pl.semaphore_signal(barrier, inc=1, device_id=peer, device_id_type=MESH)
    pl.semaphore_wait(barrier, len(peers))


GATHER_KINDS = (
    "own_up",
    "own_down",
    "on_up",
    "on_down",
    "cross_own",
    "cross_up",
    "cross_down",
    "cross_far",
    "other_up",
    "other_down",
    "other_on_up",
    "other_on_down",
) + tuple(f"share_{n}_{s}" for n in range(3) for s in ("up", "down", "far", "other"))
GATHER_KINDS += tuple(f"core_{s}" for s in ("own", "up", "down", "far", "other"))
KIND_AT = {kind: at for at, kind in enumerate(GATHER_KINDS)}
KINDS = len(GATHER_KINDS)


class Gather:
    def __init__(self, place, buffers, send_sem, recv_sem):
        self.place, self.buffers, self.send_sem, self.recv_sem = place, buffers, send_sem, recv_sem
        self.sent = []

    def region(self, g, kind, receiving):
        p = self.place
        rows, cols = SHARD_ROWS[g], COLUMNS[g]
        half = cols // 2
        here, there = p.y_hi, 1 - p.y_hi
        whole, top, low = pl.ds(0, rows), pl.ds(0, rows // 2), pl.ds(rows // 2, rows // 2)
        low_first = pl.ds(rows // 2, rows // 4)
        low_last = pl.ds(rows // 2 + rows // 4, rows // 4)
        color = p.color
        if kind.startswith("share") and receiving:
            color = 1 - color
        first = color * half
        mine = pl.ds(pl.multiple_of(first, 128), half)
        below, above = p.z_down, p.z_up
        z, far = p.z, p.z_far
        buf = self.buffers[g]

        def at(y, zz, r, c):
            return buf.at[y, zz, p.core, r, c]

        if kind == "own_up":
            return at(here, below if receiving else z, whole, mine), p.to_z_up
        if kind == "own_down":
            return at(here, above if receiving else z, whole, mine), p.to_z_down
        if kind == "on_up":
            return at(here, far if receiving else below, top, mine), p.to_z_up
        if kind == "on_down":
            return at(here, far if receiving else above, low, mine), p.to_z_down
        if kind.startswith("cross"):
            y = there if receiving else here
            which = kind[6:]
            if which == "own":
                return at(y, z, whole, mine), p.to_cross
            return at(y, {"up": above, "down": below, "far": far}[which], top, mine), p.to_cross
        if kind == "other_up":
            return at(there, below if receiving else z, low, mine), p.to_z_up
        if kind == "other_down":
            return at(there, above if receiving else z, low, mine), p.to_z_down
        if kind == "other_on_up":
            return at(there, far if receiving else below, low_first, mine), p.to_z_up
        if kind == "other_on_down":
            return at(there, far if receiving else above, low_last, mine), p.to_z_down
        if kind.startswith("share"):
            _, n, which = kind.split("_")
            n = int(n)
            start = sum(THIRDS[g][:n])
            part = pl.ds(pl.multiple_of(first + start, 128), THIRDS[g][n])
            to = (p.to_x_up, p.to_x_down, p.to_pair)[n]
            if which == "other":
                return buf.at[there, :, p.core, :, part], to
            return at(here, {"up": above, "down": below, "far": far}[which], whole, part), to
        which = kind[5:]
        core = 1 - p.core if receiving else p.core
        if which == "other":
            return buf.at[there, :, core], p.to_core
        return buf.at[here, {"own": z, "up": above, "down": below, "far": far}[which], core], p.to_core

    def copy(self, g, kind, receiving=False):
        region, to = self.region(g, kind, receiving)
        at = KIND_AT[kind]
        return pltpu.make_async_remote_copy(
            src_ref=region,
            dst_ref=region,
            send_sem=self.send_sem.at[g, at],
            recv_sem=self.recv_sem.at[g, at],
            device_id=to,
            device_id_type=MESH,
        )

    def send(self, g, *kinds):
        for kind in kinds:
            self.copy(g, kind).start()
            self.sent.append((g, kind))

    def take(self, g, *kinds):
        for kind in kinds:
            self.copy(g, kind, True).wait_recv()

    def share(self, g, which):
        self.send(g, *(f"share_{n}_{which}" for n in range(3)))

    def taken(self, g, which):
        self.take(g, *(f"share_{n}_{which}" for n in range(3)))

    def phase(self, number, g):
        if number == 0:
            self.send(g, "own_up", "own_down", "cross_own", "core_own")
        elif number == 1:
            self.take(g, "own_up", "own_down")
            self.send(g, "on_up", "on_down", "cross_up", "cross_down")
            self.share(g, "up")
            self.share(g, "down")
        elif number == 2:
            self.take(g, "cross_own")
            self.send(g, "other_up", "other_down")
            self.take(g, "on_up", "on_down")
            self.send(g, "cross_far")
            self.share(g, "far")
        elif number == 3:
            self.take(g, "other_up", "other_down")
            self.send(g, "other_on_up", "other_on_down")
        elif number == 4:
            self.take(g, "cross_up", "cross_down", "cross_far", "other_on_up", "other_on_down")
            self.share(g, "other")
        elif number == 5:
            for which in ("up", "down", "far"):
                self.taken(g, which)
                self.send(g, f"core_{which}")
        elif number == 6:
            self.taken(g, "other")
            self.send(g, "core_other")
        else:
            self.take(g, "core_own", "core_up", "core_down", "core_far", "core_other")

    def finish(self):
        for g, kind in self.sent:
            self.copy(g, kind).wait_send()
        self.sent = []


def own_places(place, buffers):
    mine = [buf.at[place.y_hi, place.z, place.core] for buf in buffers]
    return (
        mine[0].at[:, pl.ds(0, 2048)],
        mine[0].at[:, pl.ds(2048, 1024)],
        mine[0].at[:, pl.ds(3072, 1024)],
        mine[1],
        mine[2].at[:, pl.ds(0, 3072)],
        mine[2].at[:, pl.ds(3072, 3072)],
        mine[3],
    )


class GatherSmall:
    def __init__(self, place, buffer, send_sem, recv_sem):
        self.place, self.buffer, self.send_sem, self.recv_sem = place, buffer, send_sem, recv_sem

    def copy(self, step, receiving=False):
        p, buf = self.place, self.buffer
        if step == 0:
            region, to = buf.at[p.y_hi, p.z, 1 - p.core if receiving else p.core], p.to_core
        elif step == 1:
            region, to = buf.at[1 - p.y_hi if receiving else p.y_hi, p.z], p.to_cross
        elif step == 2:
            region, to = buf.at[:, p.z_down if receiving else p.z], p.to_z_up
        elif step == 3:
            region, to = buf.at[:, p.z_up if receiving else p.z], p.to_z_down
        else:
            region, to = buf.at[:, p.z_far if receiving else p.z_down], p.to_z_up
        return pltpu.make_async_remote_copy(
            src_ref=region,
            dst_ref=region,
            send_sem=self.send_sem.at[step],
            recv_sem=self.recv_sem.at[step],
            device_id=to,
            device_id_type=MESH,
        )

    def start(self, step):
        self.copy(step).start()

    def take(self, step):
        self.copy(step, True).wait_recv()

    def finish(self):
        for step in range(5):
            self.copy(step).wait_send()


PART_ORDER = ("xyz", "yzx", "zxy")
FREE = ((("yl", "yh", "z"), ("z",), ()), (("z", "x"), ("x",), ()), (("yl", "yh", "x"), ("yl", "yh"), ()))
EXTENT = {"yl": 2, "yh": 2, "z": 4, "x": 4}


def half_shape(part, step):
    free = FREE[part][step]
    first = EXTENT[free[0]] // 2
    return ((first,) if first > 1 else ()) + tuple(EXTENT[d] for d in free[1:])


def near_shape(part, step):
    return tuple(EXTENT[d] for d in FREE[part][step])


def reduce_scratch():
    shapes = []
    for g in range(4):
        rows, half = SHARD_ROWS[g] // 4, COLUMNS[g] // 2
        shapes.append(pltpu.VMEM((2, 2, 4, 4, rows, half), bf16))
        shapes.append(pltpu.VMEM((2, 4, rows, half), bf16))
        for part in range(3):
            tail = (rows, THIRDS[g][part])
            for step in range(3):
                if step < 2:
                    shapes.append(pltpu.VMEM((2,) + half_shape(part, step) + tail, bf16))
                else:
                    shapes.append(pltpu.VMEM((1,) + tail, bf16))
                shapes.append(pltpu.VMEM((2,) + near_shape(part, step) + tail, bf16))
    return shapes


SCRATCH_PER_GROUP = 2 + 18


def accumulate(dst, src):
    lead = dst.shape[:-2]
    count = 1
    for n in lead:
        count *= n
    if not lead:
        dst[...] = dst[...] + src[...]
        return

    def body(i, carry):
        at, rest = [], i
        for n in reversed(lead):
            at.append(rest % n)
            rest = rest // n
        at = tuple(reversed(at))
        dst.at[at][...] = dst.at[at][...] + src.at[at][...]
        return carry

    lax.fori_loop(0, count, body, 0)


class Reduce:
    def __init__(self, place, grads, scratch, send_sem, recv_sem, load_sem):
        self.place, self.grads = place, grads
        self.send_sem, self.recv_sem, self.load_sem = send_sem, recv_sem, load_sem
        self.sent = []
        self.groups = [scratch[g * SCRATCH_PER_GROUP : (g + 1) * SCRATCH_PER_GROUP] for g in range(4)]

    def total(self, g):
        return self.groups[g][0]

    def result(self, g):
        return self.groups[g][1]

    def halves(self, g, part, step):
        return self.groups[g][2 + (part * 3 + step) * 2]

    def nears(self, g, part, step):
        return self.groups[g][3 + (part * 3 + step) * 2]

    def cols(self, g, part):
        return pl.ds(sum(THIRDS[g][:part]), THIRDS[g][part])

    def moved(self, dim, by):
        p = self.place
        if dim == "x":
            x = (p.x + by) % 4
            return {"x": x}, (p.dp, x * 2 + p.y_lo)
        if dim == "z":
            z = (p.z + by) % 4
            return {"z": z}, (p.y_hi * 8 + z * 2 + p.core, p.seq)
        y = (p.y_hi * 2 + p.y_lo + by) % 4
        return {"yl": y % 2, "yh": y // 2}, ((y // 2) * 8 + p.z * 2 + p.core, p.x * 2 + y % 2)

    def chunk(self, g, part, step, by, half=None):
        at = {}
        for earlier in range(step):
            at.update(self.moved(PART_ORDER[part][earlier], 0)[0])
        at.update(self.moved(PART_ORDER[part][step], by)[0])
        if half is not None:
            cut = FREE[part][step][0]
            size = EXTENT[cut] // 2
            at[cut] = half if size == 1 else pl.ds(half * size, size)
        index = tuple(at.get(name, slice(None)) for name in ("yl", "yh", "z", "x"))
        return self.total(g).at[index + (slice(None), self.cols(g, part))]

    def remote(self, g, sem, src, dst, to):
        return pltpu.make_async_remote_copy(
            src_ref=src,
            dst_ref=dst,
            send_sem=self.send_sem.at[g, sem],
            recv_sem=self.recv_sem.at[g, sem],
            device_id=to,
            device_id_type=MESH,
        )

    def send(self, g, sem, src, dst, to):
        copy = self.remote(g, sem, src, dst, to)
        copy.start()
        self.sent.append(copy)

    def take(self, g, sem, dst):
        self.remote(g, sem, dst, dst, self.place.to_core).wait_recv()

    def load(self, g):
        return pltpu.make_async_copy(self.grads[g], self.total(g), self.load_sem.at[g])

    def send_far(self, g, step):
        for part in range(3):
            sem, dim = part * 12 + step * 4, PART_ORDER[part][step]
            buf = self.halves(g, part, step)
            up, down = self.moved(dim, 1)[1], self.moved(dim, 3)[1]
            if step < 2:
                self.send(g, sem, self.chunk(g, part, step, 2, 0), buf.at[0], up)
                self.send(g, sem + 1, self.chunk(g, part, step, 2, 1), buf.at[1], down)
            else:
                self.send(g, sem, self.chunk(g, part, step, 2), buf.at[0], up)

    def send_near(self, g, step):
        for part in range(3):
            sem, dim = part * 12 + step * 4, PART_ORDER[part][step]
            buf, near = self.halves(g, part, step), self.nears(g, part, step)
            up, down = self.moved(dim, 1)[1], self.moved(dim, 3)[1]
            self.take(g, sem, buf.at[0])
            accumulate(self.chunk(g, part, step, 1, 0 if step < 2 else None), buf.at[0])
            self.send(g, sem + 2, self.chunk(g, part, step, 1), near.at[0], up)
            if step < 2:
                self.take(g, sem + 1, buf.at[1])
                accumulate(self.chunk(g, part, step, 3, 1), buf.at[1])
            self.send(g, sem + 3, self.chunk(g, part, step, 3), near.at[1], down)

    def join_near(self, g, step):
        for part in range(3):
            sem, near = part * 12 + step * 4, self.nears(g, part, step)
            for way in range(2):
                self.take(g, sem + 2 + way, near.at[way])
                accumulate(self.chunk(g, part, step, 0), near.at[way])

    def stage(self, number, g):
        p = self.place
        result = self.result(g)
        if number == 0:
            self.load(g).wait()
            self.send_far(g, 0)
        elif number in (1, 3, 5):
            self.send_near(g, number // 2)
        elif number in (2, 4):
            self.join_near(g, number // 2 - 1)
            self.send_far(g, number // 2)
        elif number == 6:
            self.join_near(g, 2)
            result.at[p.y_lo, p.x][...] = self.total(g).at[p.y_lo, p.y_hi, p.z, p.x][...]
            mine = result.at[p.y_lo, p.x]
            self.send(g, 37, mine, mine, p.to_pair)
        elif number == 7:
            self.take(g, 37, result.at[1 - p.y_lo, p.x])
            mine = result.at[:, p.x]
            self.send(g, 38, mine, mine, p.to_x_up)
            self.send(g, 39, mine, mine, p.to_x_down)
        elif number == 8:
            below, above = (p.x + 3) % 4, (p.x + 1) % 4
            self.take(g, 38, result.at[:, below])
            self.send(g, 40, result.at[0, below], result.at[0, below], p.to_x_up)
            self.take(g, 39, result.at[:, above])
            self.send(g, 41, result.at[1, above], result.at[1, above], p.to_x_down)
        else:
            far = (p.x + 2) % 4
            self.take(g, 40, result.at[0, far])
            self.take(g, 41, result.at[1, far])

    def finish(self):
        for copy in self.sent:
            copy.wait_send()
        self.sent = []


class ReduceSmall:
    STEPS = (("core", 2), ("pair", 2), ("cross", 2), ("x", 4), ("z", 4))

    def __init__(self, place, slots, send_sem, recv_sem):
        self.place, self.slots, self.send_sem, self.recv_sem = place, slots, send_sem, recv_sem

    def peers(self, step):
        p = self.place
        name, count = self.STEPS[step]
        if count == 2:
            mine, to = {
                "core": (p.core, p.to_core),
                "pair": (p.y_lo, p.to_pair),
                "cross": (p.y_hi, p.to_cross),
            }[name]
            return mine, [(1 - mine, to)]
        if name == "x":
            return p.x, [((p.x + by) % 4, (p.dp, (p.x + by) % 4 * 2 + p.y_lo)) for by in (1, 2, 3)]
        return p.z, [
            ((p.z + by) % 4, (p.y_hi * 8 + (p.z + by) % 4 * 2 + p.core, p.seq)) for by in (1, 2, 3)
        ]

    def copies(self, step, receiving):
        mine, peers = self.peers(step)
        if receiving:
            peers = peers[::-1]
        for at, (place, to) in enumerate(peers):
            slot = self.slots.at[step, place if receiving else mine]
            yield pltpu.make_async_remote_copy(
                src_ref=slot,
                dst_ref=slot,
                send_sem=self.send_sem.at[step, at],
                recv_sem=self.recv_sem.at[step, at],
                device_id=to,
                device_id_type=MESH,
            )

    def put(self, step, values):
        mine, _ = self.peers(step)
        self.slots.at[step, mine][...] = values
        for copy in self.copies(step, False):
            copy.start()

    def sum(self, step):
        for copy in self.copies(step, True):
            copy.wait_recv()
        for copy in self.copies(step, False):
            copy.wait_send()
        total = self.slots[step, 0]
        for at in range(1, self.STEPS[step][1]):
            total = total + self.slots[step, at]
        return total


SCALE = 128 ** (-0.5)
OFFSETS = tuple((dx, dy) for dx in range(4) for dy in range(2) if (dx, dy) != (0, 0))


def mm(left, right):
    return jnp.dot(left, right, preferred_element_type=f32)


def mm_nt(left, right):
    return lax.dot_general(left, right, (((1,), (1,)), ((), ())), preferred_element_type=f32)


def mm_tn(left, right):
    return lax.dot_general(left, right, (((0,), (0,)), ((), ())), preferred_element_type=f32)


def inv_rms(v):
    return lax.rsqrt(jnp.mean(v * v, axis=-1, keepdims=True) + epsilon)


class Exchange:
    def __init__(self, place, send_sem, recv_sem):
        self.place, self.send_sem, self.recv_sem, self.sent = place, send_sem, recv_sem, []

    def partner(self, at, back=False):
        dx, dy = OFFSETS[at]
        x = (self.place.x + (4 - dx if back else dx)) % 4
        return x * 2 + (self.place.y_lo + dy) % 2

    def send(self, kind, src, dst):
        for at in range(7):
            partner = self.partner(at)
            copy = pltpu.make_async_remote_copy(
                src_ref=src(partner),
                dst_ref=dst(self.place.seq),
                send_sem=self.send_sem.at[kind, at],
                recv_sem=self.recv_sem.at[kind, at],
                device_id=(self.place.dp, partner),
                device_id_type=MESH,
            )
            copy.start()
            self.sent.append(copy)

    def take(self, kind, dst):
        for at in range(7):
            partner = self.partner(at, back=True)
            pltpu.make_async_remote_copy(
                src_ref=dst(partner),
                dst_ref=dst(partner),
                send_sem=self.send_sem.at[kind, at],
                recv_sem=self.recv_sem.at[kind, at],
                device_id=(self.place.dp, partner),
                device_id_type=MESH,
            ).wait_recv()

    def finish(self):
        for copy in self.sent:
            copy.wait_send()
        self.sent = []


def token_rows(seq):
    return pl.ds(pl.multiple_of(seq * 128, 128), 128)


def head_cols(seq, width):
    return pl.ds(pl.multiple_of(seq * width, 128), width)


def gain_rows(tile_ref):
    tiles = tile_ref[...].astype(f32).reshape(8, 2, 16, 128)
    pairs = tiles[:, 0] + tiles[:, 1]
    total = pairs[0]
    for at in range(1, 8):
        total = total + pairs[at]

    def wide(row):
        return jnp.concatenate([pairs[at, row : row + 1, :] for at in range(8)], axis=-1)

    return wide(0), total[1:2, :], total[2:3, :], wide(3)


def causal_scores(q, k, first):
    scores = mm_nt(q, k) * SCALE
    row = first + lax.broadcasted_iota(jnp.int32, scores.shape, 0)
    col = lax.broadcasted_iota(jnp.int32, scores.shape, 1)
    return jnp.where(col <= row, scores, -1e30)


FORWARD_IN = (
    "w_query", "w_key", "w_value", "w_output", "w_gate", "w_up", "w_down", "gains",
    "hidden", "cot", "cos", "sin", "valid",
)
FORWARD_OUT = (
    "out", "d_residual", "d_attended", "dg_ffn", "x_in", "q_flat", "k_flat",
    "total_output", "total_gate_up", "total_down", "weights_qkv", "q_heads", "k_heads", "v_heads", "gain_tiles",
)
FORWARD_SCRATCH = (
    "buf_qkv", "buf_output", "buf_gate_up", "buf_down", "tiles", "rows", "core_down",
    "q_in", "k_in", "v_in", "att", "context", "residual", "mid_in", "result", "d_mid", "d_branch",
    "gather_send", "gather_recv", "small_send", "small_recv", "local_sem", "swap_send", "swap_recv", "out_sem",
    "core_free", "core_send", "core_recv",
)
FF_TILE = 768


def forward_kernel(*refs):
    r = dict(zip(FORWARD_IN + FORWARD_OUT + FORWARD_SCRATCH, refs))
    place = Place()
    me = place.seq
    buffers = [r["buf_qkv"], r["buf_output"], r["buf_gate_up"], r["buf_down"]]
    tiles = r["tiles"]
    sources = [r[name] for name in FORWARD_IN[:8]]
    copies = [
        pltpu.make_async_copy(shard, there, r["local_sem"].at[at])
        for at, (shard, there) in enumerate(
            zip(sources, own_places(place, buffers) + (tiles.at[place.y_hi, place.z, place.core],))
        )
    ]
    for copy in copies:
        copy.start()
    greet(
        place.torus()
        + tuple(
            (place.dp, (place.x + dx) % 4 * 2 + (place.y_lo + dy) % 2)
            for dx, dy in OFFSETS
            if (dx, dy) not in ((1, 0), (3, 0), (0, 1))
        )
    )
    for copy in copies:
        copy.wait()
    gather = Gather(place, buffers, r["gather_send"], r["gather_recv"])
    little = GatherSmall(place, tiles, r["small_send"], r["small_recv"])
    swap = Exchange(place, r["swap_send"], r["swap_recv"])
    saved = []

    def save(name, src, dst=None):
        at = len(saved)
        copy = pltpu.make_async_copy(src, r[name] if dst is None else dst, r["out_sem"].at[at])
        copy.start()
        saved.append(copy)

    def phases(*steps):
        for number, g in steps:
            gather.phase(number, g)

    little.start(0)
    phases((0, 0))
    little.take(0)
    little.start(1)
    little.take(1)
    little.start(2)
    little.start(3)
    little.take(2)
    little.take(3)
    little.start(4)
    phases((1, 0), (0, 1), (2, 0), (3, 0), (0, 3), (4, 0), (5, 0), (1, 1), (6, 0))
    little.take(4)
    g_attn, g_query, g_key, g_ffn = gain_rows(tiles)
    x = r["hidden"][...].reshape(256, 1024).astype(f32)
    r["x_in"][...] = (x * inv_rms(x) * g_attn).astype(bf16)
    phases((0, 2), (7, 0))
    save("weights_qkv", buffers[0])
    save("gain_tiles", tiles)

    cos, sin = r["cos"], r["sin"]

    def qkv_weights(first):
        return buffers[0][:, :, :, :, pl.ds(pl.multiple_of(first, 128), 512)].reshape(1024, 512)

    def head_tile(j, flat_ref, rows_ref, first, gain):
        flat = mm(r["x_in"][...], qkv_weights(first + j * 512))
        cols = pl.ds(pl.multiple_of(j * 512, 128), 512)
        flat_ref[:, cols] = flat
        done = []
        for h in range(4):
            v = flat[:, h * 128 : (h + 1) * 128]
            v = v * inv_rms(v) * gain
            done.append((v * cos[...] + pltpu.roll(v, 64, 1) * sin[...]).astype(bf16))
        rows_ref[...] = jnp.concatenate(done, axis=-1).reshape(2, 128, 512)

    def query_tile(j, carry):
        head_tile(j, r["q_flat"], r["rows"].at[0, :, :, pl.ds(pl.multiple_of(j * 512, 128), 512)], 0, g_query)
        return carry

    def key_tile(j, carry):
        head_tile(j, r["k_flat"], r["rows"].at[1, :, :, pl.ds(pl.multiple_of(j * 512, 128), 512)], 2048, g_key)
        return carry

    def value_tile(j, carry):
        cols = pl.ds(pl.multiple_of(1024 + j * 512, 128), 512)
        r["rows"][1, :, :, cols] = mm(r["x_in"][...], qkv_weights(3072 + j * 512)).astype(bf16).reshape(2, 128, 512)
        return carry

    def to_heads(kind, at, first, heads, width):
        def cols(seq):
            return pl.ds(pl.multiple_of(first + seq * width, 128), width)

        swap.send(
            kind,
            lambda partner: r["rows"].at[at, :, :, cols(partner)],
            lambda sender: r[heads].at[:, token_rows(sender), :],
        )
        r[heads][:, token_rows(me), :] = r["rows"][at, :, :, cols(me)]

    lax.fori_loop(0, 4, query_tile, 0)
    to_heads(0, 0, 0, "q_in", 256)
    lax.fori_loop(0, 2, key_tile, 0)
    to_heads(1, 1, 0, "k_in", 128)
    lax.fori_loop(0, 2, value_tile, 0)
    to_heads(2, 1, 1024, "v_in", 128)
    phases((2, 1), (1, 3), (3, 1), (1, 2), (4, 1), (2, 3), (2, 2), (5, 1), (3, 3), (6, 1), (3, 2))
    swap.take(0, lambda sender: r["q_in"].at[:, token_rows(sender), :])
    swap.take(1, lambda sender: r["k_in"].at[:, token_rows(sender), :])
    swap.take(2, lambda sender: r["v_in"].at[:, token_rows(sender), :])
    save("q_heads", r["q_in"])
    save("k_heads", r["k_in"])
    save("v_heads", r["v_in"])

    def attend(slot, head):
        cols = slice(head * 128, (head + 1) * 128)
        for block in range(4):
            rows, upto = slice(block * 256, (block + 1) * 256), (block + 1) * 256
            q = r["q_in"][slot, rows, cols]
            scores = causal_scores(q, r["k_in"][slot, :upto, :], block * 256)
            top = jnp.max(scores, axis=-1, keepdims=True)
            shifted = jnp.exp(scores - top)
            total = jnp.sum(shifted, axis=-1, keepdims=True)
            prob = (shifted * (1.0 / total)).astype(bf16)
            r["att"][slot, rows, cols] = mm(prob, r["v_in"][slot, :upto, :]).astype(bf16)

    for slot in range(2):
        attend(slot, 0)
        attend(slot, 1)
        swap.send(
            3 + slot,
            lambda partner: r["att"].at[slot, token_rows(partner), :],
            lambda sender: r["context"].at[slot, :, head_cols(sender, 256)],
        )
        r["context"][slot, :, head_cols(me, 256)] = r["att"][slot, token_rows(me), :]
        if slot == 0:
            phases((4, 3), (4, 2))
    phases((7, 1), (5, 3), (5, 2), (6, 3), (6, 2))
    for slot in range(2):
        swap.take(3 + slot, lambda sender: r["context"].at[slot, :, head_cols(sender, 256)])

    for half in range(2):
        cols = slice(half * 512, (half + 1) * 512)
        weights = buffers[1][:, :, :, :, cols].reshape(2048, 512)
        x = r["hidden"][:, :, cols].reshape(256, 512).astype(f32)
        r["residual"][:, cols] = x + mm(r["context"][...].reshape(256, 2048), weights)
    residual = r["residual"][...]
    r["mid_in"][...] = (residual * inv_rms(residual) * g_ffn).astype(bf16)
    d_result = jnp.where(r["valid"][...] > 0.5, r["cot"][...].reshape(256, 1024).astype(f32), 0.0)
    r["d_branch"][...] = d_result.astype(bf16)
    phases((7, 2), (7, 3))
    gather.finish()
    little.finish()
    swap.finish()
    for copy in saved:
        copy.wait()
    saved.clear()
    pl.semaphore_signal(r["core_free"], inc=1, device_id=place.to_core, device_id_type=MESH)
    pl.semaphore_wait(r["core_free"], 1)
    core, other = place.core, 1 - place.core

    def to_core(src, dst, *at):
        return pltpu.make_async_remote_copy(
            src_ref=src,
            dst_ref=dst,
            send_sem=r["core_send"].at[at],
            recv_sem=r["core_recv"].at[at],
            device_id=place.to_core,
            device_id_type=MESH,
        )

    def ffn_copies(f):
        here = pl.ds(pl.multiple_of(f * FF_TILE, 128), FF_TILE)
        up = pl.ds(pl.multiple_of(3072 + f * FF_TILE, 128), FF_TILE)
        y, z = f // 2, pl.ds(f % 2 * 2, 2)
        return (
            to_core(buffers[2].at[:, :, other, :, here], buffers[0].at[:, :, 0, :, here], f, 0),
            to_core(buffers[2].at[:, :, other, :, up], buffers[0].at[:, :, 1, :, here], f, 1),
            to_core(buffers[3].at[y, z, other], r["core_down"].at[y, z], f, 2),
        )

    def ffn_join(f):
        here = pl.ds(pl.multiple_of(f * FF_TILE, 128), FF_TILE)
        up = pl.ds(pl.multiple_of(3072 + f * FF_TILE, 128), FF_TILE)
        y, z = f // 2, pl.ds(f % 2 * 2, 2)
        for copy in ffn_copies(f):
            copy.wait_recv()
        buffers[2][:, :, core, :, here] = buffers[2][:, :, core, :, here] + buffers[0][:, :, 0, :, here]
        buffers[2][:, :, core, :, up] = buffers[2][:, :, core, :, up] + buffers[0][:, :, 1, :, here]
        buffers[3][y, z, core] = buffers[3][y, z, core] + r["core_down"][y, z]

    r["result"][...] = residual
    r["d_mid"][...] = jnp.zeros((256, 1024), f32)

    def ffn_tile(f, carry):
        def weights(first):
            cols = pl.ds(pl.multiple_of(first + f * FF_TILE, 128), FF_TILE)
            return cols, buffers[2][:, :, :, :, cols].reshape(1024, FF_TILE)

        gate_cols, w_gate = weights(0)
        up_cols, w_up = weights(3072)
        y, z = f // 2, pl.ds(f % 2 * 2, 2)
        w_down = buffers[3][y, z].reshape(FF_TILE, 1024)
        mid, d_branch = r["mid_in"][...], r["d_branch"][...]
        gate, up = mm(mid, w_gate), mm(mid, w_up)
        sig = 1.0 / (1.0 + jnp.exp(-gate))
        silu = gate * sig
        unit = (silu * up).astype(bf16)
        d_unit = mm_nt(d_branch, w_down)
        d_gate = (d_unit * up * (sig * (1.0 + gate * (1.0 - sig)))).astype(bf16)
        d_up = (d_unit * silu).astype(bf16)
        r["result"][...] += mm(unit, w_down)
        r["d_mid"][...] += mm_nt(d_gate, w_gate) + mm_nt(d_up, w_up)
        shape = (4, 2, 64, FF_TILE)
        for part in range(2):
            mid_part = mid[:, part * 512 : (part + 1) * 512]
            buffers[2][part, :, :, :, gate_cols] = mm_tn(mid_part, d_gate).astype(bf16).reshape(shape)
            buffers[2][part, :, :, :, up_cols] = mm_tn(mid_part, d_up).astype(bf16).reshape(shape)
        buffers[3][y, z] = mm_tn(unit, d_branch).astype(bf16).reshape(2, 2, 192, 1024)
        for copy in ffn_copies(f):
            copy.start()

        @pl.when(f > 0)
        def _():
            ffn_join(f - 1)

        return carry

    lax.fori_loop(0, 3072 // FF_TILE, ffn_tile, 0)
    valid = r["valid"][...] > 0.5
    r["out"][...] = jnp.where(valid, r["result"][...], 0.0).astype(bf16).reshape(2, 128, 1024)

    residual, d_mid = r["residual"][...], r["d_mid"][...]
    scale = inv_rms(residual)
    weighed = g_ffn * d_mid
    d_norm = scale * weighed - residual * (scale * scale * scale) * jnp.mean(
        residual * weighed, axis=-1, keepdims=True
    )
    r["dg_ffn"][...] = jnp.sum(d_mid * residual * scale, axis=0, keepdims=True)
    d_result = jnp.where(valid, r["cot"][...].reshape(256, 1024).astype(f32), 0.0)
    r["d_residual"][...] = d_result + d_norm
    r["d_branch"][...] = r["d_residual"][...].astype(bf16)

    def output_tile(j, carry):
        y, z = j // 2, j % 2 * 2
        cols = pl.ds(pl.multiple_of(j * 512, 128), 512)
        d_attn = r["d_branch"][...]
        weights = buffers[1][y, pl.ds(z, 2)].reshape(512, 1024)
        r["d_attended"][:, :, cols] = mm_nt(d_attn, weights).astype(bf16).reshape(2, 128, 512)
        context = r["context"][:, :, cols].reshape(256, 512)
        buffers[1][y, pl.ds(z, 2)] = mm_tn(context, d_attn).astype(bf16).reshape(2, 2, 128, 1024)
        for copy in output_copies(j):
            copy.start()
        return carry

    def output_copies(j):
        y, z = j // 2, j % 2
        return tuple(
            to_core(
                buffers[1].at[y, z * 2 + k, other],
                r["rows"].at[y, z, :, pl.ds(k * 1024, 1024)],
                4 + j,
                k,
            )
            for k in range(2)
        )

    lax.fori_loop(0, 4, output_tile, 0)
    ffn_join(3)
    for half in range(2):
        save("total_gate_up", buffers[2].at[:, :, core, :, pl.ds(half * 3072, 3072)], r["total_gate_up"].at[half])
        save("total_down", buffers[3].at[:, :, core, :, pl.ds(half * 512, 512)], r["total_down"].at[half])

    def output_join(j, carry):
        y, z = j // 2, j % 2
        for k, copy in enumerate(output_copies(j)):
            copy.wait_recv()
            cols = slice(k * 1024, (k + 1) * 1024)
            buffers[1][y, z * 2 + k, core] = buffers[1][y, z * 2 + k, core] + r["rows"][y, z, :, cols]
        return carry

    lax.fori_loop(0, 4, output_join, 0)
    for half in range(2):
        save("total_output", buffers[1].at[:, :, core, :, pl.ds(half * 512, 512)], r["total_output"].at[half])
    for at in range(4):
        for copy in ffn_copies(at) + output_copies(at):
            copy.wait_send()
    for copy in saved:
        copy.wait()


def forward(shards, gains, hidden, cot, cos, sin, valid):
    def shape(*dims, dtype=bf16):
        return jax.ShapeDtypeStruct(dims, dtype)

    outs = {
        "out": shape(2, 128, 1024),
        "d_residual": shape(256, 1024, dtype=f32),
        "d_attended": shape(2, 128, 2048),
        "dg_ffn": shape(1, 1024, dtype=f32),
        "x_in": shape(256, 1024),
        "q_flat": shape(256, 2048, dtype=f32),
        "k_flat": shape(256, 1024, dtype=f32),
        "total_output": shape(2, 2, 4, 128, 512),
        "total_gate_up": shape(2, 2, 4, 64, 3072),
        "total_down": shape(2, 2, 4, 192, 512),
        "weights_qkv": shape(2, 4, 2, 64, 4096),
        "q_heads": shape(2, 1024, 256),
        "k_heads": shape(2, 1024, 128),
        "v_heads": shape(2, 1024, 128),
        "gain_tiles": shape(2, 4, 2, 16, 128),
    }
    vmem = pl.BlockSpec(memory_space=pltpu.VMEM)
    hbm = pl.BlockSpec(memory_space=pl.ANY)
    scratch = {
        "buf_qkv": (2, 4, 2, 64, 4096),
        "buf_output": (2, 4, 2, 128, 1024),
        "buf_gate_up": (2, 4, 2, 64, 6144),
        "buf_down": (2, 4, 2, 192, 1024),
        "tiles": (2, 4, 2, 16, 128),
        "rows": (2, 2, 128, 2048),
        "core_down": (2, 4, 192, 1024),
        "q_in": (2, 1024, 256),
        "k_in": (2, 1024, 128),
        "v_in": (2, 1024, 128),
        "att": (2, 1024, 256),
        "context": (2, 128, 2048),
        "residual": ((256, 1024), f32),
        "mid_in": (256, 1024),
        "result": ((256, 1024), f32),
        "d_mid": ((256, 1024), f32),
        "d_branch": (256, 1024),
    }
    dma = pltpu.SemaphoreType.DMA
    sems = [dma((4, KINDS)), dma((4, KINDS)), dma((5,)), dma((5,)), dma((8,)), dma((5, 7)), dma((5, 7)), dma((6,))]
    sems += [pltpu.SemaphoreType.REGULAR, dma((8, 3)), dma((8, 3))]
    buffers = [
        pltpu.VMEM(*(dims if isinstance(dims[0], tuple) else (dims, bf16))) for dims in scratch.values()
    ]
    results = pl.pallas_call(
        functools.partial(forward_kernel),
        out_shape=list(outs.values()),
        in_specs=[vmem] * 13,
        out_specs=[vmem] * 7 + [hbm] * 8,
        scratch_shapes=buffers + sems,
        compiler_params=pltpu.CompilerParams(
            collective_id=1, has_side_effects=True, vmem_limit_bytes=63 * 1024 * 1024
        ),
        name="forward",
    )(*shards, gains, hidden, cot, cos, sin, valid)
    return dict(zip(outs, results))


BACKWARD_IN = (
    "total_output", "total_gate_up", "total_down", "weights_qkv", "d_attended", "q_heads", "k_heads", "v_heads",
    "q_flat", "k_flat", "x_in", "hidden", "d_residual", "cos", "sin", "gain_tiles", "dg_ffn",
)
BACKWARD_OUT = ("d_input", "gains_sum", "sum_qkv", "sum_output", "sum_gate_up", "sum_down")
BACKWARD_SCRATCH = (
    "buf_qkv", "q_in", "k_in", "v_in", "grad_in", "dq", "dk", "dv", "dk_sum", "dv_sum", "dq_rows", "dk_rows", "dv_rows",
    "q_flat_in", "k_flat_in", "x_in_in", "d_x", "dg_query", "dg_key", "slots",
    "reduce_send", "reduce_recv", "load_sem", "small_send", "small_recv", "out_sem", "swap_send", "swap_recv", "in_sem",
)
FAR_STAGES = 10


def backward_kernel(*refs):
    names = BACKWARD_IN + BACKWARD_OUT
    count = 4 * SCRATCH_PER_GROUP
    r = dict(zip(names, refs))
    scratch = refs[len(names) : len(names) + count]
    r.update(zip(BACKWARD_SCRATCH, refs[len(names) + count :]))
    place = Place()
    me = place.seq
    loads = {
        name: pltpu.make_async_copy(r[name], r[there], r["in_sem"].at[at])
        for at, (name, there) in enumerate(
            (
                ("q_heads", "q_in"),
                ("k_heads", "k_in"),
                ("v_heads", "v_in"),
                ("q_flat", "q_flat_in"),
                ("k_flat", "k_flat_in"),
                ("x_in", "x_in_in"),
                ("weights_qkv", "buf_qkv"),
            )
        )
    }
    grads = (None, r["total_output"], r["total_gate_up"], r["total_down"])
    outs = (r["sum_qkv"], r["sum_output"], r["sum_gate_up"], r["sum_down"])
    reduce = Reduce(place, grads, scratch, r["reduce_send"], r["reduce_recv"], r["load_sem"])
    little = ReduceSmall(place, r["slots"], r["small_send"], r["small_recv"])
    swap = Exchange(place, r["swap_send"], r["swap_recv"])
    for name in ("q_heads", "k_heads", "v_heads"):
        loads[name].start()
    reduce.load(3).start()
    greet(
        place.torus()
        + tuple(
            (place.dp, (place.x + dx) % 4 * 2 + (place.y_lo + dy) % 2)
            for dx, dy in OFFSETS
            if (dx, dy) not in ((1, 0), (3, 0), (0, 1))
        )
        + ((place.y_hi * 8 + place.z_far * 2 + place.core, place.seq),)
    )
    own = []
    for slot in range(2):
        swap.send(
            slot,
            lambda partner: r["d_attended"].at[slot, :, head_cols(partner, 256)],
            lambda sender: r["grad_in"].at[slot, token_rows(sender), :],
        )
        copy = pltpu.make_async_copy(
            r["d_attended"].at[slot, :, head_cols(me, 256)], r["grad_in"].at[slot, token_rows(me), :], r["in_sem"].at[7 + slot]
        )
        copy.start()
        own.append(copy)
    reduce.load(2).start()
    reduce.load(1).start()
    for name in ("q_flat", "k_flat", "x_in", "weights_qkv"):
        loads[name].start()

    def stages(*steps):
        for number, g in steps:
            reduce.stage(number, g)
            if number == 9:
                pltpu.make_async_copy(reduce.result(g), outs[g], r["out_sem"].at[g]).start()

    stages((0, 3), (0, 2))
    for name in ("q_heads", "k_heads", "v_heads"):
        loads[name].wait()

    def attend_back(slot, head):
        cols = slice(head * 128, (head + 1) * 128)
        if head == 0:
            r["dk_sum"][...] = jnp.zeros((1024, 128), f32)
            r["dv_sum"][...] = jnp.zeros((1024, 128), f32)
        for block in range(4):
            rows, upto = slice(block * 256, (block + 1) * 256), (block + 1) * 256
            q, grad = r["q_in"][slot, rows, cols], r["grad_in"][slot, rows, cols]
            k, v = r["k_in"][slot, :upto, :], r["v_in"][slot, :upto, :]
            scores = mm_nt(k, q) * SCALE
            key = lax.broadcasted_iota(jnp.int32, scores.shape, 0)
            query = block * 256 + lax.broadcasted_iota(jnp.int32, scores.shape, 1)
            scores = jnp.where(key <= query, scores, -1e30)
            shifted = jnp.exp(scores - jnp.max(scores, axis=0, keepdims=True))
            prob = shifted * (1.0 / jnp.sum(shifted, axis=0, keepdims=True))
            d_prob = mm_nt(v, grad)
            dot = jnp.sum(prob * d_prob, axis=0, keepdims=True)
            d_score = (prob * (d_prob - dot) * SCALE).astype(bf16)
            r["dk_sum"][:upto, :] += mm(d_score, q)
            r["dv_sum"][:upto, :] += mm(prob.astype(bf16), grad)
            r["dq"][slot, rows, cols] = mm_tn(d_score, k).astype(bf16)

    def to_rows(kind, slot, heads, rows, width):
        swap.send(
            kind,
            lambda partner: r[heads].at[slot, token_rows(partner), :],
            lambda sender: r[rows].at[slot, :, head_cols(sender, width)],
        )
        r[rows][slot, :, head_cols(me, width)] = r[heads][slot, token_rows(me), :]

    between = (
        ((1, 3), (0, 1)),
        ((2, 3), (1, 2), (3, 3)),
        ((4, 3), (2, 2), (1, 1)),
        ((5, 3), (3, 2), (2, 1)),
    )
    for slot in range(2):
        own[slot].wait()
        swap.take(slot, lambda sender: r["grad_in"].at[slot, token_rows(sender), :])
        attend_back(slot, 0)
        stages(*between[2 * slot])
        attend_back(slot, 1)
        r["dk"][slot] = r["dk_sum"][...].astype(bf16)
        r["dv"][slot] = r["dv_sum"][...].astype(bf16)
        to_rows(2 + 3 * slot, slot, "dq", "dq_rows", 256)
        to_rows(3 + 3 * slot, slot, "dk", "dk_rows", 128)
        to_rows(4 + 3 * slot, slot, "dv", "dv_rows", 128)
        stages(*between[2 * slot + 1])
    g_attn, g_query, g_key, _ = gain_rows(r["gain_tiles"])
    for name in ("q_flat", "k_flat", "x_in", "weights_qkv"):
        loads[name].wait()
    stages((6, 3), (4, 2), (3, 1), (7, 3), (5, 2), (8, 3), (4, 1), (9, 3), (6, 2), (5, 1))
    for slot in range(2):
        swap.take(2 + 3 * slot, lambda sender: r["dq_rows"].at[slot, :, head_cols(sender, 256)])
        swap.take(3 + 3 * slot, lambda sender: r["dk_rows"].at[slot, :, head_cols(sender, 128)])
        swap.take(4 + 3 * slot, lambda sender: r["dv_rows"].at[slot, :, head_cols(sender, 128)])

    cos, sin = r["cos"], r["sin"]
    r["d_x"][...] = jnp.zeros((256, 1024), f32)
    r["dg_query"][...] = jnp.zeros((1, 128), f32)
    r["dg_key"][...] = jnp.zeros((1, 128), f32)

    def project_back(d_flat, first):
        cols = pl.ds(pl.multiple_of(first, 128), 512)
        weights = r["buf_qkv"][:, :, :, :, :, cols].reshape(1024, 512)
        r["d_x"][...] += mm_nt(d_flat, weights)
        grad = mm_tn(r["x_in_in"][...], d_flat).astype(bf16)
        r["buf_qkv"][:, :, :, :, :, cols] = grad.reshape(2, 4, 2, 4, 16, 512)

    def head_tile(j, rows_ref, flat_ref, first, gain, dg_ref):
        cols = pl.ds(pl.multiple_of(j * 512, 128), 512)
        grads_in = rows_ref[:, :, cols].reshape(256, 512).astype(f32)
        flat = flat_ref[:, cols]
        done = []
        for h in range(4):
            e = grads_in[:, h * 128 : (h + 1) * 128]
            v = flat[:, h * 128 : (h + 1) * 128]
            e = e * cos[...] - pltpu.roll(e, 64, 1) * sin[...]
            scale = inv_rms(v)
            weighed = gain * e
            d = scale * weighed - v * (scale * scale * scale) * jnp.mean(v * weighed, axis=-1, keepdims=True)
            dg_ref[...] += jnp.sum(e * v * scale, axis=0, keepdims=True)
            done.append(d.astype(bf16))
        project_back(jnp.concatenate(done, axis=-1), first + j * 512)

    def query_tile(j, carry):
        head_tile(j, r["dq_rows"], r["q_flat_in"], 0, g_query, r["dg_query"])
        return carry

    def key_tile(j, carry):
        head_tile(j, r["dk_rows"], r["k_flat_in"], 2048, g_key, r["dg_key"])
        return carry

    def value_tile(j, carry):
        cols = pl.ds(pl.multiple_of(j * 512, 128), 512)
        project_back(r["dv_rows"][:, :, cols].reshape(256, 512), 3072 + j * 512)
        return carry

    def swap_cores(half):
        reduce.send(
            0, 36 + 6 * half,
            r["buf_qkv"].at[:, :, 1 - place.core, :, :, pl.ds(half * 2048, 2048)],
            reduce.total(0).at[half],
            place.to_core,
        )

    lax.fori_loop(0, 4, query_tile, 0)
    swap_cores(0)
    lax.fori_loop(0, 2, key_tile, 0)
    lax.fori_loop(0, 2, value_tile, 0)
    swap_cores(1)
    for half in range(2):
        reduce.take(0, 36 + 6 * half, reduce.total(0).at[half])
        accumulate(
            reduce.total(0).at[half],
            r["buf_qkv"].at[:, :, place.core, :, :, pl.ds(half * 2048, 2048)],
        )
    reduce.send_far(0, 0)

    x, d_x = r["hidden"][...].reshape(256, 1024).astype(f32), r["d_x"][...]
    scale = inv_rms(x)
    weighed = g_attn * d_x
    d_norm = scale * weighed - x * (scale * scale * scale) * jnp.mean(x * weighed, axis=-1, keepdims=True)
    r["d_input"][...] = r["d_residual"][...] + d_norm
    dg_attn = jnp.sum(d_x * x * scale, axis=0, keepdims=True)
    rows = [dg_attn[:, at * 128 : (at + 1) * 128] for at in range(8)]
    rows += [r["dg_query"][...], r["dg_key"][...]]
    rows += [r["dg_ffn"][:, at * 128 : (at + 1) * 128] for at in range(8)]
    rows += [jnp.zeros((6, 128), f32)]
    little.put(0, jnp.concatenate(rows, axis=0))
    stages((1, 0), (7, 2), (6, 1))
    little.put(1, little.sum(0))
    stages((2, 0), (8, 2), (7, 1))
    little.put(2, little.sum(1))
    stages((3, 0), (9, 2), (8, 1))
    little.put(3, little.sum(2))
    stages((4, 0), (9, 1))
    little.put(4, little.sum(3))
    stages((5, 0), (6, 0))
    r["gains_sum"][...] = little.sum(4)
    stages((7, 0), (8, 0), (9, 0))
    reduce.finish()
    swap.finish()
    for g in range(4):
        pltpu.make_async_copy(reduce.result(g), outs[g], r["out_sem"].at[g]).wait()


def backward(inputs):
    def shape(*dims, dtype=bf16):
        return jax.ShapeDtypeStruct(dims, dtype)

    outs = [shape(256, 1024, dtype=f32), shape(24, 128, dtype=f32)] + [
        shape(2, 4, rows // 4, cols // 2) for rows, cols in zip(SHARD_ROWS, COLUMNS)
    ]
    vmem = pl.BlockSpec(memory_space=pltpu.VMEM)
    hbm = pl.BlockSpec(memory_space=pl.ANY)
    in_hbm = set(BACKWARD_IN[:11])
    buffers = [
        pltpu.VMEM(dims, dtype)
        for dims, dtype in (
            ((2, 4, 2, 4, 16, 4096), bf16),
            ((2, 1024, 256), bf16),
            ((2, 1024, 128), bf16),
            ((2, 1024, 128), bf16),
            ((2, 1024, 256), bf16),
            ((2, 1024, 256), bf16),
            ((2, 1024, 128), bf16),
            ((2, 1024, 128), bf16),
            ((1024, 128), f32),
            ((1024, 128), f32),
            ((2, 128, 2048), bf16),
            ((2, 128, 1024), bf16),
            ((2, 128, 1024), bf16),
            ((256, 2048), f32),
            ((256, 1024), f32),
            ((256, 1024), bf16),
            ((256, 1024), f32),
            ((1, 128), f32),
            ((1, 128), f32),
            ((5, 4, 24, 128), f32),
        )
    ]
    dma = pltpu.SemaphoreType.DMA
    sems = [
        dma((4, 44)),
        dma((4, 44)),
        dma((4,)),
        dma((5, 3)),
        dma((5, 3)),
        dma((4,)),
        dma((8, 7)),
        dma((8, 7)),
        dma((9,)),
    ]
    results = pl.pallas_call(
        functools.partial(backward_kernel),
        out_shape=outs,
        in_specs=[hbm if name in in_hbm else vmem for name in BACKWARD_IN],
        out_specs=[vmem] * 2 + [hbm] * 4,
        scratch_shapes=reduce_scratch() + buffers + sems,
        compiler_params=pltpu.CompilerParams(
            collective_id=2, has_side_effects=True, vmem_limit_bytes=63 * 1024 * 1024
        ),
        name="backward",
    )(*[inputs[name] for name in BACKWARD_IN])
    return dict(zip(BACKWARD_OUT, results))


def rotary_tables(positions):
    frequency = jnp.exp(jnp.arange(64, dtype=f32) * (-2.0 * math.log(rope_base) / 128))
    angles = positions.astype(f32)[:, None] * frequency[None, :]
    cos_half, sin_half = jnp.cos(angles), jnp.sin(angles)
    return (
        jnp.concatenate([cos_half, cos_half], axis=-1),
        jnp.concatenate([-sin_half, sin_half], axis=-1),
    )


def per_device(
    hidden_in,
    out_cotangent,
    slot_lengths,
    position_ids,
    attn_gain,
    w_query,
    key_weight,
    value_weight,
    query_gain,
    key_gain,
    w_output,
    ffn_gain,
    w_gate,
    w_up,
    w_down,
):
    dp = lax.axis_index("dp")
    tile = jnp.zeros((16, 128), bf16)
    for row, (gain, lane) in enumerate(
        ((attn_gain, dp % 2 * 64), (query_gain, dp * 8), (key_gain, dp * 8), (ffn_gain, dp % 2 * 64))
    ):
        tile = lax.dynamic_update_slice(tile, gain[None, :], (row, lane))
    index = lax.axis_index("seq") * 128 + jnp.arange(128, dtype=jnp.int32)
    valid = (index[None, :] < slot_lengths[:, None]).astype(f32).reshape(256, 1)
    cos, sin = rotary_tables(position_ids.reshape(256))
    shards = (w_query, key_weight, value_weight, w_output, w_gate, w_up, w_down)
    done = forward(shards, tile, hidden_in, out_cotangent, cos, sin, valid)
    done.update(hidden=hidden_in, cos=cos, sin=sin)
    for name, rows, cols in (("total_output", 32, 512), ("total_gate_up", 16, 3072), ("total_down", 48, 512)):
        done[name] = done[name].reshape(2, 2, 4, 4, rows, cols)
    done["weights_qkv"] = done["weights_qkv"].reshape(2, 4, 2, 4, 16, 4096)
    last = backward(done)
    sums = [last[name] for name in ("sum_qkv", "sum_output", "sum_gate_up", "sum_down")]
    d_input, gains_sum = last["d_input"].reshape(2, 128, 1024), last["gains_sum"]
    qkv, output, gate_up, down = [
        part.reshape(2, rows, cols // 2).astype(f32) for part, rows, cols in zip(sums, SHARD_ROWS, COLUMNS)
    ]
    gq, gk, gv, gg, gu = qkv[0], qkv[1, :, :1024], qkv[1, :, 1024:], gate_up[0], gate_up[1]
    go, gd = jnp.concatenate([output[0], output[1]], 1), jnp.concatenate([down[0], down[1]], 1)
    gains_sum = gains_sum.reshape(-1)
    dg_attn, dg_query, dg_key, dg_ffn = [
        lax.dynamic_slice(gains_sum, (start + dp * size,), (size,))
        for start, size in ((0, 64), (1024, 8), (1152, 8), (1280, 64))
    ]
    return (done["out"], d_input, dg_attn, gq, gk, gv, dg_query, dg_key, go, dg_ffn, gg, gu, gd)


def solution(mesh):
    slots, rows, vector, matrix = P("dp", "seq", None), P("dp", "seq"), P("dp"), P("dp", None)
    in_specs = (
        slots,
        slots,
        vector,
        rows,
        vector,
        matrix,
        matrix,
        matrix,
        vector,
        vector,
        matrix,
        vector,
        matrix,
        matrix,
        matrix,
    )
    out_specs = (
        slots,
        slots,
        vector,
        matrix,
        matrix,
        matrix,
        vector,
        vector,
        matrix,
        vector,
        matrix,
        matrix,
        matrix,
    )
    return jax.shard_map(
        per_device, mesh=mesh, in_specs=in_specs, out_specs=out_specs, check_vma=False
    )
```

```python
import functools
import math

import jax
import jax.numpy as jnp
from jax import lax
from jax.experimental import pallas as pl
from jax.experimental.pallas import tpu as pltpu
from jax.sharding import PartitionSpec as P

epsilon = 1e-06
rope_base = 1000000.0
bf16 = jnp.bfloat16
f32 = jnp.float32


MESH = pl.DeviceIdType.MESH
SHARD_ROWS = (64, 128, 64, 192)
COLUMNS = (4096, 1024, 6144, 1024)
THIRDS = ((640, 640, 768), (256, 128, 128), (1024, 1024, 1024), (128, 256, 128))


GATHER_ROWS = (64, 128, 64, 64, 192)
GATHER_COLUMNS = (4096, 1024, 3072, 3072, 1024)
SHARED = (1280, 384, 1024, 1024, 384)
SHARES = ((384, 384, 512), (128, 128, 128), (384, 256, 384), (256, 384, 384), (128, 128, 128))


class Place:
    def __init__(self):
        dp, seq = lax.axis_index("dp"), lax.axis_index("seq")
        x, y_lo = seq // 2, seq % 2
        y_hi, z, core = dp // 8, (dp // 2) % 4, dp % 2
        self.dp, self.seq, self.x, self.y_lo = dp, seq, x, y_lo
        self.y_hi, self.z, self.core = y_hi, z, core
        self.z_up, self.z_down, self.z_far = (z + 1) % 4, (z + 3) % 4, (z + 2) % 4
        self.color = (x + y_lo + y_hi) % 2
        self.to_z_up = (y_hi * 8 + self.z_up * 2 + core, seq)
        self.to_z_down = (y_hi * 8 + self.z_down * 2 + core, seq)
        self.to_x_up = (dp, ((x + 1) % 4) * 2 + y_lo)
        self.to_x_down = (dp, ((x + 3) % 4) * 2 + y_lo)
        self.to_pair = (dp, x * 2 + 1 - y_lo)
        self.to_cross = ((1 - y_hi) * 8 + z * 2 + core, x * 2 + 1 - y_lo)
        self.to_core = (y_hi * 8 + z * 2 + 1 - core, seq)

    def torus(self):
        return (
            self.to_z_up,
            self.to_z_down,
            self.to_x_up,
            self.to_x_down,
            self.to_pair,
            self.to_cross,
            self.to_core,
        )


def greet(peers):
    barrier = pltpu.get_barrier_semaphore()
    for peer in peers:
        pl.semaphore_signal(barrier, inc=1, device_id=peer, device_id_type=MESH)
    pl.semaphore_wait(barrier, len(peers))


GATHER_KINDS = (
    "own_up",
    "own_down",
    "on_up",
    "on_down",
    "cross_own",
    "cross_up",
    "cross_down",
    "cross_far",
    "other_up",
    "other_down",
    "other_on_up",
    "other_on_down",
) + tuple(f"share_{n}_{s}" for n in range(3) for s in ("up", "down", "far", "other"))
GATHER_KINDS += tuple(f"core_{s}" for s in ("own", "up", "down", "far", "other"))
KIND_AT = {kind: at for at, kind in enumerate(GATHER_KINDS)}
KINDS = len(GATHER_KINDS)


class Gather:
    def __init__(self, place, buffers, send_sem, recv_sem):
        self.place, self.buffers, self.send_sem, self.recv_sem = place, buffers, send_sem, recv_sem
        self.sent = []

    def region(self, g, kind, receiving):
        p = self.place
        rows, cols = GATHER_ROWS[g], GATHER_COLUMNS[g]
        shared = SHARED[g]
        here, there = p.y_hi, 1 - p.y_hi
        whole, top, low = pl.ds(0, rows), pl.ds(0, rows // 2), pl.ds(rows // 2, rows // 2)
        low_first = pl.ds(rows // 2, rows // 4)
        low_last = pl.ds(rows // 2 + rows // 4, rows // 4)
        color = p.color
        if kind.startswith("share") and receiving:
            color = 1 - color
        mine = pl.ds(pl.multiple_of(color * shared, 128), cols - shared)
        below, above = p.z_down, p.z_up
        z, far = p.z, p.z_far
        buf = self.buffers[g]

        def at(y, zz, r, c):
            return buf.at[y, zz, p.core, r, c]

        if kind == "own_up":
            return at(here, below if receiving else z, whole, mine), p.to_z_up
        if kind == "own_down":
            return at(here, above if receiving else z, whole, mine), p.to_z_down
        if kind == "on_up":
            return at(here, far if receiving else below, top, mine), p.to_z_up
        if kind == "on_down":
            return at(here, far if receiving else above, low, mine), p.to_z_down
        if kind.startswith("cross"):
            y = there if receiving else here
            which = kind[6:]
            if which == "own":
                return at(y, z, whole, mine), p.to_cross
            return at(y, {"up": above, "down": below, "far": far}[which], top, mine), p.to_cross
        if kind == "other_up":
            return at(there, below if receiving else z, low, mine), p.to_z_up
        if kind == "other_down":
            return at(there, above if receiving else z, low, mine), p.to_z_down
        if kind == "other_on_up":
            return at(there, far if receiving else below, low_first, mine), p.to_z_up
        if kind == "other_on_down":
            return at(there, far if receiving else above, low_last, mine), p.to_z_down
        if kind.startswith("share"):
            _, n, which = kind.split("_")
            n = int(n)
            start = color * (cols - shared) + sum(SHARES[g][:n])
            part = pl.ds(pl.multiple_of(start, 128), SHARES[g][n])
            to = (p.to_x_up, p.to_x_down, p.to_pair)[n]
            if which == "other":
                return buf.at[there, :, p.core, :, part], to
            return at(here, {"up": above, "down": below, "far": far}[which], whole, part), to
        which = kind[5:]
        core = 1 - p.core if receiving else p.core
        if which == "other":
            return buf.at[there, :, core], p.to_core
        return buf.at[here, {"own": z, "up": above, "down": below, "far": far}[which], core], p.to_core

    def copy(self, g, kind, receiving=False):
        region, to = self.region(g, kind, receiving)
        at = KIND_AT[kind]
        return pltpu.make_async_remote_copy(
            src_ref=region,
            dst_ref=region,
            send_sem=self.send_sem.at[g, at],
            recv_sem=self.recv_sem.at[g, at],
            device_id=to,
            device_id_type=MESH,
        )

    def send(self, g, *kinds):
        for kind in kinds:
            self.copy(g, kind).start()
            self.sent.append((g, kind))

    def take(self, g, *kinds):
        for kind in kinds:
            self.copy(g, kind, True).wait_recv()

    def share(self, g, which):
        self.send(g, *(f"share_{n}_{which}" for n in range(3)))

    def taken(self, g, which):
        self.take(g, *(f"share_{n}_{which}" for n in range(3)))

    def phase(self, number, g):
        if number == 0:
            self.send(g, "own_up", "own_down", "cross_own", "core_own")
        elif number == 1:
            self.take(g, "own_up", "own_down")
            self.send(g, "on_up", "on_down", "cross_up", "cross_down")
            self.share(g, "up")
            self.share(g, "down")
        elif number == 2:
            self.take(g, "cross_own")
            self.send(g, "other_up", "other_down")
        elif number == 8:
            self.take(g, "on_up", "on_down")
            self.send(g, "cross_far")
            self.share(g, "far")
        elif number == 3:
            self.take(g, "other_up", "other_down")
            self.send(g, "other_on_up", "other_on_down")
        elif number == 4:
            self.take(g, "cross_up", "cross_down", "cross_far", "other_on_up", "other_on_down")
            self.share(g, "other")
        elif number == 5:
            for which in ("up", "down", "far"):
                self.taken(g, which)
                self.send(g, f"core_{which}")
        elif number == 6:
            self.taken(g, "other")
            self.send(g, "core_other")
        else:
            self.take(g, "core_own", "core_up", "core_down", "core_far", "core_other")

    def finish(self, *groups):
        for g, kind in self.sent:
            if g in groups:
                self.copy(g, kind).wait_send()
        self.sent = [one for one in self.sent if one[0] not in groups]


def own_copies(place, shards, buffers):
    mine = [buf.at[place.y_hi, place.z, place.core] for buf in buffers]
    query, key, value, output, gate, up, down = shards
    first, last = pl.ds(0, 1536), pl.ds(1536, 1536)
    return (
        (query, mine[0].at[:, pl.ds(0, 2048)]),
        (key, mine[0].at[:, pl.ds(2048, 1024)]),
        (value, mine[0].at[:, pl.ds(3072, 1024)]),
        (output, mine[1]),
        (gate.at[:, first], mine[2].at[:, first]),
        (up.at[:, first], mine[2].at[:, last]),
        (gate.at[:, last], mine[3].at[:, first]),
        (up.at[:, last], mine[3].at[:, last]),
        (down, mine[4]),
    )


class GatherSmall:
    def __init__(self, place, buffer, send_sem, recv_sem):
        self.place, self.buffer, self.send_sem, self.recv_sem = place, buffer, send_sem, recv_sem

    def copy(self, step, receiving=False):
        p, buf = self.place, self.buffer
        if step == 0:
            region, to = buf.at[p.y_hi, p.z, 1 - p.core if receiving else p.core], p.to_core
        elif step == 1:
            region, to = buf.at[1 - p.y_hi if receiving else p.y_hi, p.z], p.to_cross
        elif step == 2:
            region, to = buf.at[:, p.z_down if receiving else p.z], p.to_z_up
        elif step == 3:
            region, to = buf.at[:, p.z_up if receiving else p.z], p.to_z_down
        else:
            region, to = buf.at[:, p.z_far if receiving else p.z_down], p.to_z_up
        return pltpu.make_async_remote_copy(
            src_ref=region,
            dst_ref=region,
            send_sem=self.send_sem.at[step],
            recv_sem=self.recv_sem.at[step],
            device_id=to,
            device_id_type=MESH,
        )

    def start(self, step):
        self.copy(step).start()

    def take(self, step):
        self.copy(step, True).wait_recv()

    def finish(self):
        for step in range(5):
            self.copy(step).wait_send()


PART_ORDER = ("xyz", "yzx", "zxy")
FREE = ((("yl", "yh", "z"), ("z",), ()), (("z", "x"), ("x",), ()), (("yl", "yh", "x"), ("yl", "yh"), ()))
EXTENT = {"yl": 2, "yh": 2, "z": 4, "x": 4}


def half_shape(part, step):
    free = FREE[part][step]
    first = EXTENT[free[0]] // 2
    return ((first,) if first > 1 else ()) + tuple(EXTENT[d] for d in free[1:])


def near_shape(part, step):
    return tuple(EXTENT[d] for d in FREE[part][step])


def reduce_scratch():
    shapes = []
    for g in range(4):
        rows, half = SHARD_ROWS[g] // 4, COLUMNS[g] // 2
        shapes.append(pltpu.VMEM((2, 2, 4, 4, rows, half), bf16))
        shapes.append(pltpu.VMEM((2, 4, rows, half), bf16))
        for part in range(3):
            tail = (rows, THIRDS[g][part])
            for step in range(3):
                if step < 2:
                    shapes.append(pltpu.VMEM((2,) + half_shape(part, step) + tail, bf16))
                else:
                    shapes.append(pltpu.VMEM((1,) + tail, bf16))
                shapes.append(pltpu.VMEM((2,) + near_shape(part, step) + tail, bf16))
    return shapes


SCRATCH_PER_GROUP = 2 + 18


def accumulate(dst, src):
    lead = dst.shape[:-2]
    count = 1
    for n in lead:
        count *= n
    if not lead:
        dst[...] = dst[...] + src[...]
        return

    def body(i, carry):
        at, rest = [], i
        for n in reversed(lead):
            at.append(rest % n)
            rest = rest // n
        at = tuple(reversed(at))
        dst.at[at][...] = dst.at[at][...] + src.at[at][...]
        return carry

    lax.fori_loop(0, count, body, 0)


class Reduce:
    def __init__(self, place, grads, scratch, send_sem, recv_sem, load_sem):
        self.place, self.grads = place, grads
        self.send_sem, self.recv_sem, self.load_sem = send_sem, recv_sem, load_sem
        self.sent = []
        self.groups = [scratch[g * SCRATCH_PER_GROUP : (g + 1) * SCRATCH_PER_GROUP] for g in range(4)]

    def total(self, g):
        return self.groups[g][0]

    def result(self, g):
        return self.groups[g][1]

    def halves(self, g, part, step):
        return self.groups[g][2 + (part * 3 + step) * 2]

    def nears(self, g, part, step):
        return self.groups[g][3 + (part * 3 + step) * 2]

    def cols(self, g, part):
        return pl.ds(sum(THIRDS[g][:part]), THIRDS[g][part])

    def moved(self, dim, by):
        p = self.place
        if dim == "x":
            x = (p.x + by) % 4
            return {"x": x}, (p.dp, x * 2 + p.y_lo)
        if dim == "z":
            z = (p.z + by) % 4
            return {"z": z}, (p.y_hi * 8 + z * 2 + p.core, p.seq)
        y = (p.y_hi * 2 + p.y_lo + by) % 4
        return {"yl": y % 2, "yh": y // 2}, ((y // 2) * 8 + p.z * 2 + p.core, p.x * 2 + y % 2)

    def chunk(self, g, part, step, by, half=None):
        at = {}
        for earlier in range(step):
            at.update(self.moved(PART_ORDER[part][earlier], 0)[0])
        at.update(self.moved(PART_ORDER[part][step], by)[0])
        if half is not None:
            cut = FREE[part][step][0]
            size = EXTENT[cut] // 2
            at[cut] = half if size == 1 else pl.ds(half * size, size)
        index = tuple(at.get(name, slice(None)) for name in ("yl", "yh", "z", "x"))
        return self.total(g).at[index + (slice(None), self.cols(g, part))]

    def remote(self, g, sem, src, dst, to):
        return pltpu.make_async_remote_copy(
            src_ref=src,
            dst_ref=dst,
            send_sem=self.send_sem.at[g, sem],
            recv_sem=self.recv_sem.at[g, sem],
            device_id=to,
            device_id_type=MESH,
        )

    def send(self, g, sem, src, dst, to):
        copy = self.remote(g, sem, src, dst, to)
        copy.start()
        self.sent.append(copy)

    def take(self, g, sem, dst):
        self.remote(g, sem, dst, dst, self.place.to_core).wait_recv()

    def load(self, g):
        return pltpu.make_async_copy(self.grads[g], self.total(g), self.load_sem.at[g])

    def send_far(self, g, step):
        for part in range(3):
            sem, dim = part * 12 + step * 4, PART_ORDER[part][step]
            buf = self.halves(g, part, step)
            up, down = self.moved(dim, 1)[1], self.moved(dim, 3)[1]
            if step < 2:
                self.send(g, sem, self.chunk(g, part, step, 2, 0), buf.at[0], up)
                self.send(g, sem + 1, self.chunk(g, part, step, 2, 1), buf.at[1], down)
            else:
                self.send(g, sem, self.chunk(g, part, step, 2), buf.at[0], up)

    def send_near(self, g, step):
        for part in range(3):
            sem, dim = part * 12 + step * 4, PART_ORDER[part][step]
            buf, near = self.halves(g, part, step), self.nears(g, part, step)
            up, down = self.moved(dim, 1)[1], self.moved(dim, 3)[1]
            self.take(g, sem, buf.at[0])
            accumulate(self.chunk(g, part, step, 1, 0 if step < 2 else None), buf.at[0])
            self.send(g, sem + 2, self.chunk(g, part, step, 1), near.at[0], up)
            if step < 2:
                self.take(g, sem + 1, buf.at[1])
                accumulate(self.chunk(g, part, step, 3, 1), buf.at[1])
            self.send(g, sem + 3, self.chunk(g, part, step, 3), near.at[1], down)

    def join_near(self, g, step):
        for part in range(3):
            sem, near = part * 12 + step * 4, self.nears(g, part, step)
            for way in range(2):
                self.take(g, sem + 2 + way, near.at[way])
                accumulate(self.chunk(g, part, step, 0), near.at[way])

    def stage(self, number, g):
        p = self.place
        result = self.result(g)
        if number == 0:
            self.load(g).wait()
            self.send_far(g, 0)
        elif number in (1, 3, 5):
            self.send_near(g, number // 2)
        elif number in (2, 4):
            self.join_near(g, number // 2 - 1)
            self.send_far(g, number // 2)
        elif number == 6:
            self.join_near(g, 2)
            result.at[p.y_lo, p.x][...] = self.total(g).at[p.y_lo, p.y_hi, p.z, p.x][...]
            mine = result.at[p.y_lo, p.x]
            self.send(g, 37, mine, mine, p.to_pair)
        elif number == 7:
            self.take(g, 37, result.at[1 - p.y_lo, p.x])
            mine = result.at[:, p.x]
            self.send(g, 38, mine, mine, p.to_x_up)
            self.send(g, 39, mine, mine, p.to_x_down)
        elif number == 8:
            below, above = (p.x + 3) % 4, (p.x + 1) % 4
            self.take(g, 38, result.at[:, below])
            self.send(g, 40, result.at[0, below], result.at[0, below], p.to_x_up)
            self.take(g, 39, result.at[:, above])
            self.send(g, 41, result.at[1, above], result.at[1, above], p.to_x_down)
        else:
            far = (p.x + 2) % 4
            self.take(g, 40, result.at[0, far])
            self.take(g, 41, result.at[1, far])

    def finish(self):
        for copy in self.sent:
            copy.wait_send()
        self.sent = []


class ReduceSmall:
    STEPS = (("core", 2), ("pair", 2), ("cross", 2), ("x", 4), ("z", 4))

    def __init__(self, place, slots, send_sem, recv_sem):
        self.place, self.slots, self.send_sem, self.recv_sem = place, slots, send_sem, recv_sem

    def peers(self, step):
        p = self.place
        name, count = self.STEPS[step]
        if count == 2:
            mine, to = {
                "core": (p.core, p.to_core),
                "pair": (p.y_lo, p.to_pair),
                "cross": (p.y_hi, p.to_cross),
            }[name]
            return mine, [(1 - mine, to)]
        if name == "x":
            return p.x, [((p.x + by) % 4, (p.dp, (p.x + by) % 4 * 2 + p.y_lo)) for by in (1, 2, 3)]
        return p.z, [
            ((p.z + by) % 4, (p.y_hi * 8 + (p.z + by) % 4 * 2 + p.core, p.seq)) for by in (1, 2, 3)
        ]

    def copies(self, step, receiving):
        mine, peers = self.peers(step)
        if receiving:
            peers = peers[::-1]
        for at, (place, to) in enumerate(peers):
            slot = self.slots.at[step, place if receiving else mine]
            yield pltpu.make_async_remote_copy(
                src_ref=slot,
                dst_ref=slot,
                send_sem=self.send_sem.at[step, at],
                recv_sem=self.recv_sem.at[step, at],
                device_id=to,
                device_id_type=MESH,
            )

    def put(self, step, values):
        mine, _ = self.peers(step)
        self.slots.at[step, mine][...] = values
        for copy in self.copies(step, False):
            copy.start()

    def sum(self, step):
        for copy in self.copies(step, True):
            copy.wait_recv()
        for copy in self.copies(step, False):
            copy.wait_send()
        total = self.slots[step, 0]
        for at in range(1, self.STEPS[step][1]):
            total = total + self.slots[step, at]
        return total


SCALE = 128 ** (-0.5)
OFFSETS = tuple((dx, dy) for dx in range(4) for dy in range(2) if (dx, dy) != (0, 0))


def mm(left, right):
    return jnp.dot(left, right, preferred_element_type=f32)


def mm_nt(left, right):
    return lax.dot_general(left, right, (((1,), (1,)), ((), ())), preferred_element_type=f32)


def mm_tn(left, right):
    return lax.dot_general(left, right, (((0,), (0,)), ((), ())), preferred_element_type=f32)


def inv_rms(v):
    return lax.rsqrt(jnp.mean(v * v, axis=-1, keepdims=True) + epsilon)


class Exchange:
    def __init__(self, place, send_sem, recv_sem):
        self.place, self.send_sem, self.recv_sem, self.sent = place, send_sem, recv_sem, []

    def partner(self, at, back=False):
        dx, dy = OFFSETS[at]
        x = (self.place.x + (4 - dx if back else dx)) % 4
        return x * 2 + (self.place.y_lo + dy) % 2

    def send(self, kind, src, dst):
        for at in range(7):
            partner = self.partner(at)
            copy = pltpu.make_async_remote_copy(
                src_ref=src(partner),
                dst_ref=dst(self.place.seq),
                send_sem=self.send_sem.at[kind, at],
                recv_sem=self.recv_sem.at[kind, at],
                device_id=(self.place.dp, partner),
                device_id_type=MESH,
            )
            copy.start()
            self.sent.append(copy)

    def take(self, kind, dst):
        for at in range(7):
            partner = self.partner(at, back=True)
            pltpu.make_async_remote_copy(
                src_ref=dst(partner),
                dst_ref=dst(partner),
                send_sem=self.send_sem.at[kind, at],
                recv_sem=self.recv_sem.at[kind, at],
                device_id=(self.place.dp, partner),
                device_id_type=MESH,
            ).wait_recv()

    def finish(self):
        for copy in self.sent:
            copy.wait_send()
        self.sent = []


def token_rows(seq):
    return pl.ds(pl.multiple_of(seq * 128, 128), 128)


def head_cols(seq, width):
    return pl.ds(pl.multiple_of(seq * width, 128), width)


def gain_rows(tile_ref):
    tiles = tile_ref[...].astype(f32).reshape(8, 2, 16, 128)
    pairs = tiles[:, 0] + tiles[:, 1]
    total = pairs[0]
    for at in range(1, 8):
        total = total + pairs[at]

    def wide(row):
        return jnp.concatenate([pairs[at, row : row + 1, :] for at in range(8)], axis=-1)

    return wide(0), total[1:2, :], total[2:3, :], wide(3)


def causal_scores(q, k, first):
    scores = mm_nt(q, k) * SCALE
    row = first + lax.broadcasted_iota(jnp.int32, scores.shape, 0)
    col = lax.broadcasted_iota(jnp.int32, scores.shape, 1)
    return jnp.where(col <= row, scores, -1e30)


FORWARD_IN = (
    "w_query", "w_key", "w_value", "w_output", "w_gate", "w_up", "w_down", "gains",
    "hidden", "cot", "cos", "sin", "valid",
)
FORWARD_OUT = (
    "out", "d_residual", "d_attended", "dg_ffn", "x_in", "q_flat", "k_flat",
    "total_output", "total_gate_up", "total_down", "weights_qkv", "q_heads", "k_heads", "v_heads", "gain_tiles",
)
FORWARD_SCRATCH = (
    "buf_qkv", "buf_output", "buf_gate_up_0", "buf_gate_up_1", "buf_down", "tiles", "rows", "core_down",
    "q_in", "k_in", "v_in", "att", "context", "residual", "mid_in", "result", "d_mid", "d_branch",
    "gather_send", "gather_recv", "small_send", "small_recv", "local_sem", "swap_send", "swap_recv", "out_sem",
    "core_free", "core_send", "core_recv",
    "out_out", "d_residual_out", "d_attended_out", "x_in_out", "q_flat_out", "k_flat_out",
)
FF_TILE = 768


def forward_kernel(*refs):
    r = dict(zip(FORWARD_IN + FORWARD_OUT + FORWARD_SCRATCH, refs))
    place = Place()
    me = place.seq
    buffers = [r["buf_qkv"], r["buf_output"], r["buf_gate_up_0"], r["buf_gate_up_1"], r["buf_down"]]
    tiles = r["tiles"]
    pairs = own_copies(place, [r[name] for name in FORWARD_IN[:7]], buffers)
    pairs += ((r["gains"], tiles.at[place.y_hi, place.z, place.core]),)
    copies = [
        pltpu.make_async_copy(shard, there, r["local_sem"].at[at]) for at, (shard, there) in enumerate(pairs)
    ]
    for copy in copies:
        copy.start()
    greet(
        place.torus()
        + tuple(
            (place.dp, (place.x + dx) % 4 * 2 + (place.y_lo + dy) % 2)
            for dx, dy in OFFSETS
            if (dx, dy) not in ((1, 0), (3, 0), (0, 1))
        )
    )
    for copy in copies:
        copy.wait()
    gather = Gather(place, buffers, r["gather_send"], r["gather_recv"])
    little = GatherSmall(place, tiles, r["small_send"], r["small_recv"])
    swap = Exchange(place, r["swap_send"], r["swap_recv"])
    saved = []

    def save(name, src, dst=None):
        at = len(saved)
        copy = pltpu.make_async_copy(src, r[name] if dst is None else dst, r["out_sem"].at[at])
        copy.start()
        saved.append(copy)

    def phases(*steps):
        for number, g in steps:
            gather.phase(number, g)

    little.start(0)
    phases((0, 0))
    little.take(0)
    little.start(1)
    little.take(1)
    little.start(2)
    little.start(3)
    little.take(2)
    little.take(3)
    little.start(4)
    phases((0, 1), (1, 0), (2, 0), (8, 0), (3, 0), (0, 2), (1, 1), (2, 1), (4, 0))
    little.take(4)
    g_attn, g_query, g_key, g_ffn = gain_rows(tiles)
    x = r["hidden"][...].reshape(256, 1024).astype(f32)
    r["x_in_out"][...] = (x * inv_rms(x) * g_attn).astype(bf16)
    phases((5, 0), (6, 0), (8, 1), (3, 1), (1, 2), (4, 1), (5, 1), (0, 4), (7, 0))
    save("weights_qkv", buffers[0])
    save("gain_tiles", tiles)

    cos, sin = r["cos"], r["sin"]

    def qkv_weights(first):
        return buffers[0][:, :, :, :, pl.ds(pl.multiple_of(first, 128), 512)].reshape(1024, 512)

    def head_tile(j, flat_ref, rows_ref, first, gain):
        flat = mm(r["x_in_out"][...], qkv_weights(first + j * 512))
        cols = pl.ds(pl.multiple_of(j * 512, 128), 512)
        flat_ref[:, cols] = flat
        done = []
        for h in range(4):
            v = flat[:, h * 128 : (h + 1) * 128]
            v = v * inv_rms(v) * gain
            done.append((v * cos[...] + pltpu.roll(v, 64, 1) * sin[...]).astype(bf16))
        rows_ref[...] = jnp.concatenate(done, axis=-1).reshape(2, 128, 512)

    def query_tile(j, carry):
        head_tile(j, r["q_flat_out"], r["rows"].at[0, :, :, pl.ds(pl.multiple_of(j * 512, 128), 512)], 0, g_query)
        return carry

    def key_tile(j, carry):
        head_tile(j, r["k_flat_out"], r["rows"].at[1, :, :, pl.ds(pl.multiple_of(j * 512, 128), 512)], 2048, g_key)
        return carry

    def value_tile(j, carry):
        cols = pl.ds(pl.multiple_of(1024 + j * 512, 128), 512)
        r["rows"][1, :, :, cols] = mm(r["x_in_out"][...], qkv_weights(3072 + j * 512)).astype(bf16).reshape(2, 128, 512)
        return carry

    def to_heads(kind, at, first, heads, width):
        def cols(seq):
            return pl.ds(pl.multiple_of(first + seq * width, 128), width)

        swap.send(
            kind,
            lambda partner: r["rows"].at[at, :, :, cols(partner)],
            lambda sender: r[heads].at[:, token_rows(sender), :],
        )
        r[heads][:, token_rows(me), :] = r["rows"][at, :, :, cols(me)]

    lax.fori_loop(0, 4, query_tile, 0)
    to_heads(0, 0, 0, "q_in", 256)
    lax.fori_loop(0, 2, key_tile, 0)
    to_heads(1, 1, 0, "k_in", 128)
    lax.fori_loop(0, 2, value_tile, 0)
    to_heads(2, 1, 1024, "v_in", 128)
    phases((0, 3), (2, 2), (3, 2), (8, 2), (1, 3), (1, 4), (2, 4), (2, 3), (4, 2), (8, 4), (3, 4), (6, 1))
    save("x_in", r["x_in_out"])
    save("q_flat", r["q_flat_out"])
    save("k_flat", r["k_flat_out"])
    swap.take(0, lambda sender: r["q_in"].at[:, token_rows(sender), :])
    swap.take(1, lambda sender: r["k_in"].at[:, token_rows(sender), :])
    swap.take(2, lambda sender: r["v_in"].at[:, token_rows(sender), :])
    save("q_heads", r["q_in"])
    save("k_heads", r["k_in"])
    save("v_heads", r["v_in"])

    def attend(slot, head):
        cols = slice(head * 128, (head + 1) * 128)
        for block in range(4):
            rows, upto = slice(block * 256, (block + 1) * 256), (block + 1) * 256
            q = r["q_in"][slot, rows, cols]
            scores = causal_scores(q, r["k_in"][slot, :upto, :], block * 256)
            top = jnp.max(scores, axis=-1, keepdims=True)
            shifted = jnp.exp(scores - top)
            total = jnp.sum(shifted, axis=-1, keepdims=True)
            prob = (shifted * (1.0 / total)).astype(bf16)
            r["att"][slot, rows, cols] = mm(prob, r["v_in"][slot, :upto, :]).astype(bf16)

    for slot in range(2):
        attend(slot, 0)
        attend(slot, 1)
        swap.send(
            3 + slot,
            lambda partner: r["att"].at[slot, token_rows(partner), :],
            lambda sender: r["context"].at[slot, :, head_cols(sender, 256)],
        )
        r["context"][slot, :, head_cols(me, 256)] = r["att"][slot, token_rows(me), :]
        if slot == 0:
            phases((7, 1), (5, 2), (3, 3))
    phases((4, 4), (8, 3), (5, 4))
    for slot in range(2):
        swap.take(3 + slot, lambda sender: r["context"].at[slot, :, head_cols(sender, 256)])

    for half in range(2):
        cols = slice(half * 512, (half + 1) * 512)
        weights = buffers[1][:, :, :, :, cols].reshape(2048, 512)
        x = r["hidden"][:, :, cols].reshape(256, 512).astype(f32)
        r["residual"][:, cols] = x + mm(r["context"][...].reshape(256, 2048), weights)
    residual = r["residual"][...]
    r["mid_in"][...] = (residual * inv_rms(residual) * g_ffn).astype(bf16)
    d_result = jnp.where(r["valid"][...] > 0.5, r["cot"][...].reshape(256, 1024).astype(f32), 0.0)
    r["d_branch"][...] = d_result.astype(bf16)
    phases((6, 2), (4, 3), (6, 4), (5, 3), (7, 4), (7, 2), (6, 3))
    gather.finish(0, 2, 4)
    little.finish()
    swap.finish()
    for copy in saved:
        copy.wait()
    saved.clear()
    pl.semaphore_signal(r["core_free"], inc=1, device_id=place.to_core, device_id_type=MESH)
    pl.semaphore_wait(r["core_free"], 1)
    core, other = place.core, 1 - place.core

    def to_core(src, dst, *at):
        return pltpu.make_async_remote_copy(
            src_ref=src,
            dst_ref=dst,
            send_sem=r["core_send"].at[at],
            recv_sem=r["core_recv"].at[at],
            device_id=place.to_core,
            device_id_type=MESH,
        )

    def ffn_places(f):
        here = pl.ds(pl.multiple_of(f % 2 * FF_TILE, 128), FF_TILE)
        up = pl.ds(pl.multiple_of(1536 + f % 2 * FF_TILE, 128), FF_TILE)
        there = pl.ds(pl.multiple_of(f * FF_TILE, 128), FF_TILE)
        return here, up, there, pl.ds(f % 2 * 2, 2)

    def ffn_copies(b, f):
        here, up, there, z = ffn_places(f)
        weights = buffers[2 + b]
        return (
            to_core(weights.at[:, :, other, :, here], buffers[0].at[:, :, 0, :, there], f, 0),
            to_core(weights.at[:, :, other, :, up], buffers[0].at[:, :, 1, :, there], f, 1),
            to_core(buffers[4].at[b, z, other], r["core_down"].at[b, z], f, 2),
        )

    def ffn_join(b, f):
        here, up, there, z = ffn_places(f)
        weights = buffers[2 + b]
        for copy in ffn_copies(b, f):
            copy.wait_recv()
        weights[:, :, core, :, here] = weights[:, :, core, :, here] + buffers[0][:, :, 0, :, there]
        weights[:, :, core, :, up] = weights[:, :, core, :, up] + buffers[0][:, :, 1, :, there]
        buffers[4][b, z, core] = buffers[4][b, z, core] + r["core_down"][b, z]

    r["result"][...] = residual
    r["d_mid"][...] = jnp.zeros((256, 1024), f32)

    def ffn_tile(b, f):
        gate_cols, up_cols, _, z = ffn_places(f)
        w_gate = buffers[2 + b][:, :, :, :, gate_cols].reshape(1024, FF_TILE)
        w_up = buffers[2 + b][:, :, :, :, up_cols].reshape(1024, FF_TILE)
        w_down = buffers[4][b, z].reshape(FF_TILE, 1024)
        mid, d_branch = r["mid_in"][...], r["d_branch"][...]
        gate, up = mm(mid, w_gate), mm(mid, w_up)
        sig = 1.0 / (1.0 + jnp.exp(-gate))
        silu = gate * sig
        unit = (silu * up).astype(bf16)
        d_unit = mm_nt(d_branch, w_down)
        d_gate = (d_unit * up * (sig * (1.0 + gate * (1.0 - sig)))).astype(bf16)
        d_up = (d_unit * silu).astype(bf16)
        r["result"][...] += mm(unit, w_down)
        r["d_mid"][...] += mm_nt(d_gate, w_gate) + mm_nt(d_up, w_up)
        shape = (4, 2, 64, FF_TILE)
        for part in range(2):
            mid_part = mid[:, part * 512 : (part + 1) * 512]
            buffers[2 + b][part, :, :, :, gate_cols] = mm_tn(mid_part, d_gate).astype(bf16).reshape(shape)
            buffers[2 + b][part, :, :, :, up_cols] = mm_tn(mid_part, d_up).astype(bf16).reshape(shape)
        buffers[4][b, z] = mm_tn(unit, d_branch).astype(bf16).reshape(2, 2, 192, 1024)
        for copy in ffn_copies(b, f):
            copy.start()

    def first_half(f, carry):
        ffn_tile(0, f)

        @pl.when(f > 0)
        def _():
            ffn_join(0, f - 1)

        return carry

    def last_half(f, carry):
        ffn_tile(1, f)

        @pl.when(f > 2)
        def _():
            ffn_join(1, f - 1)

        return carry

    lax.fori_loop(0, 2, first_half, 0)
    phases((7, 3))
    gather.finish(1, 3)
    ffn_join(0, 1)
    lax.fori_loop(2, 4, last_half, 0)
    valid = r["valid"][...] > 0.5
    r["out_out"][...] = jnp.where(valid, r["result"][...], 0.0).astype(bf16).reshape(2, 128, 1024)
    save("out", r["out_out"])

    residual, d_mid = r["residual"][...], r["d_mid"][...]
    scale = inv_rms(residual)
    weighed = g_ffn * d_mid
    d_norm = scale * weighed - residual * (scale * scale * scale) * jnp.mean(
        residual * weighed, axis=-1, keepdims=True
    )
    r["dg_ffn"][...] = jnp.sum(d_mid * residual * scale, axis=0, keepdims=True)
    d_result = jnp.where(valid, r["cot"][...].reshape(256, 1024).astype(f32), 0.0)
    r["d_residual_out"][...] = d_result + d_norm
    r["d_branch"][...] = r["d_residual_out"][...].astype(bf16)

    def output_tile(j, carry):
        y, z = j // 2, j % 2 * 2
        cols = pl.ds(pl.multiple_of(j * 512, 128), 512)
        d_attn = r["d_branch"][...]
        weights = buffers[1][y, pl.ds(z, 2)].reshape(512, 1024)
        r["d_attended_out"][:, :, cols] = mm_nt(d_attn, weights).astype(bf16).reshape(2, 128, 512)
        context = r["context"][:, :, cols].reshape(256, 512)
        buffers[1][y, pl.ds(z, 2)] = mm_tn(context, d_attn).astype(bf16).reshape(2, 2, 128, 1024)
        for copy in output_copies(j):
            copy.start()
        return carry

    def output_copies(j):
        y, z = j // 2, j % 2
        return tuple(
            to_core(
                buffers[1].at[y, z * 2 + k, other],
                r["rows"].at[y, z, :, pl.ds(k * 1024, 1024)],
                4 + j,
                k,
            )
            for k in range(2)
        )

    lax.fori_loop(0, 4, output_tile, 0)
    save("d_residual", r["d_residual_out"])
    save("d_attended", r["d_attended_out"])
    ffn_join(1, 3)
    for half in range(2):
        for b in range(2):
            save(
                "total_gate_up",
                buffers[2 + b].at[:, :, core, :, pl.ds(half * 1536, 1536)],
                r["total_gate_up"].at[half, :, :, :, pl.ds(b * 1536, 1536)],
            )
        save("total_down", buffers[4].at[:, :, core, :, pl.ds(half * 512, 512)], r["total_down"].at[half])

    def output_join(j, carry):
        y, z = j // 2, j % 2
        for k, copy in enumerate(output_copies(j)):
            copy.wait_recv()
            cols = slice(k * 1024, (k + 1) * 1024)
            buffers[1][y, z * 2 + k, core] = buffers[1][y, z * 2 + k, core] + r["rows"][y, z, :, cols]
        return carry

    lax.fori_loop(0, 4, output_join, 0)
    for half in range(2):
        save("total_output", buffers[1].at[:, :, core, :, pl.ds(half * 512, 512)], r["total_output"].at[half])
    for at in range(4):
        for copy in ffn_copies(at // 2, at) + output_copies(at):
            copy.wait_send()
    for copy in saved:
        copy.wait()


def forward(shards, gains, hidden, cot, cos, sin, valid):
    def shape(*dims, dtype=bf16):
        return jax.ShapeDtypeStruct(dims, dtype)

    outs = {
        "out": shape(2, 128, 1024),
        "d_residual": shape(256, 1024, dtype=f32),
        "d_attended": shape(2, 128, 2048),
        "dg_ffn": shape(1, 1024, dtype=f32),
        "x_in": shape(256, 1024),
        "q_flat": shape(256, 2048, dtype=f32),
        "k_flat": shape(256, 1024, dtype=f32),
        "total_output": shape(2, 2, 4, 128, 512),
        "total_gate_up": shape(2, 2, 4, 64, 3072),
        "total_down": shape(2, 2, 4, 192, 512),
        "weights_qkv": shape(2, 4, 2, 64, 4096),
        "q_heads": shape(2, 1024, 256),
        "k_heads": shape(2, 1024, 128),
        "v_heads": shape(2, 1024, 128),
        "gain_tiles": shape(2, 4, 2, 16, 128),
    }
    vmem = pl.BlockSpec(memory_space=pltpu.VMEM)
    hbm = pl.BlockSpec(memory_space=pl.ANY)
    scratch = {
        "buf_qkv": (2, 4, 2, 64, 4096),
        "buf_output": (2, 4, 2, 128, 1024),
        "buf_gate_up_0": (2, 4, 2, 64, 3072),
        "buf_gate_up_1": (2, 4, 2, 64, 3072),
        "buf_down": (2, 4, 2, 192, 1024),
        "tiles": (2, 4, 2, 16, 128),
        "rows": (2, 2, 128, 2048),
        "core_down": (2, 4, 192, 1024),
        "q_in": (2, 1024, 256),
        "k_in": (2, 1024, 128),
        "v_in": (2, 1024, 128),
        "att": (2, 1024, 256),
        "context": (2, 128, 2048),
        "residual": ((256, 1024), f32),
        "mid_in": (256, 1024),
        "result": ((256, 1024), f32),
        "d_mid": ((256, 1024), f32),
        "d_branch": (256, 1024),
    }
    dma = pltpu.SemaphoreType.DMA
    sems = [dma((5, KINDS)), dma((5, KINDS)), dma((5,)), dma((5,)), dma((10,)), dma((5, 7)), dma((5, 7)), dma((11,))]
    sems += [pltpu.SemaphoreType.REGULAR, dma((8, 3)), dma((8, 3))]
    buffers = [
        pltpu.VMEM(*(dims if isinstance(dims[0], tuple) else (dims, bf16))) for dims in scratch.values()
    ]
    results = pl.pallas_call(
        functools.partial(forward_kernel),
        out_shape=list(outs.values()),
        in_specs=[hbm] * 8 + [vmem] * 5,
        out_specs=[vmem if name == "dg_ffn" else hbm for name in outs],
        scratch_shapes=buffers
        + sems
        + [
            pltpu.VMEM(outs[name].shape, outs[name].dtype)
            for name in ("out", "d_residual", "d_attended", "x_in", "q_flat", "k_flat")
        ],
        compiler_params=pltpu.CompilerParams(
            collective_id=1, has_side_effects=True, vmem_limit_bytes=63 * 1024 * 1024
        ),
        name="forward",
    )(*shards, gains, hidden, cot, cos, sin, valid)
    return dict(zip(outs, results))


BACKWARD_IN = (
    "total_output", "total_gate_up", "total_down", "weights_qkv", "d_attended", "q_heads", "k_heads", "v_heads",
    "q_flat", "k_flat", "x_in", "hidden", "d_residual", "cos", "sin", "gain_tiles", "dg_ffn",
)
BACKWARD_OUT = ("d_input", "gains_sum", "sum_qkv", "sum_output", "sum_gate_up", "sum_down")
BACKWARD_SCRATCH = (
    "buf_qkv", "q_in", "k_in", "v_in", "grad_in", "dq", "dk", "dv", "dk_sum", "dv_sum", "dq_rows", "dk_rows", "dv_rows",
    "q_flat_in", "k_flat_in", "x_in_in", "hidden_in", "d_residual_in", "cos_in", "sin_in", "tiles_in", "dg_ffn_in", "d_x", "dg_query", "dg_key", "slots",
    "reduce_send", "reduce_recv", "load_sem", "small_send", "small_recv", "out_sem", "swap_send", "swap_recv", "in_sem",
)
LATE_LOADS = (
    "q_flat", "k_flat", "x_in", "weights_qkv", "hidden", "d_residual", "cos", "sin", "gain_tiles", "dg_ffn",
)


def backward_kernel(*refs):
    names = BACKWARD_IN + BACKWARD_OUT
    count = 4 * SCRATCH_PER_GROUP
    r = dict(zip(names, refs))
    scratch = refs[len(names) : len(names) + count]
    r.update(zip(BACKWARD_SCRATCH, refs[len(names) + count :]))
    place = Place()
    me = place.seq
    loads = {
        name: pltpu.make_async_copy(r[name], r[there], r["in_sem"].at[at])
        for at, (name, there) in enumerate(
            (
                ("q_heads", "q_in"),
                ("k_heads", "k_in"),
                ("v_heads", "v_in"),
                ("q_flat", "q_flat_in"),
                ("k_flat", "k_flat_in"),
                ("x_in", "x_in_in"),
                ("weights_qkv", "buf_qkv"),
                ("hidden", "hidden_in"),
                ("d_residual", "d_residual_in"),
                ("cos", "cos_in"),
                ("sin", "sin_in"),
                ("gain_tiles", "tiles_in"),
                ("dg_ffn", "dg_ffn_in"),
            )
        )
    }
    grads = (None, r["total_output"], r["total_gate_up"], r["total_down"])
    outs = (r["sum_qkv"], r["sum_output"], r["sum_gate_up"], r["sum_down"])
    reduce = Reduce(place, grads, scratch, r["reduce_send"], r["reduce_recv"], r["load_sem"])
    little = ReduceSmall(place, r["slots"], r["small_send"], r["small_recv"])
    swap = Exchange(place, r["swap_send"], r["swap_recv"])
    for name in ("q_heads", "k_heads", "v_heads"):
        loads[name].start()
    reduce.load(3).start()
    greet(
        place.torus()
        + tuple(
            (place.dp, (place.x + dx) % 4 * 2 + (place.y_lo + dy) % 2)
            for dx, dy in OFFSETS
            if (dx, dy) not in ((1, 0), (3, 0), (0, 1))
        )
        + ((place.y_hi * 8 + place.z_far * 2 + place.core, place.seq),)
    )
    own = []
    for slot in range(2):
        swap.send(
            slot,
            lambda partner: r["d_attended"].at[slot, :, head_cols(partner, 256)],
            lambda sender: r["grad_in"].at[slot, token_rows(sender), :],
        )
        copy = pltpu.make_async_copy(
            r["d_attended"].at[slot, :, head_cols(me, 256)], r["grad_in"].at[slot, token_rows(me), :], r["in_sem"].at[13 + slot]
        )
        copy.start()
        own.append(copy)
    reduce.load(2).start()
    reduce.load(1).start()
    for name in LATE_LOADS:
        loads[name].start()

    def stages(*steps):
        for number, g in steps:
            reduce.stage(number, g)
            if number == 9:
                pltpu.make_async_copy(reduce.result(g), outs[g], r["out_sem"].at[g]).start()

    stages((0, 3))
    for name in ("q_heads", "k_heads", "v_heads"):
        loads[name].wait()

    def attend_back(slot, head):
        cols = slice(head * 128, (head + 1) * 128)
        if head == 0:
            r["dk_sum"][...] = jnp.zeros((1024, 128), f32)
            r["dv_sum"][...] = jnp.zeros((1024, 128), f32)
        for block in range(4):
            rows, upto = slice(block * 256, (block + 1) * 256), (block + 1) * 256
            q, grad = r["q_in"][slot, rows, cols], r["grad_in"][slot, rows, cols]
            k, v = r["k_in"][slot, :upto, :], r["v_in"][slot, :upto, :]
            scores = mm_nt(k, q) * SCALE
            key = lax.broadcasted_iota(jnp.int32, scores.shape, 0)
            query = block * 256 + lax.broadcasted_iota(jnp.int32, scores.shape, 1)
            scores = jnp.where(key <= query, scores, -1e30)
            shifted = jnp.exp(scores - jnp.max(scores, axis=0, keepdims=True))
            prob = shifted * (1.0 / jnp.sum(shifted, axis=0, keepdims=True))
            d_prob = mm_nt(v, grad)
            dot = jnp.sum(prob * d_prob, axis=0, keepdims=True)
            d_score = (prob * (d_prob - dot) * SCALE).astype(bf16)
            r["dk_sum"][:upto, :] += mm(d_score, q)
            r["dv_sum"][:upto, :] += mm(prob.astype(bf16), grad)
            r["dq"][slot, rows, cols] = mm_tn(d_score, k).astype(bf16)

    def to_rows(kind, slot, heads, rows, width):
        swap.send(
            kind,
            lambda partner: r[heads].at[slot, token_rows(partner), :],
            lambda sender: r[rows].at[slot, :, head_cols(sender, width)],
        )
        r[rows][slot, :, head_cols(me, width)] = r[heads][slot, token_rows(me), :]

    for slot in range(2):
        own[slot].wait()
        swap.take(slot, lambda sender: r["grad_in"].at[slot, token_rows(sender), :])
        attend_back(slot, 0)
        attend_back(slot, 1)
        r["dk"][slot] = r["dk_sum"][...].astype(bf16)
        r["dv"][slot] = r["dv_sum"][...].astype(bf16)
        to_rows(2 + 3 * slot, slot, "dq", "dq_rows", 256)
        to_rows(3 + 3 * slot, slot, "dk", "dk_rows", 128)
        to_rows(4 + 3 * slot, slot, "dv", "dv_rows", 128)
        if slot == 0:
            stages((1, 3))
    for name in LATE_LOADS:
        loads[name].wait()
    g_attn, g_query, g_key, _ = gain_rows(r["tiles_in"])
    stages((0, 1), (2, 3), (0, 2), (1, 1), (3, 3))
    for slot in range(2):
        swap.take(2 + 3 * slot, lambda sender: r["dq_rows"].at[slot, :, head_cols(sender, 256)])
        swap.take(3 + 3 * slot, lambda sender: r["dk_rows"].at[slot, :, head_cols(sender, 128)])
        swap.take(4 + 3 * slot, lambda sender: r["dv_rows"].at[slot, :, head_cols(sender, 128)])

    cos, sin = r["cos_in"], r["sin_in"]
    r["d_x"][...] = jnp.zeros((256, 1024), f32)
    r["dg_query"][...] = jnp.zeros((1, 128), f32)
    r["dg_key"][...] = jnp.zeros((1, 128), f32)

    def project_back(d_flat, first):
        cols = pl.ds(pl.multiple_of(first, 128), 512)
        weights = r["buf_qkv"][:, :, :, :, :, cols].reshape(1024, 512)
        r["d_x"][...] += mm_nt(d_flat, weights)
        grad = mm_tn(r["x_in_in"][...], d_flat).astype(bf16)
        r["buf_qkv"][:, :, :, :, :, cols] = grad.reshape(2, 4, 2, 4, 16, 512)

    def head_tile(j, rows_ref, flat_ref, first, gain, dg_ref):
        cols = pl.ds(pl.multiple_of(j * 512, 128), 512)
        grads_in = rows_ref[:, :, cols].reshape(256, 512).astype(f32)
        flat = flat_ref[:, cols]
        done = []
        for h in range(4):
            e = grads_in[:, h * 128 : (h + 1) * 128]
            v = flat[:, h * 128 : (h + 1) * 128]
            e = e * cos[...] - pltpu.roll(e, 64, 1) * sin[...]
            scale = inv_rms(v)
            weighed = gain * e
            d = scale * weighed - v * (scale * scale * scale) * jnp.mean(v * weighed, axis=-1, keepdims=True)
            dg_ref[...] += jnp.sum(e * v * scale, axis=0, keepdims=True)
            done.append(d.astype(bf16))
        project_back(jnp.concatenate(done, axis=-1), first + j * 512)

    def query_tile(j, carry):
        head_tile(j, r["dq_rows"], r["q_flat_in"], 0, g_query, r["dg_query"])
        return carry

    def key_tile(j, carry):
        head_tile(j, r["dk_rows"], r["k_flat_in"], 2048, g_key, r["dg_key"])
        return carry

    def value_tile(j, carry):
        cols = pl.ds(pl.multiple_of(j * 512, 128), 512)
        project_back(r["dv_rows"][:, :, cols].reshape(256, 512), 3072 + j * 512)
        return carry

    def swap_cores(half):
        reduce.send(
            0, 36 + 6 * half,
            r["buf_qkv"].at[:, :, 1 - place.core, :, :, pl.ds(half * 2048, 2048)],
            reduce.total(0).at[half],
            place.to_core,
        )

    stages((1, 2), (4, 3))
    lax.fori_loop(0, 4, query_tile, 0)
    swap_cores(0)
    stages((2, 1), (5, 3))
    lax.fori_loop(0, 2, key_tile, 0)
    lax.fori_loop(0, 2, value_tile, 0)
    swap_cores(1)
    stages((2, 2), (3, 1), (6, 3))
    for half in range(2):
        reduce.take(0, 36 + 6 * half, reduce.total(0).at[half])
        accumulate(
            reduce.total(0).at[half],
            r["buf_qkv"].at[:, :, place.core, :, :, pl.ds(half * 2048, 2048)],
        )
    reduce.send_far(0, 0)

    x, d_x = r["hidden_in"][...].reshape(256, 1024).astype(f32), r["d_x"][...]
    scale = inv_rms(x)
    weighed = g_attn * d_x
    d_norm = scale * weighed - x * (scale * scale * scale) * jnp.mean(x * weighed, axis=-1, keepdims=True)
    dg_attn = jnp.sum(d_x * x * scale, axis=0, keepdims=True)
    r["d_x"][...] = r["d_residual_in"][...] + d_norm
    give = pltpu.make_async_copy(r["d_x"], r["d_input"], r["in_sem"].at[15])
    give.start()
    rows = [dg_attn[:, at * 128 : (at + 1) * 128] for at in range(8)]
    rows += [r["dg_query"][...], r["dg_key"][...]]
    rows += [r["dg_ffn_in"][:, at * 128 : (at + 1) * 128] for at in range(8)]
    rows += [jnp.zeros((6, 128), f32)]
    little.put(0, jnp.concatenate(rows, axis=0))
    stages((3, 2), (4, 1), (7, 3), (1, 0))
    little.put(1, little.sum(0))
    stages((4, 2), (5, 1), (8, 3), (2, 0))
    little.put(2, little.sum(1))
    stages((5, 2), (6, 1), (9, 3), (3, 0))
    little.put(3, little.sum(2))
    stages((6, 2), (7, 1), (4, 0))
    little.put(4, little.sum(3))
    stages((7, 2), (8, 1), (5, 0), (8, 2), (9, 1), (6, 0))
    r["gains_sum"][...] = little.sum(4)
    stages((9, 2), (7, 0), (8, 0), (9, 0))
    reduce.finish()
    swap.finish()
    give.wait()
    for g in range(4):
        pltpu.make_async_copy(reduce.result(g), outs[g], r["out_sem"].at[g]).wait()


def backward(inputs):
    def shape(*dims, dtype=bf16):
        return jax.ShapeDtypeStruct(dims, dtype)

    outs = [shape(256, 1024, dtype=f32), shape(24, 128, dtype=f32)] + [
        shape(2, 4, rows // 4, cols // 2) for rows, cols in zip(SHARD_ROWS, COLUMNS)
    ]
    vmem = pl.BlockSpec(memory_space=pltpu.VMEM)
    hbm = pl.BlockSpec(memory_space=pl.ANY)
    buffers = [
        pltpu.VMEM(dims, dtype)
        for dims, dtype in (
            ((2, 4, 2, 4, 16, 4096), bf16),
            ((2, 1024, 256), bf16),
            ((2, 1024, 128), bf16),
            ((2, 1024, 128), bf16),
            ((2, 1024, 256), bf16),
            ((2, 1024, 256), bf16),
            ((2, 1024, 128), bf16),
            ((2, 1024, 128), bf16),
            ((1024, 128), f32),
            ((1024, 128), f32),
            ((2, 128, 2048), bf16),
            ((2, 128, 1024), bf16),
            ((2, 128, 1024), bf16),
            ((256, 2048), f32),
            ((256, 1024), f32),
            ((256, 1024), bf16),
            ((2, 128, 1024), bf16),
            ((256, 1024), f32),
            ((256, 128), f32),
            ((256, 128), f32),
            ((2, 4, 2, 16, 128), bf16),
            ((1, 1024), f32),
            ((256, 1024), f32),
            ((1, 128), f32),
            ((1, 128), f32),
            ((5, 4, 24, 128), f32),
        )
    ]
    dma = pltpu.SemaphoreType.DMA
    sems = [
        dma((4, 44)),
        dma((4, 44)),
        dma((4,)),
        dma((5, 3)),
        dma((5, 3)),
        dma((4,)),
        dma((8, 7)),
        dma((8, 7)),
        dma((16,)),
    ]
    results = pl.pallas_call(
        functools.partial(backward_kernel),
        out_shape=outs,
        in_specs=[hbm] * len(BACKWARD_IN),
        out_specs=[hbm, vmem] + [hbm] * 4,
        scratch_shapes=reduce_scratch() + buffers + sems,
        compiler_params=pltpu.CompilerParams(
            collective_id=2, has_side_effects=True, vmem_limit_bytes=63 * 1024 * 1024
        ),
        name="backward",
    )(*[inputs[name] for name in BACKWARD_IN])
    return dict(zip(BACKWARD_OUT, results))


def finish_kernel(*refs):
    qkv, output, gate_up, down, gains = refs[:5]
    gq, gk, gv, go, gg, gu, gd, d_attn, d_query, d_key, d_ffn = refs[5:]
    gq[...] = qkv[0].astype(f32)
    gk[...] = qkv[1, :, :1024].astype(f32)
    gv[...] = qkv[1, :, 1024:].astype(f32)
    for half in range(2):
        cols = slice(half * 512, (half + 1) * 512)
        go[:, cols] = output[half].astype(f32)
        gd[:, cols] = down[half].astype(f32)
    gg[...] = gate_up[0].astype(f32)
    gu[...] = gate_up[1].astype(f32)
    dp = lax.axis_index("dp")
    row, lane = dp // 2, dp % 2 * 64
    for ref, at in ((d_attn, row), (d_ffn, 10 + row)):
        ref[...] = pltpu.roll(gains[pl.ds(at, 1), :], lane, 1)[:, :64]
    for ref, at in ((d_query, 8), (d_key, 9)):
        ref[...] = pltpu.roll(gains[at : at + 1, :], (128 - dp * 8) % 128, 1)[:, :8]


def finish(sums, gains):
    def shape(*dims):
        return jax.ShapeDtypeStruct(dims, f32)

    outs = [
        shape(64, 2048),
        shape(64, 1024),
        shape(64, 1024),
        shape(128, 1024),
        shape(64, 3072),
        shape(64, 3072),
        shape(192, 1024),
        shape(1, 64),
        shape(1, 8),
        shape(1, 8),
        shape(1, 64),
    ]
    vmem = pl.BlockSpec(memory_space=pltpu.VMEM)
    sums = [part.reshape(2, rows, cols // 2) for part, rows, cols in zip(sums, SHARD_ROWS, COLUMNS)]
    return pl.pallas_call(
        functools.partial(finish_kernel),
        out_shape=outs,
        in_specs=[vmem] * 5,
        out_specs=[vmem] * 11,
        compiler_params=pltpu.CompilerParams(vmem_limit_bytes=32 * 1024 * 1024),
        name="finish",
    )(*sums, gains)


def rotary_tables(positions):
    frequency = jnp.exp(jnp.arange(64, dtype=f32) * (-2.0 * math.log(rope_base) / 128))
    angles = positions.astype(f32)[:, None] * frequency[None, :]
    cos_half, sin_half = jnp.cos(angles), jnp.sin(angles)
    return (
        jnp.concatenate([cos_half, cos_half], axis=-1),
        jnp.concatenate([-sin_half, sin_half], axis=-1),
    )


def per_device(
    hidden_in,
    out_cotangent,
    slot_lengths,
    position_ids,
    attn_gain,
    w_query,
    key_weight,
    value_weight,
    query_gain,
    key_gain,
    w_output,
    ffn_gain,
    w_gate,
    w_up,
    w_down,
):
    dp = lax.axis_index("dp")
    tile = jnp.zeros((16, 128), bf16)
    for row, (gain, lane) in enumerate(
        ((attn_gain, dp % 2 * 64), (query_gain, dp * 8), (key_gain, dp * 8), (ffn_gain, dp % 2 * 64))
    ):
        tile = lax.dynamic_update_slice(tile, gain[None, :], (row, lane))
    index = lax.axis_index("seq") * 128 + jnp.arange(128, dtype=jnp.int32)
    valid = (index[None, :] < slot_lengths[:, None]).astype(f32).reshape(256, 1)
    cos, sin = rotary_tables(position_ids.reshape(256))
    shards = (w_query, key_weight, value_weight, w_output, w_gate, w_up, w_down)
    done = forward(shards, tile, hidden_in, out_cotangent, cos, sin, valid)
    done.update(hidden=hidden_in, cos=cos, sin=sin)
    for name, rows, cols in (("total_output", 32, 512), ("total_gate_up", 16, 3072), ("total_down", 48, 512)):
        done[name] = done[name].reshape(2, 2, 4, 4, rows, cols)
    done["weights_qkv"] = done["weights_qkv"].reshape(2, 4, 2, 4, 16, 4096)
    last = backward(done)
    sums = [last[name] for name in ("sum_qkv", "sum_output", "sum_gate_up", "sum_down")]
    d_input = last["d_input"].reshape(2, 128, 1024)
    gq, gk, gv, go, gg, gu, gd, *gains = finish(sums, last["gains_sum"])
    dg_attn, dg_query, dg_key, dg_ffn = [gain.reshape(-1) for gain in gains]
    return (done["out"], d_input, dg_attn, gq, gk, gv, dg_query, dg_key, go, dg_ffn, gg, gu, gd)


def solution(mesh):
    slots, rows, vector, matrix = P("dp", "seq", None), P("dp", "seq"), P("dp"), P("dp", None)
    in_specs = (
        slots,
        slots,
        vector,
        rows,
        vector,
        matrix,
        matrix,
        matrix,
        vector,
        vector,
        matrix,
        vector,
        matrix,
        matrix,
        matrix,
    )
    out_specs = (
        slots,
        slots,
        vector,
        matrix,
        matrix,
        matrix,
        vector,
        vector,
        matrix,
        vector,
        matrix,
        matrix,
        matrix,
    )
    return jax.shard_map(
        per_device, mesh=mesh, in_specs=in_specs, out_specs=out_specs, check_vma=False
    )
```

```python
import functools
import math

import jax
import jax.numpy as jnp
from jax import lax
from jax.experimental import pallas as pl
from jax.experimental.pallas import tpu as pltpu
from jax.sharding import PartitionSpec as P

epsilon = 1e-06
rope_base = 1000000.0
bf16 = jnp.bfloat16
f32 = jnp.float32


MESH = pl.DeviceIdType.MESH
SHARD_ROWS = (64, 128, 64, 192)
COLUMNS = (4096, 1024, 6144, 1024)
THIRDS = ((640, 640, 768), (256, 128, 128), (1024, 1024, 1024), (128, 256, 128))


GATHER_ROWS = (64, 128, 64, 64, 192)
GATHER_COLUMNS = (4096, 1024, 3072, 3072, 1024)
SHARED = (1280, 384, 1024, 1024, 384)
SHARES = ((384, 384, 512), (128, 128, 128), (384, 256, 384), (256, 384, 384), (128, 128, 128))


class Place:
    def __init__(self):
        dp, seq = lax.axis_index("dp"), lax.axis_index("seq")
        x, y_lo = seq // 2, seq % 2
        y_hi, z, core = dp // 8, (dp // 2) % 4, dp % 2
        self.dp, self.seq, self.x, self.y_lo = dp, seq, x, y_lo
        self.y_hi, self.z, self.core = y_hi, z, core
        self.z_up, self.z_down, self.z_far = (z + 1) % 4, (z + 3) % 4, (z + 2) % 4
        self.color = (x + y_lo + y_hi) % 2
        self.to_z_up = (y_hi * 8 + self.z_up * 2 + core, seq)
        self.to_z_down = (y_hi * 8 + self.z_down * 2 + core, seq)
        self.to_x_up = (dp, ((x + 1) % 4) * 2 + y_lo)
        self.to_x_down = (dp, ((x + 3) % 4) * 2 + y_lo)
        self.to_pair = (dp, x * 2 + 1 - y_lo)
        self.to_cross = ((1 - y_hi) * 8 + z * 2 + core, x * 2 + 1 - y_lo)
        self.to_core = (y_hi * 8 + z * 2 + 1 - core, seq)

    def torus(self):
        return (
            self.to_z_up,
            self.to_z_down,
            self.to_x_up,
            self.to_x_down,
            self.to_pair,
            self.to_cross,
            self.to_core,
        )


def greet(peers):
    barrier = pltpu.get_barrier_semaphore()
    for peer in peers:
        pl.semaphore_signal(barrier, inc=1, device_id=peer, device_id_type=MESH)
    pl.semaphore_wait(barrier, len(peers))


GATHER_KINDS = (
    "own_up",
    "own_down",
    "on_up",
    "on_down",
    "cross_own",
    "cross_up",
    "cross_down",
    "cross_far",
    "other_up",
    "other_down",
    "other_on_up",
    "other_on_down",
) + tuple(f"share_{n}_{s}" for n in range(3) for s in ("up", "down", "far", "other"))
GATHER_KINDS += tuple(f"core_{s}" for s in ("own", "up", "down", "far", "other"))
KIND_AT = {kind: at for at, kind in enumerate(GATHER_KINDS)}
KINDS = len(GATHER_KINDS)


class Gather:
    def __init__(self, place, buffers, send_sem, recv_sem):
        self.place, self.buffers, self.send_sem, self.recv_sem = place, buffers, send_sem, recv_sem
        self.sent = []

    def region(self, g, kind, receiving):
        p = self.place
        rows, cols = GATHER_ROWS[g], GATHER_COLUMNS[g]
        shared = SHARED[g]
        here, there = p.y_hi, 1 - p.y_hi
        whole, top, low = pl.ds(0, rows), pl.ds(0, rows // 2), pl.ds(rows // 2, rows // 2)
        low_first = pl.ds(rows // 2, rows // 4)
        low_last = pl.ds(rows // 2 + rows // 4, rows // 4)
        color = p.color
        if kind.startswith("share") and receiving:
            color = 1 - color
        mine = pl.ds(pl.multiple_of(color * shared, 128), cols - shared)
        below, above = p.z_down, p.z_up
        z, far = p.z, p.z_far
        buf = self.buffers[g]

        def at(y, zz, r, c):
            return buf.at[y, zz, p.core, r, c]

        if kind == "own_up":
            return at(here, below if receiving else z, whole, mine), p.to_z_up
        if kind == "own_down":
            return at(here, above if receiving else z, whole, mine), p.to_z_down
        if kind == "on_up":
            return at(here, far if receiving else below, top, mine), p.to_z_up
        if kind == "on_down":
            return at(here, far if receiving else above, low, mine), p.to_z_down
        if kind.startswith("cross"):
            y = there if receiving else here
            which = kind[6:]
            if which == "own":
                return at(y, z, whole, mine), p.to_cross
            return at(y, {"up": above, "down": below, "far": far}[which], top, mine), p.to_cross
        if kind == "other_up":
            return at(there, below if receiving else z, low, mine), p.to_z_up
        if kind == "other_down":
            return at(there, above if receiving else z, low, mine), p.to_z_down
        if kind == "other_on_up":
            return at(there, far if receiving else below, low_first, mine), p.to_z_up
        if kind == "other_on_down":
            return at(there, far if receiving else above, low_last, mine), p.to_z_down
        if kind.startswith("share"):
            _, n, which = kind.split("_")
            n = int(n)
            start = color * (cols - shared) + sum(SHARES[g][:n])
            part = pl.ds(pl.multiple_of(start, 128), SHARES[g][n])
            to = (p.to_x_up, p.to_x_down, p.to_pair)[n]
            if which == "other":
                return buf.at[there, :, p.core, :, part], to
            return at(here, {"up": above, "down": below, "far": far}[which], whole, part), to
        which = kind[5:]
        core = 1 - p.core if receiving else p.core
        if which == "other":
            return buf.at[there, :, core], p.to_core
        return buf.at[here, {"own": z, "up": above, "down": below, "far": far}[which], core], p.to_core

    def copy(self, g, kind, receiving=False):
        region, to = self.region(g, kind, receiving)
        at = KIND_AT[kind]
        return pltpu.make_async_remote_copy(
            src_ref=region,
            dst_ref=region,
            send_sem=self.send_sem.at[g, at],
            recv_sem=self.recv_sem.at[g, at],
            device_id=to,
            device_id_type=MESH,
        )

    def send(self, g, *kinds):
        for kind in kinds:
            self.copy(g, kind).start()
            self.sent.append((g, kind))

    def take(self, g, *kinds):
        for kind in kinds:
            self.copy(g, kind, True).wait_recv()

    def share(self, g, which):
        self.send(g, *(f"share_{n}_{which}" for n in range(3)))

    def taken(self, g, which):
        self.take(g, *(f"share_{n}_{which}" for n in range(3)))

    def phase(self, number, g):
        if number == 0:
            self.send(g, "own_up", "own_down", "cross_own", "core_own")
        elif number == 1:
            self.take(g, "own_up", "own_down")
            self.send(g, "on_up", "on_down", "cross_up", "cross_down")
            self.share(g, "up")
            self.share(g, "down")
        elif number == 2:
            self.take(g, "cross_own")
            self.send(g, "other_up", "other_down")
        elif number == 8:
            self.take(g, "on_up", "on_down")
            self.send(g, "cross_far")
            self.share(g, "far")
        elif number == 3:
            self.take(g, "other_up", "other_down")
            self.send(g, "other_on_up", "other_on_down")
        elif number == 4:
            self.take(g, "cross_up", "cross_down", "cross_far", "other_on_up", "other_on_down")
            self.share(g, "other")
        elif number == 5:
            for which in ("up", "down", "far"):
                self.taken(g, which)
                self.send(g, f"core_{which}")
        elif number == 6:
            self.taken(g, "other")
            self.send(g, "core_other")
        else:
            self.take(g, "core_own", "core_up", "core_down", "core_far", "core_other")

    def finish(self, *groups):
        for g, kind in self.sent:
            if g in groups:
                self.copy(g, kind).wait_send()
        self.sent = [one for one in self.sent if one[0] not in groups]


def own_copies(place, shards, buffers):
    mine = [buf.at[place.y_hi, place.z, place.core] for buf in buffers]
    query, key, value, output, gate, up, down = shards
    first, last = pl.ds(0, 1536), pl.ds(1536, 1536)
    return (
        (query, mine[0].at[:, pl.ds(0, 2048)]),
        (key, mine[0].at[:, pl.ds(2048, 1024)]),
        (value, mine[0].at[:, pl.ds(3072, 1024)]),
        (output, mine[1]),
        (gate.at[:, first], mine[2].at[:, first]),
        (up.at[:, first], mine[2].at[:, last]),
        (gate.at[:, last], mine[3].at[:, first]),
        (up.at[:, last], mine[3].at[:, last]),
        (down, mine[4]),
    )


class GatherSmall:
    def __init__(self, place, buffer, send_sem, recv_sem):
        self.place, self.buffer, self.send_sem, self.recv_sem = place, buffer, send_sem, recv_sem

    def copy(self, step, receiving=False):
        p, buf = self.place, self.buffer
        if step == 0:
            region, to = buf.at[p.y_hi, p.z, 1 - p.core if receiving else p.core], p.to_core
        elif step == 1:
            region, to = buf.at[1 - p.y_hi if receiving else p.y_hi, p.z], p.to_cross
        elif step == 2:
            region, to = buf.at[:, p.z_down if receiving else p.z], p.to_z_up
        elif step == 3:
            region, to = buf.at[:, p.z_up if receiving else p.z], p.to_z_down
        else:
            region, to = buf.at[:, p.z_far if receiving else p.z_down], p.to_z_up
        return pltpu.make_async_remote_copy(
            src_ref=region,
            dst_ref=region,
            send_sem=self.send_sem.at[step],
            recv_sem=self.recv_sem.at[step],
            device_id=to,
            device_id_type=MESH,
        )

    def start(self, step):
        self.copy(step).start()

    def take(self, step):
        self.copy(step, True).wait_recv()

    def finish(self):
        for step in range(5):
            self.copy(step).wait_send()


PART_ORDER = ("xyz", "yzx", "zxy")
FREE = ((("yl", "yh", "z"), ("z",), ()), (("z", "x"), ("x",), ()), (("yl", "yh", "x"), ("yl", "yh"), ()))
EXTENT = {"yl": 2, "yh": 2, "z": 4, "x": 4}


def half_shape(part, step):
    free = FREE[part][step]
    first = EXTENT[free[0]] // 2
    return ((first,) if first > 1 else ()) + tuple(EXTENT[d] for d in free[1:])


def near_shape(part, step):
    return tuple(EXTENT[d] for d in FREE[part][step])


def reduce_scratch():
    shapes = []
    for g in range(4):
        rows, half = SHARD_ROWS[g] // 4, COLUMNS[g] // 2
        shapes.append(pltpu.VMEM((2, 2, 4, 4, rows, half), bf16))
        shapes.append(pltpu.VMEM((2, 4, rows, half), bf16))
        for part in range(3):
            tail = (rows, THIRDS[g][part])
            for step in range(3):
                if step < 2:
                    shapes.append(pltpu.VMEM((2,) + half_shape(part, step) + tail, bf16))
                else:
                    shapes.append(pltpu.VMEM((1,) + tail, bf16))
                shapes.append(pltpu.VMEM((2,) + near_shape(part, step) + tail, bf16))
    return shapes


SCRATCH_PER_GROUP = 2 + 18


def accumulate(dst, src):
    lead = dst.shape[:-2]
    count = 1
    for n in lead:
        count *= n
    if not lead:
        dst[...] = dst[...] + src[...]
        return

    def body(i, carry):
        at, rest = [], i
        for n in reversed(lead):
            at.append(rest % n)
            rest = rest // n
        at = tuple(reversed(at))
        dst.at[at][...] = dst.at[at][...] + src.at[at][...]
        return carry

    lax.fori_loop(0, count, body, 0)


class Reduce:
    def __init__(self, place, grads, scratch, send_sem, recv_sem, load_sem):
        self.place, self.grads = place, grads
        self.send_sem, self.recv_sem, self.load_sem = send_sem, recv_sem, load_sem
        self.sent = []
        self.groups = [scratch[g * SCRATCH_PER_GROUP : (g + 1) * SCRATCH_PER_GROUP] for g in range(4)]

    def total(self, g):
        return self.groups[g][0]

    def result(self, g):
        return self.groups[g][1]

    def halves(self, g, part, step):
        return self.groups[g][2 + (part * 3 + step) * 2]

    def nears(self, g, part, step):
        return self.groups[g][3 + (part * 3 + step) * 2]

    def cols(self, g, part):
        return pl.ds(sum(THIRDS[g][:part]), THIRDS[g][part])

    def moved(self, dim, by):
        p = self.place
        if dim == "x":
            x = (p.x + by) % 4
            return {"x": x}, (p.dp, x * 2 + p.y_lo)
        if dim == "z":
            z = (p.z + by) % 4
            return {"z": z}, (p.y_hi * 8 + z * 2 + p.core, p.seq)
        y = (p.y_hi * 2 + p.y_lo + by) % 4
        return {"yl": y % 2, "yh": y // 2}, ((y // 2) * 8 + p.z * 2 + p.core, p.x * 2 + y % 2)

    def chunk(self, g, part, step, by, half=None):
        at = {}
        for earlier in range(step):
            at.update(self.moved(PART_ORDER[part][earlier], 0)[0])
        at.update(self.moved(PART_ORDER[part][step], by)[0])
        if half is not None:
            cut = FREE[part][step][0]
            size = EXTENT[cut] // 2
            at[cut] = half if size == 1 else pl.ds(half * size, size)
        index = tuple(at.get(name, slice(None)) for name in ("yl", "yh", "z", "x"))
        return self.total(g).at[index + (slice(None), self.cols(g, part))]

    def remote(self, g, sem, src, dst, to):
        return pltpu.make_async_remote_copy(
            src_ref=src,
            dst_ref=dst,
            send_sem=self.send_sem.at[g, sem],
            recv_sem=self.recv_sem.at[g, sem],
            device_id=to,
            device_id_type=MESH,
        )

    def send(self, g, sem, src, dst, to):
        copy = self.remote(g, sem, src, dst, to)
        copy.start()
        self.sent.append(copy)

    def take(self, g, sem, dst):
        self.remote(g, sem, dst, dst, self.place.to_core).wait_recv()

    def load(self, g):
        return pltpu.make_async_copy(self.grads[g], self.total(g), self.load_sem.at[g])

    def send_far(self, g, step):
        for part in range(3):
            sem, dim = part * 12 + step * 4, PART_ORDER[part][step]
            buf = self.halves(g, part, step)
            up, down = self.moved(dim, 1)[1], self.moved(dim, 3)[1]
            if step < 2:
                self.send(g, sem, self.chunk(g, part, step, 2, 0), buf.at[0], up)
                self.send(g, sem + 1, self.chunk(g, part, step, 2, 1), buf.at[1], down)
            else:
                self.send(g, sem, self.chunk(g, part, step, 2), buf.at[0], up)

    def send_near(self, g, step):
        for part in range(3):
            sem, dim = part * 12 + step * 4, PART_ORDER[part][step]
            buf, near = self.halves(g, part, step), self.nears(g, part, step)
            up, down = self.moved(dim, 1)[1], self.moved(dim, 3)[1]
            self.take(g, sem, buf.at[0])
            accumulate(self.chunk(g, part, step, 1, 0 if step < 2 else None), buf.at[0])
            self.send(g, sem + 2, self.chunk(g, part, step, 1), near.at[0], up)
            if step < 2:
                self.take(g, sem + 1, buf.at[1])
                accumulate(self.chunk(g, part, step, 3, 1), buf.at[1])
            self.send(g, sem + 3, self.chunk(g, part, step, 3), near.at[1], down)

    def join_near(self, g, step):
        for part in range(3):
            sem, near = part * 12 + step * 4, self.nears(g, part, step)
            for way in range(2):
                self.take(g, sem + 2 + way, near.at[way])
                accumulate(self.chunk(g, part, step, 0), near.at[way])

    def stage(self, number, g):
        p = self.place
        result = self.result(g)
        if number == 0:
            if self.grads[g] is not None:
                self.load(g).wait()
            self.send_far(g, 0)
        elif number in (1, 3, 5):
            self.send_near(g, number // 2)
        elif number in (2, 4):
            self.join_near(g, number // 2 - 1)
            self.send_far(g, number // 2)
        elif number == 6:
            self.join_near(g, 2)
            result.at[p.y_lo, p.x][...] = self.total(g).at[p.y_lo, p.y_hi, p.z, p.x][...]
            mine = result.at[p.y_lo, p.x]
            self.send(g, 37, mine, mine, p.to_pair)
        elif number == 7:
            self.take(g, 37, result.at[1 - p.y_lo, p.x])
            mine = result.at[:, p.x]
            self.send(g, 38, mine, mine, p.to_x_up)
            self.send(g, 39, mine, mine, p.to_x_down)
        elif number == 8:
            below, above = (p.x + 3) % 4, (p.x + 1) % 4
            self.take(g, 38, result.at[:, below])
            self.send(g, 40, result.at[0, below], result.at[0, below], p.to_x_up)
            self.take(g, 39, result.at[:, above])
            self.send(g, 41, result.at[1, above], result.at[1, above], p.to_x_down)
        else:
            far = (p.x + 2) % 4
            self.take(g, 40, result.at[0, far])
            self.take(g, 41, result.at[1, far])

    def finish(self):
        for copy in self.sent:
            copy.wait_send()
        self.sent = []


class ReduceSmall:
    STEPS = (("core", 2), ("pair", 2), ("cross", 2), ("x", 4), ("z", 4))

    def __init__(self, place, slots, send_sem, recv_sem):
        self.place, self.slots, self.send_sem, self.recv_sem = place, slots, send_sem, recv_sem

    def peers(self, step):
        p = self.place
        name, count = self.STEPS[step]
        if count == 2:
            mine, to = {
                "core": (p.core, p.to_core),
                "pair": (p.y_lo, p.to_pair),
                "cross": (p.y_hi, p.to_cross),
            }[name]
            return mine, [(1 - mine, to)]
        if name == "x":
            return p.x, [((p.x + by) % 4, (p.dp, (p.x + by) % 4 * 2 + p.y_lo)) for by in (1, 2, 3)]
        return p.z, [
            ((p.z + by) % 4, (p.y_hi * 8 + (p.z + by) % 4 * 2 + p.core, p.seq)) for by in (1, 2, 3)
        ]

    def copies(self, step, receiving):
        mine, peers = self.peers(step)
        if receiving:
            peers = peers[::-1]
        for at, (place, to) in enumerate(peers):
            slot = self.slots.at[step, place if receiving else mine]
            yield pltpu.make_async_remote_copy(
                src_ref=slot,
                dst_ref=slot,
                send_sem=self.send_sem.at[step, at],
                recv_sem=self.recv_sem.at[step, at],
                device_id=to,
                device_id_type=MESH,
            )

    def put(self, step, values):
        mine, _ = self.peers(step)
        self.slots.at[step, mine][...] = values
        for copy in self.copies(step, False):
            copy.start()

    def sum(self, step):
        for copy in self.copies(step, True):
            copy.wait_recv()
        for copy in self.copies(step, False):
            copy.wait_send()
        total = self.slots[step, 0]
        for at in range(1, self.STEPS[step][1]):
            total = total + self.slots[step, at]
        return total


SCALE = 128 ** (-0.5)
OFFSETS = tuple((dx, dy) for dx in range(4) for dy in range(2) if (dx, dy) != (0, 0))


def mm(left, right):
    return jnp.dot(left, right, preferred_element_type=f32)


def mm_nt(left, right):
    return lax.dot_general(left, right, (((1,), (1,)), ((), ())), preferred_element_type=f32)


def mm_tn(left, right):
    return lax.dot_general(left, right, (((0,), (0,)), ((), ())), preferred_element_type=f32)


def inv_rms(v):
    return lax.rsqrt(jnp.mean(v * v, axis=-1, keepdims=True) + epsilon)


class Exchange:
    def __init__(self, place, send_sem, recv_sem):
        self.place, self.send_sem, self.recv_sem, self.sent = place, send_sem, recv_sem, []

    def partner(self, at, back=False):
        dx, dy = OFFSETS[at]
        x = (self.place.x + (4 - dx if back else dx)) % 4
        return x * 2 + (self.place.y_lo + dy) % 2

    def send(self, kind, src, dst):
        for at in range(7):
            partner = self.partner(at)
            copy = pltpu.make_async_remote_copy(
                src_ref=src(partner),
                dst_ref=dst(self.place.seq),
                send_sem=self.send_sem.at[kind, at],
                recv_sem=self.recv_sem.at[kind, at],
                device_id=(self.place.dp, partner),
                device_id_type=MESH,
            )
            copy.start()
            self.sent.append(copy)

    def take(self, kind, dst):
        for at in range(7):
            partner = self.partner(at, back=True)
            pltpu.make_async_remote_copy(
                src_ref=dst(partner),
                dst_ref=dst(partner),
                send_sem=self.send_sem.at[kind, at],
                recv_sem=self.recv_sem.at[kind, at],
                device_id=(self.place.dp, partner),
                device_id_type=MESH,
            ).wait_recv()

    def finish(self):
        for copy in self.sent:
            copy.wait_send()
        self.sent = []


def token_rows(seq):
    return pl.ds(pl.multiple_of(seq * 128, 128), 128)


def head_cols(seq, width):
    return pl.ds(pl.multiple_of(seq * width, 128), width)


def gain_rows(tile_ref):
    tiles = tile_ref[...].astype(f32).reshape(8, 2, 16, 128)
    pairs = tiles[:, 0] + tiles[:, 1]
    total = pairs[0]
    for at in range(1, 8):
        total = total + pairs[at]

    def wide(row):
        return jnp.concatenate([pairs[at, row : row + 1, :] for at in range(8)], axis=-1)

    return wide(0), total[1:2, :], total[2:3, :], wide(3)


def causal_scores(q, k, first):
    scores = mm_nt(q, k) * SCALE
    row = first + lax.broadcasted_iota(jnp.int32, scores.shape, 0)
    col = lax.broadcasted_iota(jnp.int32, scores.shape, 1)
    return jnp.where(col <= row, scores, -1e30)


FORWARD_IN = (
    "w_query", "w_key", "w_value", "w_output", "w_gate", "w_up", "w_down", "gains",
    "hidden", "cot", "cos", "sin", "valid",
)
FORWARD_OUT = (
    "out", "d_residual", "d_attended", "dg_ffn", "x_in", "q_flat", "k_flat",
    "total_output", "total_gate_up", "total_down", "weights_qkv", "q_heads", "k_heads", "v_heads", "gain_tiles",
)
FORWARD_SCRATCH = (
    "buf_qkv", "buf_output", "buf_gate_up_0", "buf_gate_up_1", "buf_down", "tiles", "rows", "core_down",
    "q_in", "k_in", "v_in", "att", "context", "residual", "mid_in", "result", "d_mid", "d_branch",
    "gather_send", "gather_recv", "small_send", "small_recv", "local_sem", "swap_send", "swap_recv", "out_sem",
    "core_free", "core_send", "core_recv",
    "out_out", "d_residual_out", "d_attended_out", "x_in_out", "q_flat_out", "k_flat_out",
)
FF_TILE = 768


def forward_kernel(*refs):
    r = dict(zip(FORWARD_IN + FORWARD_OUT + FORWARD_SCRATCH, refs))
    place = Place()
    me = place.seq
    buffers = [r["buf_qkv"], r["buf_output"], r["buf_gate_up_0"], r["buf_gate_up_1"], r["buf_down"]]
    tiles = r["tiles"]
    pairs = own_copies(place, [r[name] for name in FORWARD_IN[:7]], buffers)
    pairs += ((r["gains"], tiles.at[place.y_hi, place.z, place.core]),)
    copies = [
        pltpu.make_async_copy(shard, there, r["local_sem"].at[at]) for at, (shard, there) in enumerate(pairs)
    ]
    for copy in copies:
        copy.start()
    greet(
        place.torus()
        + tuple(
            (place.dp, (place.x + dx) % 4 * 2 + (place.y_lo + dy) % 2)
            for dx, dy in OFFSETS
            if (dx, dy) not in ((1, 0), (3, 0), (0, 1))
        )
    )
    for copy in copies:
        copy.wait()
    gather = Gather(place, buffers, r["gather_send"], r["gather_recv"])
    little = GatherSmall(place, tiles, r["small_send"], r["small_recv"])
    swap = Exchange(place, r["swap_send"], r["swap_recv"])
    saved = []

    def save(name, src, dst=None):
        at = len(saved)
        copy = pltpu.make_async_copy(src, r[name] if dst is None else dst, r["out_sem"].at[at])
        copy.start()
        saved.append(copy)

    def phases(*steps):
        for number, g in steps:
            gather.phase(number, g)

    little.start(0)
    phases((0, 0))
    little.take(0)
    little.start(1)
    little.take(1)
    little.start(2)
    little.start(3)
    little.take(2)
    little.take(3)
    little.start(4)
    phases((0, 1), (1, 0), (2, 0), (8, 0), (3, 0), (0, 2), (1, 1), (2, 1), (4, 0))
    little.take(4)
    g_attn, g_query, g_key, g_ffn = gain_rows(tiles)
    x = r["hidden"][...].reshape(256, 1024).astype(f32)
    r["x_in_out"][...] = (x * inv_rms(x) * g_attn).astype(bf16)
    phases((5, 0), (6, 0), (8, 1), (3, 1), (1, 2), (4, 1), (5, 1), (0, 4), (7, 0))
    save("weights_qkv", buffers[0])
    save("gain_tiles", tiles)

    cos, sin = r["cos"], r["sin"]

    def qkv_weights(first):
        return buffers[0][:, :, :, :, pl.ds(pl.multiple_of(first, 128), 512)].reshape(1024, 512)

    def head_tile(j, flat_ref, rows_ref, first, gain):
        flat = mm(r["x_in_out"][...], qkv_weights(first + j * 512))
        cols = pl.ds(pl.multiple_of(j * 512, 128), 512)
        flat_ref[:, cols] = flat
        done = []
        for h in range(4):
            v = flat[:, h * 128 : (h + 1) * 128]
            v = v * inv_rms(v) * gain
            done.append((v * cos[...] + pltpu.roll(v, 64, 1) * sin[...]).astype(bf16))
        rows_ref[...] = jnp.concatenate(done, axis=-1).reshape(2, 128, 512)

    def query_tile(j, carry):
        head_tile(j, r["q_flat_out"], r["rows"].at[0, :, :, pl.ds(pl.multiple_of(j * 512, 128), 512)], 0, g_query)
        return carry

    def key_tile(j, carry):
        head_tile(j, r["k_flat_out"], r["rows"].at[1, :, :, pl.ds(pl.multiple_of(j * 512, 128), 512)], 2048, g_key)
        return carry

    def value_tile(j, carry):
        cols = pl.ds(pl.multiple_of(1024 + j * 512, 128), 512)
        r["rows"][1, :, :, cols] = mm(r["x_in_out"][...], qkv_weights(3072 + j * 512)).astype(bf16).reshape(2, 128, 512)
        return carry

    def to_heads(kind, at, first, heads, width):
        def cols(seq):
            return pl.ds(pl.multiple_of(first + seq * width, 128), width)

        swap.send(
            kind,
            lambda partner: r["rows"].at[at, :, :, cols(partner)],
            lambda sender: r[heads].at[:, token_rows(sender), :],
        )
        r[heads][:, token_rows(me), :] = r["rows"][at, :, :, cols(me)]

    lax.fori_loop(0, 4, query_tile, 0)
    to_heads(0, 0, 0, "q_in", 256)
    lax.fori_loop(0, 2, key_tile, 0)
    to_heads(1, 1, 0, "k_in", 128)
    lax.fori_loop(0, 2, value_tile, 0)
    to_heads(2, 1, 1024, "v_in", 128)
    phases((0, 3), (2, 2), (3, 2), (8, 2), (1, 3), (1, 4), (2, 4), (2, 3), (4, 2), (8, 4), (3, 4), (6, 1))
    save("x_in", r["x_in_out"])
    save("q_flat", r["q_flat_out"])
    save("k_flat", r["k_flat_out"])
    swap.take(0, lambda sender: r["q_in"].at[:, token_rows(sender), :])
    swap.take(1, lambda sender: r["k_in"].at[:, token_rows(sender), :])
    swap.take(2, lambda sender: r["v_in"].at[:, token_rows(sender), :])
    save("q_heads", r["q_in"])
    save("k_heads", r["k_in"])
    save("v_heads", r["v_in"])

    def attend(slot, head):
        cols = slice(head * 128, (head + 1) * 128)
        for block in range(4):
            rows, upto = slice(block * 256, (block + 1) * 256), (block + 1) * 256
            q = r["q_in"][slot, rows, cols]
            scores = causal_scores(q, r["k_in"][slot, :upto, :], block * 256)
            top = jnp.max(scores, axis=-1, keepdims=True)
            shifted = jnp.exp(scores - top)
            total = jnp.sum(shifted, axis=-1, keepdims=True)
            prob = (shifted * (1.0 / total)).astype(bf16)
            r["att"][slot, rows, cols] = mm(prob, r["v_in"][slot, :upto, :]).astype(bf16)

    for slot in range(2):
        attend(slot, 0)
        attend(slot, 1)
        swap.send(
            3 + slot,
            lambda partner: r["att"].at[slot, token_rows(partner), :],
            lambda sender: r["context"].at[slot, :, head_cols(sender, 256)],
        )
        r["context"][slot, :, head_cols(me, 256)] = r["att"][slot, token_rows(me), :]
        if slot == 0:
            phases((7, 1), (5, 2), (3, 3))
    phases((4, 4), (8, 3), (5, 4))
    for slot in range(2):
        swap.take(3 + slot, lambda sender: r["context"].at[slot, :, head_cols(sender, 256)])

    for half in range(2):
        cols = slice(half * 512, (half + 1) * 512)
        weights = buffers[1][:, :, :, :, cols].reshape(2048, 512)
        x = r["hidden"][:, :, cols].reshape(256, 512).astype(f32)
        r["residual"][:, cols] = x + mm(r["context"][...].reshape(256, 2048), weights)
    residual = r["residual"][...]
    r["mid_in"][...] = (residual * inv_rms(residual) * g_ffn).astype(bf16)


    def masked(values):
        order = lax.broadcasted_iota(jnp.int32, (128, 1024), 0).astype(f32)
        parts = [
            jnp.where(order < r["valid"][slot, :1, :1], values[slot * 128 : (slot + 1) * 128], 0.0)
            for slot in range(2)
        ]
        return jnp.concatenate(parts, axis=0)

    d_result = masked(r["cot"][...].reshape(256, 1024).astype(f32))
    r["d_branch"][...] = d_result.astype(bf16)
    phases((6, 2), (4, 3), (6, 4), (5, 3), (7, 4), (7, 2), (6, 3))
    gather.finish(0, 2, 4)
    little.finish()
    swap.finish()
    for copy in saved:
        copy.wait()
    saved.clear()
    pl.semaphore_signal(r["core_free"], inc=1, device_id=place.to_core, device_id_type=MESH)
    pl.semaphore_wait(r["core_free"], 1)
    core, other = place.core, 1 - place.core

    def to_core(src, dst, *at):
        return pltpu.make_async_remote_copy(
            src_ref=src,
            dst_ref=dst,
            send_sem=r["core_send"].at[at],
            recv_sem=r["core_recv"].at[at],
            device_id=place.to_core,
            device_id_type=MESH,
        )

    def ffn_places(f):
        here = pl.ds(pl.multiple_of(f % 2 * FF_TILE, 128), FF_TILE)
        up = pl.ds(pl.multiple_of(1536 + f % 2 * FF_TILE, 128), FF_TILE)
        there = pl.ds(pl.multiple_of(f * FF_TILE, 128), FF_TILE)
        return here, up, there, pl.ds(f % 2 * 2, 2)

    def ffn_copies(b, f):
        here, up, there, z = ffn_places(f)
        weights = buffers[2 + b]
        return (
            to_core(weights.at[:, :, other, :, here], buffers[0].at[:, :, 0, :, there], f, 0),
            to_core(weights.at[:, :, other, :, up], buffers[0].at[:, :, 1, :, there], f, 1),
            to_core(buffers[4].at[b, z, other], r["core_down"].at[b, z], f, 2),
        )

    def ffn_join(b, f):
        here, up, there, z = ffn_places(f)
        weights = buffers[2 + b]
        for copy in ffn_copies(b, f):
            copy.wait_recv()
        weights[:, :, core, :, here] = weights[:, :, core, :, here] + buffers[0][:, :, 0, :, there]
        weights[:, :, core, :, up] = weights[:, :, core, :, up] + buffers[0][:, :, 1, :, there]
        buffers[4][b, z, core] = buffers[4][b, z, core] + r["core_down"][b, z]

    r["result"][...] = residual
    r["d_mid"][...] = jnp.zeros((256, 1024), f32)

    def ffn_tile(b, f):
        gate_cols, up_cols, _, z = ffn_places(f)
        w_gate = buffers[2 + b][:, :, :, :, gate_cols].reshape(1024, FF_TILE)
        w_up = buffers[2 + b][:, :, :, :, up_cols].reshape(1024, FF_TILE)
        w_down = buffers[4][b, z].reshape(FF_TILE, 1024)
        mid, d_branch = r["mid_in"][...], r["d_branch"][...]
        gate, up = mm(mid, w_gate), mm(mid, w_up)
        sig = 1.0 / (1.0 + jnp.exp(-gate))
        silu = gate * sig
        unit = (silu * up).astype(bf16)
        d_unit = mm_nt(d_branch, w_down)
        d_gate = (d_unit * up * (sig * (1.0 + gate * (1.0 - sig)))).astype(bf16)
        d_up = (d_unit * silu).astype(bf16)
        r["result"][...] += mm(unit, w_down)
        r["d_mid"][...] += mm_nt(d_gate, w_gate) + mm_nt(d_up, w_up)
        shape = (4, 2, 64, FF_TILE)
        for part in range(2):
            mid_part = mid[:, part * 512 : (part + 1) * 512]
            buffers[2 + b][part, :, :, :, gate_cols] = mm_tn(mid_part, d_gate).astype(bf16).reshape(shape)
            buffers[2 + b][part, :, :, :, up_cols] = mm_tn(mid_part, d_up).astype(bf16).reshape(shape)
        buffers[4][b, z] = mm_tn(unit, d_branch).astype(bf16).reshape(2, 2, 192, 1024)
        for copy in ffn_copies(b, f):
            copy.start()

    def first_half(f, carry):
        ffn_tile(0, f)

        @pl.when(f > 0)
        def _():
            ffn_join(0, f - 1)

        return carry

    def last_half(f, carry):
        ffn_tile(1, f)

        @pl.when(f > 2)
        def _():
            ffn_join(1, f - 1)

        return carry

    lax.fori_loop(0, 2, first_half, 0)
    phases((7, 3))
    gather.finish(1, 3)
    ffn_join(0, 1)
    lax.fori_loop(2, 4, last_half, 0)
    r["out_out"][...] = masked(r["result"][...]).astype(bf16).reshape(2, 128, 1024)
    save("out", r["out_out"])

    residual, d_mid = r["residual"][...], r["d_mid"][...]
    scale = inv_rms(residual)
    weighed = g_ffn * d_mid
    d_norm = scale * weighed - residual * (scale * scale * scale) * jnp.mean(
        residual * weighed, axis=-1, keepdims=True
    )
    r["dg_ffn"][...] = jnp.sum(d_mid * residual * scale, axis=0, keepdims=True)
    d_result = masked(r["cot"][...].reshape(256, 1024).astype(f32))
    r["d_residual_out"][...] = d_result + d_norm
    r["d_branch"][...] = r["d_residual_out"][...].astype(bf16)

    def output_tile(j, carry):
        y, z = j // 2, j % 2 * 2
        cols = pl.ds(pl.multiple_of(j * 512, 128), 512)
        d_attn = r["d_branch"][...]
        weights = buffers[1][y, pl.ds(z, 2)].reshape(512, 1024)
        r["d_attended_out"][:, :, cols] = mm_nt(d_attn, weights).astype(bf16).reshape(2, 128, 512)
        context = r["context"][:, :, cols].reshape(256, 512)
        buffers[1][y, pl.ds(z, 2)] = mm_tn(context, d_attn).astype(bf16).reshape(2, 2, 128, 1024)
        for copy in output_copies(j):
            copy.start()
        return carry

    def output_copies(j):
        y, z = j // 2, j % 2
        return tuple(
            to_core(
                buffers[1].at[y, z * 2 + k, other],
                r["rows"].at[y, z, :, pl.ds(k * 1024, 1024)],
                4 + j,
                k,
            )
            for k in range(2)
        )

    lax.fori_loop(0, 4, output_tile, 0)
    save("d_residual", r["d_residual_out"])
    save("d_attended", r["d_attended_out"])
    ffn_join(1, 3)
    for half in range(2):
        for b in range(2):
            save(
                "total_gate_up",
                buffers[2 + b].at[:, :, core, :, pl.ds(half * 1536, 1536)],
                r["total_gate_up"].at[half, :, :, :, pl.ds(b * 1536, 1536)],
            )
        save("total_down", buffers[4].at[:, :, core, :, pl.ds(half * 512, 512)], r["total_down"].at[half])

    def output_join(j, carry):
        y, z = j // 2, j % 2
        for k, copy in enumerate(output_copies(j)):
            copy.wait_recv()
            cols = slice(k * 1024, (k + 1) * 1024)
            buffers[1][y, z * 2 + k, core] = buffers[1][y, z * 2 + k, core] + r["rows"][y, z, :, cols]
        return carry

    lax.fori_loop(0, 4, output_join, 0)
    for half in range(2):
        save("total_output", buffers[1].at[:, :, core, :, pl.ds(half * 512, 512)], r["total_output"].at[half])
    for at in range(4):
        for copy in ffn_copies(at // 2, at) + output_copies(at):
            copy.wait_send()
    for copy in saved:
        copy.wait()


def forward(shards, gains, hidden, cot, cos, sin, valid):
    def shape(*dims, dtype=bf16):
        return jax.ShapeDtypeStruct(dims, dtype)

    outs = {
        "out": shape(2, 128, 1024),
        "d_residual": shape(256, 1024, dtype=f32),
        "d_attended": shape(2, 128, 2048),
        "dg_ffn": shape(1, 1024, dtype=f32),
        "x_in": shape(256, 1024),
        "q_flat": shape(256, 2048, dtype=f32),
        "k_flat": shape(256, 1024, dtype=f32),
        "total_output": shape(2, 2, 4, 128, 512),
        "total_gate_up": shape(2, 2, 4, 64, 3072),
        "total_down": shape(2, 2, 4, 192, 512),
        "weights_qkv": shape(2, 4, 2, 64, 4096),
        "q_heads": shape(2, 1024, 256),
        "k_heads": shape(2, 1024, 128),
        "v_heads": shape(2, 1024, 128),
        "gain_tiles": shape(2, 4, 2, 16, 128),
    }
    vmem = pl.BlockSpec(memory_space=pltpu.VMEM)
    hbm = pl.BlockSpec(memory_space=pl.ANY)
    scratch = {
        "buf_qkv": (2, 4, 2, 64, 4096),
        "buf_output": (2, 4, 2, 128, 1024),
        "buf_gate_up_0": (2, 4, 2, 64, 3072),
        "buf_gate_up_1": (2, 4, 2, 64, 3072),
        "buf_down": (2, 4, 2, 192, 1024),
        "tiles": (2, 4, 2, 16, 128),
        "rows": (2, 2, 128, 2048),
        "core_down": (2, 4, 192, 1024),
        "q_in": (2, 1024, 256),
        "k_in": (2, 1024, 128),
        "v_in": (2, 1024, 128),
        "att": (2, 1024, 256),
        "context": (2, 128, 2048),
        "residual": ((256, 1024), f32),
        "mid_in": (256, 1024),
        "result": ((256, 1024), f32),
        "d_mid": ((256, 1024), f32),
        "d_branch": (256, 1024),
    }
    dma = pltpu.SemaphoreType.DMA
    sems = [dma((5, KINDS)), dma((5, KINDS)), dma((5,)), dma((5,)), dma((10,)), dma((5, 7)), dma((5, 7)), dma((11,))]
    sems += [pltpu.SemaphoreType.REGULAR, dma((8, 3)), dma((8, 3))]
    buffers = [
        pltpu.VMEM(*(dims if isinstance(dims[0], tuple) else (dims, bf16))) for dims in scratch.values()
    ]
    results = pl.pallas_call(
        functools.partial(forward_kernel),
        out_shape=list(outs.values()),
        in_specs=[hbm] * 8 + [vmem] * 5,
        out_specs=[vmem if name == "dg_ffn" else hbm for name in outs],
        scratch_shapes=buffers
        + sems
        + [
            pltpu.VMEM(outs[name].shape, outs[name].dtype)
            for name in ("out", "d_residual", "d_attended", "x_in", "q_flat", "k_flat")
        ],
        compiler_params=pltpu.CompilerParams(
            collective_id=1, has_side_effects=True, vmem_limit_bytes=63 * 1024 * 1024
        ),
        name="forward",
    )(*shards, gains, hidden, cot, cos, sin, valid)
    return dict(zip(outs, results))


BACKWARD_IN = (
    "total_output", "total_gate_up", "total_down", "weights_qkv", "d_attended", "q_heads", "k_heads", "v_heads",
    "q_flat", "k_flat", "x_in", "hidden", "d_residual", "cos", "sin", "gain_tiles", "dg_ffn",
)
BACKWARD_OUT = ("d_input", "gains_sum", "sum_qkv", "sum_output", "sum_gate_up", "sum_down")
BACKWARD_SCRATCH = (
    "buf_qkv", "q_in", "k_in", "v_in", "grad_in", "dq", "dk", "dv", "dk_sum", "dv_sum", "dq_rows", "dk_rows", "dv_rows",
    "q_flat_in", "k_flat_in", "x_in_in", "hidden_in", "d_residual_in", "cos_in", "sin_in", "tiles_in", "dg_ffn_in", "d_x", "dg_query", "dg_key", "slots",
    "reduce_send", "reduce_recv", "load_sem", "small_send", "small_recv", "out_sem", "swap_send", "swap_recv", "in_sem",
)
BACKWARD_ORDER = (
    (0, 2),
    ("attention", 0),
    ("attention", 1),
    (0, 3),
    (1, 2),
    ("rows",),
    ("keys_values",),
    ("queries",),
    (0, 1),
    (1, 3),
    ("join_cores",),
    ("input_grad",),
    (0, 0),
    (2, 2),
    ("small", 0),
    (1, 1),
    (2, 3),
    ("small", 1),
    (1, 0),
    (2, 1),
    ("small", 2),
    (3, 3),
    (3, 2),
    ("small", 3),
    (3, 1),
    (2, 0),
    ("small", 4),
    (4, 3),
    (4, 2),
    (4, 1),
    (5, 3),
    (3, 0),
    (6, 3),
    (5, 1),
    (5, 2),
    (4, 0),
    (7, 3),
    (6, 1),
    (6, 2),
    (5, 0),
    (7, 1),
    (8, 3),
    (7, 2),
    (8, 1),
    (6, 0),
    (7, 0),
    (9, 1),
    (8, 2),
    (8, 0),
    (9, 3),
    (9, 0),
    (9, 2),
)
LATE_LOADS = (
    "q_flat", "k_flat", "x_in", "weights_qkv", "hidden", "d_residual", "cos", "sin", "gain_tiles", "dg_ffn",
)


def backward_kernel(*refs):
    names = BACKWARD_IN + BACKWARD_OUT
    count = 4 * SCRATCH_PER_GROUP
    r = dict(zip(names, refs))
    scratch = refs[len(names) : len(names) + count]
    r.update(zip(BACKWARD_SCRATCH, refs[len(names) + count :]))
    place = Place()
    me = place.seq
    loads = {
        name: pltpu.make_async_copy(r[name], r[there], r["in_sem"].at[at])
        for at, (name, there) in enumerate(
            (
                ("q_heads", "q_in"),
                ("k_heads", "k_in"),
                ("v_heads", "v_in"),
                ("q_flat", "q_flat_in"),
                ("k_flat", "k_flat_in"),
                ("x_in", "x_in_in"),
                ("weights_qkv", "buf_qkv"),
                ("hidden", "hidden_in"),
                ("d_residual", "d_residual_in"),
                ("cos", "cos_in"),
                ("sin", "sin_in"),
                ("gain_tiles", "tiles_in"),
                ("dg_ffn", "dg_ffn_in"),
            )
        )
    }
    grads = (None, r["total_output"], r["total_gate_up"], r["total_down"])
    outs = (r["sum_qkv"], r["sum_output"], r["sum_gate_up"], r["sum_down"])
    reduce = Reduce(place, grads, scratch, r["reduce_send"], r["reduce_recv"], r["load_sem"])
    little = ReduceSmall(place, r["slots"], r["small_send"], r["small_recv"])
    swap = Exchange(place, r["swap_send"], r["swap_recv"])
    for name in ("q_heads", "k_heads", "v_heads"):
        loads[name].start()
    reduce.load(3).start()
    greet(
        place.torus()
        + tuple(
            (place.dp, (place.x + dx) % 4 * 2 + (place.y_lo + dy) % 2)
            for dx, dy in OFFSETS
            if (dx, dy) not in ((1, 0), (3, 0), (0, 1))
        )
        + ((place.y_hi * 8 + place.z_far * 2 + place.core, place.seq),)
    )
    own = []
    for slot in range(2):
        swap.send(
            slot,
            lambda partner: r["d_attended"].at[slot, :, head_cols(partner, 256)],
            lambda sender: r["grad_in"].at[slot, token_rows(sender), :],
        )
        copy = pltpu.make_async_copy(
            r["d_attended"].at[slot, :, head_cols(me, 256)], r["grad_in"].at[slot, token_rows(me), :], r["in_sem"].at[13 + slot]
        )
        copy.start()
        own.append(copy)
    reduce.load(2).start()
    reduce.load(1).start()
    for name in LATE_LOADS:
        loads[name].start()

    def stages(*steps):
        for number, g in steps:
            reduce.stage(number, g)
            if number == 9:
                pltpu.make_async_copy(reduce.result(g), outs[g], r["out_sem"].at[g]).start()

    for name in ("q_heads", "k_heads", "v_heads"):
        loads[name].wait()

    def attend_back(slot, head):
        cols = slice(head * 128, (head + 1) * 128)
        if head == 0:
            r["dk_sum"][...] = jnp.zeros((1024, 128), f32)
            r["dv_sum"][...] = jnp.zeros((1024, 128), f32)
        for block in range(4):
            rows, upto = slice(block * 256, (block + 1) * 256), (block + 1) * 256
            q, grad = r["q_in"][slot, rows, cols], r["grad_in"][slot, rows, cols]
            k, v = r["k_in"][slot, :upto, :], r["v_in"][slot, :upto, :]
            scores = mm_nt(k, q) * SCALE
            key = lax.broadcasted_iota(jnp.int32, scores.shape, 0)
            query = block * 256 + lax.broadcasted_iota(jnp.int32, scores.shape, 1)
            scores = jnp.where(key <= query, scores, -1e30)
            shifted = jnp.exp(scores - jnp.max(scores, axis=0, keepdims=True))
            prob = shifted * (1.0 / jnp.sum(shifted, axis=0, keepdims=True))
            d_prob = mm_nt(v, grad)
            dot = jnp.sum(prob * d_prob, axis=0, keepdims=True)
            d_score = (prob * (d_prob - dot) * SCALE).astype(bf16)
            r["dk_sum"][:upto, :] += mm(d_score, q)
            r["dv_sum"][:upto, :] += mm(prob.astype(bf16), grad)
            r["dq"][slot, rows, cols] = mm_tn(d_score, k).astype(bf16)

    def to_rows(kind, slot, heads, rows, width):
        swap.send(
            kind,
            lambda partner: r[heads].at[slot, token_rows(partner), :],
            lambda sender: r[rows].at[slot, :, head_cols(sender, width)],
        )
        r[rows][slot, :, head_cols(me, width)] = r[heads][slot, token_rows(me), :]

    def attention(slot):
        own[slot].wait()
        swap.take(slot, lambda sender: r["grad_in"].at[slot, token_rows(sender), :])
        attend_back(slot, 0)
        attend_back(slot, 1)
        r["dk"][slot] = r["dk_sum"][...].astype(bf16)
        r["dv"][slot] = r["dv_sum"][...].astype(bf16)
        to_rows(2 + 3 * slot, slot, "dq", "dq_rows", 256)
        to_rows(3 + 3 * slot, slot, "dk", "dk_rows", 128)
        to_rows(4 + 3 * slot, slot, "dv", "dv_rows", 128)

    gains = {}

    def rows():
        for name in LATE_LOADS:
            loads[name].wait()
        gains["attn"], gains["query"], gains["key"], _ = gain_rows(r["tiles_in"])
        for slot in range(2):
            swap.take(2 + 3 * slot, lambda sender: r["dq_rows"].at[slot, :, head_cols(sender, 256)])
            swap.take(3 + 3 * slot, lambda sender: r["dk_rows"].at[slot, :, head_cols(sender, 128)])
            swap.take(4 + 3 * slot, lambda sender: r["dv_rows"].at[slot, :, head_cols(sender, 128)])
        r["d_x"][...] = jnp.zeros((256, 1024), f32)
        r["dg_query"][...] = jnp.zeros((1, 128), f32)
        r["dg_key"][...] = jnp.zeros((1, 128), f32)

    cos, sin = r["cos_in"], r["sin_in"]

    def project_back(d_flat, first):
        cols = pl.ds(pl.multiple_of(first, 128), 512)
        weights = r["buf_qkv"][:, :, :, :, :, cols].reshape(1024, 512)
        r["d_x"][...] += mm_nt(d_flat, weights)
        grad = mm_tn(r["x_in_in"][...], d_flat).astype(bf16)
        r["buf_qkv"][:, :, :, :, :, cols] = grad.reshape(2, 4, 2, 4, 16, 512)

    def head_tile(j, rows_ref, flat_ref, first, gain, dg_ref):
        cols = pl.ds(pl.multiple_of(j * 512, 128), 512)
        grads_in = rows_ref[:, :, cols].reshape(256, 512).astype(f32)
        flat = flat_ref[:, cols]
        done = []
        for h in range(4):
            e = grads_in[:, h * 128 : (h + 1) * 128]
            v = flat[:, h * 128 : (h + 1) * 128]
            e = e * cos[...] - pltpu.roll(e, 64, 1) * sin[...]
            scale = inv_rms(v)
            weighed = gain * e
            d = scale * weighed - v * (scale * scale * scale) * jnp.mean(v * weighed, axis=-1, keepdims=True)
            dg_ref[...] += jnp.sum(e * v * scale, axis=0, keepdims=True)
            done.append(d.astype(bf16))
        project_back(jnp.concatenate(done, axis=-1), first + j * 512)

    def query_tile(j, carry):
        head_tile(j, r["dq_rows"], r["q_flat_in"], 0, gains["query"], r["dg_query"])
        return carry

    def key_tile(j, carry):
        head_tile(j, r["dk_rows"], r["k_flat_in"], 2048, gains["key"], r["dg_key"])
        return carry

    def value_tile(j, carry):
        cols = pl.ds(pl.multiple_of(j * 512, 128), 512)
        project_back(r["dv_rows"][:, :, cols].reshape(256, 512), 3072 + j * 512)
        return carry

    def swap_cores(half):
        reduce.send(
            0, 36 + 6 * half,
            r["buf_qkv"].at[:, :, 1 - place.core, :, :, pl.ds(half * 2048, 2048)],
            reduce.total(0).at[half],
            place.to_core,
        )

    def queries():
        lax.fori_loop(0, 4, query_tile, 0)
        swap_cores(0)

    def keys_values():
        lax.fori_loop(0, 2, key_tile, 0)
        lax.fori_loop(0, 2, value_tile, 0)
        swap_cores(1)

    def join_cores():
        for half in range(2):
            reduce.take(0, 36 + 6 * half, reduce.total(0).at[half])
            accumulate(
                reduce.total(0).at[half],
                r["buf_qkv"].at[:, :, place.core, :, :, pl.ds(half * 2048, 2048)],
            )

    give = pltpu.make_async_copy(r["d_x"], r["d_input"], r["in_sem"].at[15])

    def input_grad():
        x, d_x = r["hidden_in"][...].reshape(256, 1024).astype(f32), r["d_x"][...]
        scale = inv_rms(x)
        weighed = gains["attn"] * d_x
        d_norm = scale * weighed - x * (scale * scale * scale) * jnp.mean(x * weighed, axis=-1, keepdims=True)
        dg_attn = jnp.sum(d_x * x * scale, axis=0, keepdims=True)
        r["d_x"][...] = r["d_residual_in"][...] + d_norm
        give.start()
        lines = [dg_attn[:, at * 128 : (at + 1) * 128] for at in range(8)]
        lines += [r["dg_query"][...], r["dg_key"][...]]
        lines += [r["dg_ffn_in"][:, at * 128 : (at + 1) * 128] for at in range(8)]
        lines += [jnp.zeros((6, 128), f32)]
        little.put(0, jnp.concatenate(lines, axis=0))

    def small(step):
        if step < 4:
            little.put(step + 1, little.sum(step))
        else:
            r["gains_sum"][...] = little.sum(4)

    for step in BACKWARD_ORDER:
        if step[0] == "attention":
            attention(step[1])
        elif step[0] == "rows":
            rows()
        elif step[0] == "queries":
            queries()
        elif step[0] == "keys_values":
            keys_values()
        elif step[0] == "join_cores":
            join_cores()
        elif step[0] == "input_grad":
            input_grad()
        elif step[0] == "small":
            small(step[1])
        else:
            stages(step)
    reduce.finish()
    swap.finish()
    give.wait()
    for g in range(4):
        pltpu.make_async_copy(reduce.result(g), outs[g], r["out_sem"].at[g]).wait()


def backward(inputs):
    def shape(*dims, dtype=bf16):
        return jax.ShapeDtypeStruct(dims, dtype)

    outs = [shape(256, 1024, dtype=f32), shape(24, 128, dtype=f32)] + [
        shape(2, 4, rows // 4, cols // 2) for rows, cols in zip(SHARD_ROWS, COLUMNS)
    ]
    vmem = pl.BlockSpec(memory_space=pltpu.VMEM)
    hbm = pl.BlockSpec(memory_space=pl.ANY)
    buffers = [
        pltpu.VMEM(dims, dtype)
        for dims, dtype in (
            ((2, 4, 2, 4, 16, 4096), bf16),
            ((2, 1024, 256), bf16),
            ((2, 1024, 128), bf16),
            ((2, 1024, 128), bf16),
            ((2, 1024, 256), bf16),
            ((2, 1024, 256), bf16),
            ((2, 1024, 128), bf16),
            ((2, 1024, 128), bf16),
            ((1024, 128), f32),
            ((1024, 128), f32),
            ((2, 128, 2048), bf16),
            ((2, 128, 1024), bf16),
            ((2, 128, 1024), bf16),
            ((256, 2048), f32),
            ((256, 1024), f32),
            ((256, 1024), bf16),
            ((2, 128, 1024), bf16),
            ((256, 1024), f32),
            ((256, 128), f32),
            ((256, 128), f32),
            ((2, 4, 2, 16, 128), bf16),
            ((1, 1024), f32),
            ((256, 1024), f32),
            ((1, 128), f32),
            ((1, 128), f32),
            ((5, 4, 24, 128), f32),
        )
    ]
    dma = pltpu.SemaphoreType.DMA
    sems = [
        dma((4, 44)),
        dma((4, 44)),
        dma((4,)),
        dma((5, 3)),
        dma((5, 3)),
        dma((4,)),
        dma((8, 7)),
        dma((8, 7)),
        dma((16,)),
    ]
    results = pl.pallas_call(
        functools.partial(backward_kernel),
        out_shape=outs,
        in_specs=[hbm] * len(BACKWARD_IN),
        out_specs=[hbm, vmem] + [hbm] * 4,
        scratch_shapes=reduce_scratch() + buffers + sems,
        compiler_params=pltpu.CompilerParams(
            collective_id=2, has_side_effects=True, vmem_limit_bytes=63 * 1024 * 1024
        ),
        name="backward",
    )(*[inputs[name] for name in BACKWARD_IN])
    return dict(zip(BACKWARD_OUT, results))


def finish_kernel(*refs):
    gq, gk, gv, go, gg, gu, gd, d_attn, d_query, d_key, d_ffn = refs[5:16]
    qkv, output, gate_up, down, gains, sem = refs[16:]
    copies = [pltpu.make_async_copy(refs[at], refs[16 + at], sem.at[at]) for at in range(5)]
    for copy in copies:
        copy.start()
    for copy in copies:
        copy.wait()
    gq[...] = qkv[0].astype(f32)
    gk[...] = qkv[1, :, :1024].astype(f32)
    gv[...] = qkv[1, :, 1024:].astype(f32)
    for half in range(2):
        cols = slice(half * 512, (half + 1) * 512)
        go[:, cols] = output[half].astype(f32)
        gd[:, cols] = down[half].astype(f32)
    gg[...] = gate_up[0].astype(f32)
    gu[...] = gate_up[1].astype(f32)
    dp = lax.axis_index("dp")
    row, lane = dp // 2, dp % 2 * 64
    for ref, at in ((d_attn, row), (d_ffn, 10 + row)):
        ref[...] = pltpu.roll(gains[pl.ds(at, 1), :], lane, 1)[:, :64]
    for ref, at in ((d_query, 8), (d_key, 9)):
        ref[...] = pltpu.roll(gains[at : at + 1, :], (128 - dp * 8) % 128, 1)[:, :8]


def finish(sums, gains):
    def shape(*dims):
        return jax.ShapeDtypeStruct(dims, f32)

    outs = [
        shape(64, 2048),
        shape(64, 1024),
        shape(64, 1024),
        shape(128, 1024),
        shape(64, 3072),
        shape(64, 3072),
        shape(192, 1024),
        shape(1, 64),
        shape(1, 8),
        shape(1, 8),
        shape(1, 64),
    ]
    vmem = pl.BlockSpec(memory_space=pltpu.VMEM)
    sums = [part.reshape(2, rows, cols // 2) for part, rows, cols in zip(sums, SHARD_ROWS, COLUMNS)]
    return pl.pallas_call(
        functools.partial(finish_kernel),
        out_shape=outs,
        in_specs=[pl.BlockSpec(memory_space=pl.ANY)] * 5,
        out_specs=[vmem] * 11,
        scratch_shapes=[pltpu.VMEM(part.shape, part.dtype) for part in (*sums, gains)]
        + [pltpu.SemaphoreType.DMA((5,))],
        compiler_params=pltpu.CompilerParams(vmem_limit_bytes=60 * 1024 * 1024),
        name="finish",
    )(*sums, gains)


def rotary_tables(positions):
    frequency = jnp.exp(jnp.arange(64, dtype=f32) * (-2.0 * math.log(rope_base) / 128))
    angles = positions.astype(f32)[:, None] * frequency[None, :]
    cos_half, sin_half = jnp.cos(angles), jnp.sin(angles)
    return (
        jnp.concatenate([cos_half, cos_half], axis=-1),
        jnp.concatenate([-sin_half, sin_half], axis=-1),
    )


def per_device(
    hidden_in,
    out_cotangent,
    slot_lengths,
    position_ids,
    attn_gain,
    w_query,
    key_weight,
    value_weight,
    query_gain,
    key_gain,
    w_output,
    ffn_gain,
    w_gate,
    w_up,
    w_down,
):
    dp = lax.axis_index("dp")
    lane = jnp.arange(128, dtype=jnp.int32)[None, :]
    wide = jnp.stack([attn_gain, ffn_gain])
    wide = jnp.where(lane // 64 == dp % 2, jnp.concatenate([wide, wide], axis=1), 0)
    narrow = jnp.where(lane // 8 == dp, jnp.tile(jnp.stack([query_gain, key_gain]), (1, 16)), 0)
    tile = jnp.concatenate([wide[:1], narrow, wide[1:], jnp.zeros((12, 128), bf16)], axis=0)
    valid = jnp.broadcast_to((slot_lengths - lax.axis_index("seq") * 128).astype(f32)[:, None, None], (2, 8, 128))
    cos, sin = rotary_tables(position_ids.reshape(256))
    shards = (w_query, key_weight, value_weight, w_output, w_gate, w_up, w_down)
    done = forward(shards, tile, hidden_in, out_cotangent, cos, sin, valid)
    done.update(hidden=hidden_in, cos=cos, sin=sin)
    for name, rows, cols in (("total_output", 32, 512), ("total_gate_up", 16, 3072), ("total_down", 48, 512)):
        done[name] = done[name].reshape(2, 2, 4, 4, rows, cols)
    done["weights_qkv"] = done["weights_qkv"].reshape(2, 4, 2, 4, 16, 4096)
    last = backward(done)
    sums = [last[name] for name in ("sum_qkv", "sum_output", "sum_gate_up", "sum_down")]
    d_input = last["d_input"].reshape(2, 128, 1024)
    gq, gk, gv, go, gg, gu, gd, *gains = finish(sums, last["gains_sum"])
    dg_attn, dg_query, dg_key, dg_ffn = [gain.reshape(-1) for gain in gains]
    return (done["out"], d_input, dg_attn, gq, gk, gv, dg_query, dg_key, go, dg_ffn, gg, gu, gd)


def solution(mesh):
    slots, rows, vector, matrix = P("dp", "seq", None), P("dp", "seq"), P("dp"), P("dp", None)
    in_specs = (
        slots,
        slots,
        vector,
        rows,
        vector,
        matrix,
        matrix,
        matrix,
        vector,
        vector,
        matrix,
        vector,
        matrix,
        matrix,
        matrix,
    )
    out_specs = (
        slots,
        slots,
        vector,
        matrix,
        matrix,
        matrix,
        vector,
        vector,
        matrix,
        vector,
        matrix,
        matrix,
        matrix,
    )
    return jax.shard_map(
        per_device, mesh=mesh, in_specs=in_specs, out_specs=out_specs, check_vma=False
    )
```

```python
import functools
import math

import jax
import jax.numpy as jnp
from jax import lax
from jax.experimental import pallas as pl
from jax.experimental.pallas import tpu as pltpu
from jax.sharding import PartitionSpec as P

epsilon = 1e-06
rope_base = 1000000.0
bf16 = jnp.bfloat16
f32 = jnp.float32


MESH = pl.DeviceIdType.MESH
SHARD_ROWS = (64, 128, 64, 192)
COLUMNS = (4096, 1024, 6144, 1024)
THIRDS = ((640, 640, 768), (256, 128, 128), (1024, 1024, 1024), (128, 256, 128))


GATHER_ROWS = (64, 64, 128, 64, 64, 192)
GATHER_COLUMNS = (2048, 2048, 1024, 3072, 3072, 1024)
GATHER_FIRST = (0, 2048, 0, 0, 0, 0)
SHARED = (640, 640, 384, 1024, 1024, 384)
SHARES = (
    (256, 256, 128),
    (128, 256, 256),
    (128, 128, 128),
    (384, 256, 384),
    (256, 384, 384),
    (128, 128, 128),
)


class Place:
    def __init__(self):
        dp, seq = lax.axis_index("dp"), lax.axis_index("seq")
        x, y_lo = seq // 2, seq % 2
        y_hi, z, core = dp // 8, (dp // 2) % 4, dp % 2
        self.dp, self.seq, self.x, self.y_lo = dp, seq, x, y_lo
        self.y_hi, self.z, self.core = y_hi, z, core
        self.z_up, self.z_down, self.z_far = (z + 1) % 4, (z + 3) % 4, (z + 2) % 4
        self.color = (x + y_lo + y_hi) % 2
        self.to_z_up = (y_hi * 8 + self.z_up * 2 + core, seq)
        self.to_z_down = (y_hi * 8 + self.z_down * 2 + core, seq)
        self.to_x_up = (dp, ((x + 1) % 4) * 2 + y_lo)
        self.to_x_down = (dp, ((x + 3) % 4) * 2 + y_lo)
        self.to_pair = (dp, x * 2 + 1 - y_lo)
        self.to_cross = ((1 - y_hi) * 8 + z * 2 + core, x * 2 + 1 - y_lo)
        self.to_core = (y_hi * 8 + z * 2 + 1 - core, seq)

    def torus(self):
        return (
            self.to_z_up,
            self.to_z_down,
            self.to_x_up,
            self.to_x_down,
            self.to_pair,
            self.to_cross,
            self.to_core,
        )


def greet(peers):
    barrier = pltpu.get_barrier_semaphore()
    for peer in peers:
        pl.semaphore_signal(barrier, inc=1, device_id=peer, device_id_type=MESH)
    pl.semaphore_wait(barrier, len(peers))


GATHER_KINDS = (
    "own_up",
    "own_down",
    "on_up",
    "on_down",
    "cross_own",
    "cross_up",
    "cross_down",
    "cross_far",
    "other_up",
    "other_down",
    "other_on_up",
    "other_on_down",
) + tuple(f"share_{n}_{s}" for n in range(3) for s in ("up", "down", "far", "other"))
GATHER_KINDS += tuple(f"core_{s}" for s in ("own", "up", "down", "far", "other"))
KIND_AT = {kind: at for at, kind in enumerate(GATHER_KINDS)}
KINDS = len(GATHER_KINDS)


class Gather:
    def __init__(self, place, buffers, send_sem, recv_sem):
        self.place, self.buffers, self.send_sem, self.recv_sem = place, buffers, send_sem, recv_sem
        self.sent = []

    def region(self, g, kind, receiving):
        p = self.place
        rows, cols = GATHER_ROWS[g], GATHER_COLUMNS[g]
        shared = SHARED[g]
        here, there = p.y_hi, 1 - p.y_hi
        whole, top, low = pl.ds(0, rows), pl.ds(0, rows // 2), pl.ds(rows // 2, rows // 2)
        low_first = pl.ds(rows // 2, rows // 4)
        low_last = pl.ds(rows // 2 + rows // 4, rows // 4)
        color = p.color
        if kind.startswith("share") and receiving:
            color = 1 - color
        begin = GATHER_FIRST[g]
        mine = pl.ds(pl.multiple_of(begin + color * shared, 128), cols - shared)
        below, above = p.z_down, p.z_up
        z, far = p.z, p.z_far
        buf = self.buffers[g]

        def at(y, zz, r, c):
            return buf.at[y, zz, p.core, r, c]

        def at_core(y, zz, core):
            return buf.at[y, zz, core, :, pl.ds(begin, cols)]

        if kind == "own_up":
            return at(here, below if receiving else z, whole, mine), p.to_z_up
        if kind == "own_down":
            return at(here, above if receiving else z, whole, mine), p.to_z_down
        if kind == "on_up":
            return at(here, far if receiving else below, top, mine), p.to_z_up
        if kind == "on_down":
            return at(here, far if receiving else above, low, mine), p.to_z_down
        if kind.startswith("cross"):
            y = there if receiving else here
            which = kind[6:]
            if which == "own":
                return at(y, z, whole, mine), p.to_cross
            return at(y, {"up": above, "down": below, "far": far}[which], top, mine), p.to_cross
        if kind == "other_up":
            return at(there, below if receiving else z, low, mine), p.to_z_up
        if kind == "other_down":
            return at(there, above if receiving else z, low, mine), p.to_z_down
        if kind == "other_on_up":
            return at(there, far if receiving else below, low_first, mine), p.to_z_up
        if kind == "other_on_down":
            return at(there, far if receiving else above, low_last, mine), p.to_z_down
        if kind.startswith("share"):
            _, n, which = kind.split("_")
            n = int(n)
            start = begin + color * (cols - shared) + sum(SHARES[g][:n])
            part = pl.ds(pl.multiple_of(start, 128), SHARES[g][n])
            to = (p.to_x_up, p.to_x_down, p.to_pair)[n]
            if which == "other":
                return buf.at[there, :, p.core, :, part], to
            return at(here, {"up": above, "down": below, "far": far}[which], whole, part), to
        which = kind[5:]
        core = 1 - p.core if receiving else p.core
        if which == "other":
            return buf.at[there, :, core, :, pl.ds(begin, cols)], p.to_core
        return at_core(here, {"own": z, "up": above, "down": below, "far": far}[which], core), p.to_core

    def copy(self, g, kind, receiving=False):
        region, to = self.region(g, kind, receiving)
        at = KIND_AT[kind]
        return pltpu.make_async_remote_copy(
            src_ref=region,
            dst_ref=region,
            send_sem=self.send_sem.at[g, at],
            recv_sem=self.recv_sem.at[g, at],
            device_id=to,
            device_id_type=MESH,
        )

    def send(self, g, *kinds):
        for kind in kinds:
            self.copy(g, kind).start()
            self.sent.append((g, kind))

    def take(self, g, *kinds):
        for kind in kinds:
            self.copy(g, kind, True).wait_recv()

    def share(self, g, which):
        self.send(g, *(f"share_{n}_{which}" for n in range(3)))

    def taken(self, g, which):
        self.take(g, *(f"share_{n}_{which}" for n in range(3)))

    def phase(self, number, g):
        if number == 0:
            self.send(g, "own_up", "own_down", "cross_own", "core_own")
        elif number == 1:
            self.take(g, "own_up", "own_down")
            self.send(g, "on_up", "on_down", "cross_up", "cross_down")
            self.share(g, "up")
            self.share(g, "down")
        elif number == 2:
            self.take(g, "cross_own")
            self.send(g, "other_up", "other_down")
        elif number == 8:
            self.take(g, "on_up", "on_down")
            self.send(g, "cross_far")
            self.share(g, "far")
        elif number == 3:
            self.take(g, "other_up", "other_down")
            self.send(g, "other_on_up", "other_on_down")
        elif number == 4:
            self.take(g, "cross_up", "cross_down", "cross_far", "other_on_up", "other_on_down")
            self.share(g, "other")
        elif number == 5:
            for which in ("up", "down", "far"):
                self.taken(g, which)
                self.send(g, f"core_{which}")
        elif number == 6:
            self.taken(g, "other")
            self.send(g, "core_other")
        else:
            self.take(g, "core_own", "core_up", "core_down", "core_far", "core_other")

    def finish(self, *groups):
        for g, kind in self.sent:
            if g in groups:
                self.copy(g, kind).wait_send()
        self.sent = [one for one in self.sent if one[0] not in groups]


def own_copies(place, shards, buffers):
    mine = [buf.at[place.y_hi, place.z, place.core] for buf in buffers]
    query, key, value, output, gate, up, down = shards
    first, last = pl.ds(0, 1536), pl.ds(1536, 1536)
    return (
        (query, mine[0].at[:, pl.ds(0, 2048)]),
        (key, mine[0].at[:, pl.ds(2048, 1024)]),
        (value, mine[0].at[:, pl.ds(3072, 1024)]),
        (output, mine[1]),
        (gate.at[:, first], mine[2].at[:, first]),
        (up.at[:, first], mine[2].at[:, last]),
        (gate.at[:, last], mine[3].at[:, first]),
        (up.at[:, last], mine[3].at[:, last]),
        (down, mine[4]),
    )


class GatherSmall:
    def __init__(self, place, buffer, send_sem, recv_sem):
        self.place, self.buffer, self.send_sem, self.recv_sem = place, buffer, send_sem, recv_sem

    def copy(self, step, receiving=False):
        p, buf = self.place, self.buffer
        if step == 0:
            region, to = buf.at[p.y_hi, p.z, 1 - p.core if receiving else p.core], p.to_core
        elif step == 1:
            region, to = buf.at[1 - p.y_hi if receiving else p.y_hi, p.z], p.to_cross
        elif step == 2:
            region, to = buf.at[:, p.z_down if receiving else p.z], p.to_z_up
        elif step == 3:
            region, to = buf.at[:, p.z_up if receiving else p.z], p.to_z_down
        else:
            region, to = buf.at[:, p.z_far if receiving else p.z_down], p.to_z_up
        return pltpu.make_async_remote_copy(
            src_ref=region,
            dst_ref=region,
            send_sem=self.send_sem.at[step],
            recv_sem=self.recv_sem.at[step],
            device_id=to,
            device_id_type=MESH,
        )

    def start(self, step):
        self.copy(step).start()

    def take(self, step):
        self.copy(step, True).wait_recv()

    def finish(self):
        for step in range(5):
            self.copy(step).wait_send()


PART_ORDER = ("xyz", "yzx", "zxy")
FREE = ((("yl", "yh", "z"), ("z",), ()), (("z", "x"), ("x",), ()), (("yl", "yh", "x"), ("yl", "yh"), ()))
EXTENT = {"yl": 2, "yh": 2, "z": 4, "x": 4}


def half_shape(part, step):
    free = FREE[part][step]
    first = EXTENT[free[0]] // 2
    return ((first,) if first > 1 else ()) + tuple(EXTENT[d] for d in free[1:])


def near_shape(part, step):
    return tuple(EXTENT[d] for d in FREE[part][step])


def reduce_scratch():
    shapes = []
    for g in range(4):
        rows, half = SHARD_ROWS[g] // 4, COLUMNS[g] // 2
        shapes.append(pltpu.VMEM((2, 2, 4, 4, rows, half), bf16))
        shapes.append(pltpu.VMEM((2, 4, rows, half), bf16))
        for part in range(3):
            tail = (rows, THIRDS[g][part])
            for step in range(3):
                if step < 2:
                    shapes.append(pltpu.VMEM((2,) + half_shape(part, step) + tail, bf16))
                else:
                    shapes.append(pltpu.VMEM((1,) + tail, bf16))
                shapes.append(pltpu.VMEM((2,) + near_shape(part, step) + tail, bf16))
    return shapes


SCRATCH_PER_GROUP = 2 + 18


def accumulate(dst, src):
    lead = dst.shape[:-2]
    count = 1
    for n in lead:
        count *= n
    if not lead:
        dst[...] = dst[...] + src[...]
        return

    def body(i, carry):
        at, rest = [], i
        for n in reversed(lead):
            at.append(rest % n)
            rest = rest // n
        at = tuple(reversed(at))
        dst.at[at][...] = dst.at[at][...] + src.at[at][...]
        return carry

    lax.fori_loop(0, count, body, 0)


class Reduce:
    def __init__(self, place, grads, scratch, send_sem, recv_sem, load_sem):
        self.place, self.grads = place, grads
        self.send_sem, self.recv_sem, self.load_sem = send_sem, recv_sem, load_sem
        self.sent = []
        self.groups = [scratch[g * SCRATCH_PER_GROUP : (g + 1) * SCRATCH_PER_GROUP] for g in range(4)]

    def total(self, g):
        return self.groups[g][0]

    def result(self, g):
        return self.groups[g][1]

    def halves(self, g, part, step):
        return self.groups[g][2 + (part * 3 + step) * 2]

    def nears(self, g, part, step):
        return self.groups[g][3 + (part * 3 + step) * 2]

    def cols(self, g, part):
        return pl.ds(sum(THIRDS[g][:part]), THIRDS[g][part])

    def moved(self, dim, by):
        p = self.place
        if dim == "x":
            x = (p.x + by) % 4
            return {"x": x}, (p.dp, x * 2 + p.y_lo)
        if dim == "z":
            z = (p.z + by) % 4
            return {"z": z}, (p.y_hi * 8 + z * 2 + p.core, p.seq)
        y = (p.y_hi * 2 + p.y_lo + by) % 4
        return {"yl": y % 2, "yh": y // 2}, ((y // 2) * 8 + p.z * 2 + p.core, p.x * 2 + y % 2)

    def chunk(self, g, part, step, by, half=None):
        at = {}
        for earlier in range(step):
            at.update(self.moved(PART_ORDER[part][earlier], 0)[0])
        at.update(self.moved(PART_ORDER[part][step], by)[0])
        if half is not None:
            cut = FREE[part][step][0]
            size = EXTENT[cut] // 2
            at[cut] = half if size == 1 else pl.ds(half * size, size)
        index = tuple(at.get(name, slice(None)) for name in ("yl", "yh", "z", "x"))
        return self.total(g).at[index + (slice(None), self.cols(g, part))]

    def remote(self, g, sem, src, dst, to):
        return pltpu.make_async_remote_copy(
            src_ref=src,
            dst_ref=dst,
            send_sem=self.send_sem.at[g, sem],
            recv_sem=self.recv_sem.at[g, sem],
            device_id=to,
            device_id_type=MESH,
        )

    def send(self, g, sem, src, dst, to):
        copy = self.remote(g, sem, src, dst, to)
        copy.start()
        self.sent.append(copy)

    def take(self, g, sem, dst):
        self.remote(g, sem, dst, dst, self.place.to_core).wait_recv()

    def load(self, g):
        return pltpu.make_async_copy(self.grads[g], self.total(g), self.load_sem.at[g])

    def send_far(self, g, step):
        for part in range(3):
            sem, dim = part * 12 + step * 4, PART_ORDER[part][step]
            buf = self.halves(g, part, step)
            up, down = self.moved(dim, 1)[1], self.moved(dim, 3)[1]
            if step < 2:
                self.send(g, sem, self.chunk(g, part, step, 2, 0), buf.at[0], up)
                self.send(g, sem + 1, self.chunk(g, part, step, 2, 1), buf.at[1], down)
            else:
                self.send(g, sem, self.chunk(g, part, step, 2), buf.at[0], up)

    def send_near(self, g, step):
        for part in range(3):
            sem, dim = part * 12 + step * 4, PART_ORDER[part][step]
            buf, near = self.halves(g, part, step), self.nears(g, part, step)
            up, down = self.moved(dim, 1)[1], self.moved(dim, 3)[1]
            self.take(g, sem, buf.at[0])
            accumulate(self.chunk(g, part, step, 1, 0 if step < 2 else None), buf.at[0])
            self.send(g, sem + 2, self.chunk(g, part, step, 1), near.at[0], up)
            if step < 2:
                self.take(g, sem + 1, buf.at[1])
                accumulate(self.chunk(g, part, step, 3, 1), buf.at[1])
            self.send(g, sem + 3, self.chunk(g, part, step, 3), near.at[1], down)

    def join_near(self, g, step):
        for part in range(3):
            sem, near = part * 12 + step * 4, self.nears(g, part, step)
            for way in range(2):
                self.take(g, sem + 2 + way, near.at[way])
                accumulate(self.chunk(g, part, step, 0), near.at[way])

    def stage(self, number, g):
        p = self.place
        result = self.result(g)
        if number == 0:
            if self.grads[g] is not None:
                self.load(g).wait()
            self.send_far(g, 0)
        elif number in (1, 3, 5):
            self.send_near(g, number // 2)
        elif number in (2, 4):
            self.join_near(g, number // 2 - 1)
            self.send_far(g, number // 2)
        elif number == 6:
            self.join_near(g, 2)
            result.at[p.y_lo, p.x][...] = self.total(g).at[p.y_lo, p.y_hi, p.z, p.x][...]
            mine = result.at[p.y_lo, p.x]
            self.send(g, 37, mine, mine, p.to_pair)
        elif number == 7:
            self.take(g, 37, result.at[1 - p.y_lo, p.x])
            mine = result.at[:, p.x]
            self.send(g, 38, mine, mine, p.to_x_up)
            self.send(g, 39, mine, mine, p.to_x_down)
        elif number == 8:
            below, above = (p.x + 3) % 4, (p.x + 1) % 4
            self.take(g, 38, result.at[:, below])
            self.send(g, 40, result.at[0, below], result.at[0, below], p.to_x_up)
            self.take(g, 39, result.at[:, above])
            self.send(g, 41, result.at[1, above], result.at[1, above], p.to_x_down)
        else:
            far = (p.x + 2) % 4
            self.take(g, 40, result.at[0, far])
            self.take(g, 41, result.at[1, far])

    def finish(self):
        for copy in self.sent:
            copy.wait_send()
        self.sent = []


class ReduceSmall:
    STEPS = (("core", 2), ("pair", 2), ("cross", 2), ("x", 4), ("z", 4))

    def __init__(self, place, slots, send_sem, recv_sem):
        self.place, self.slots, self.send_sem, self.recv_sem = place, slots, send_sem, recv_sem

    def peers(self, step):
        p = self.place
        name, count = self.STEPS[step]
        if count == 2:
            mine, to = {
                "core": (p.core, p.to_core),
                "pair": (p.y_lo, p.to_pair),
                "cross": (p.y_hi, p.to_cross),
            }[name]
            return mine, [(1 - mine, to)]
        if name == "x":
            return p.x, [((p.x + by) % 4, (p.dp, (p.x + by) % 4 * 2 + p.y_lo)) for by in (1, 2, 3)]
        return p.z, [
            ((p.z + by) % 4, (p.y_hi * 8 + (p.z + by) % 4 * 2 + p.core, p.seq)) for by in (1, 2, 3)
        ]

    def copies(self, step, receiving):
        mine, peers = self.peers(step)
        if receiving:
            peers = peers[::-1]
        for at, (place, to) in enumerate(peers):
            slot = self.slots.at[step, place if receiving else mine]
            yield pltpu.make_async_remote_copy(
                src_ref=slot,
                dst_ref=slot,
                send_sem=self.send_sem.at[step, at],
                recv_sem=self.recv_sem.at[step, at],
                device_id=to,
                device_id_type=MESH,
            )

    def put(self, step, values):
        mine, _ = self.peers(step)
        self.slots.at[step, mine][...] = values
        for copy in self.copies(step, False):
            copy.start()

    def sum(self, step):
        for copy in self.copies(step, True):
            copy.wait_recv()
        for copy in self.copies(step, False):
            copy.wait_send()
        total = self.slots[step, 0]
        for at in range(1, self.STEPS[step][1]):
            total = total + self.slots[step, at]
        return total


SCALE = 128 ** (-0.5)
OFFSETS = tuple((dx, dy) for dx in range(4) for dy in range(2) if (dx, dy) != (0, 0))


def mm(left, right):
    return jnp.dot(left, right, preferred_element_type=f32)


def mm_nt(left, right):
    return lax.dot_general(left, right, (((1,), (1,)), ((), ())), preferred_element_type=f32)


def mm_tn(left, right):
    return lax.dot_general(left, right, (((0,), (0,)), ((), ())), preferred_element_type=f32)


def inv_rms(v):
    return lax.rsqrt(jnp.mean(v * v, axis=-1, keepdims=True) + epsilon)


class Exchange:
    def __init__(self, place, send_sem, recv_sem):
        self.place, self.send_sem, self.recv_sem, self.sent = place, send_sem, recv_sem, []

    def partner(self, at, back=False):
        dx, dy = OFFSETS[at]
        x = (self.place.x + (4 - dx if back else dx)) % 4
        return x * 2 + (self.place.y_lo + dy) % 2

    def send(self, kind, src, dst):
        for at in range(7):
            partner = self.partner(at)
            copy = pltpu.make_async_remote_copy(
                src_ref=src(partner),
                dst_ref=dst(self.place.seq),
                send_sem=self.send_sem.at[kind, at],
                recv_sem=self.recv_sem.at[kind, at],
                device_id=(self.place.dp, partner),
                device_id_type=MESH,
            )
            copy.start()
            self.sent.append(copy)

    def take(self, kind, dst):
        for at in range(7):
            partner = self.partner(at, back=True)
            pltpu.make_async_remote_copy(
                src_ref=dst(partner),
                dst_ref=dst(partner),
                send_sem=self.send_sem.at[kind, at],
                recv_sem=self.recv_sem.at[kind, at],
                device_id=(self.place.dp, partner),
                device_id_type=MESH,
            ).wait_recv()

    def finish(self):
        for copy in self.sent:
            copy.wait_send()
        self.sent = []


def token_rows(seq):
    return pl.ds(pl.multiple_of(seq * 128, 128), 128)


def head_cols(seq, width):
    return pl.ds(pl.multiple_of(seq * width, 128), width)


def gain_rows(tile_ref):
    tiles = tile_ref[...].astype(f32).reshape(8, 2, 16, 128)
    pairs = tiles[:, 0] + tiles[:, 1]
    total = pairs[0]
    for at in range(1, 8):
        total = total + pairs[at]

    def wide(row):
        return jnp.concatenate([pairs[at, row : row + 1, :] for at in range(8)], axis=-1)

    return wide(0), total[1:2, :], total[2:3, :], wide(3)


def causal_scores(q, k, first):
    scores = mm_nt(q, k) * SCALE
    row = first + lax.broadcasted_iota(jnp.int32, scores.shape, 0)
    col = lax.broadcasted_iota(jnp.int32, scores.shape, 1)
    return jnp.where(col <= row, scores, -1e30)


FORWARD_IN = (
    "w_query", "w_key", "w_value", "w_output", "w_gate", "w_up", "w_down", "gains",
    "hidden", "cot", "cos", "sin", "valid",
)
FORWARD_OUT = (
    "out", "d_residual", "d_attended", "dg_ffn", "x_in", "q_flat", "k_flat",
    "total_output", "total_gate_up", "total_down", "weights_qkv", "q_heads", "k_heads", "v_heads", "gain_tiles",
)
FORWARD_SCRATCH = (
    "buf_qkv", "buf_output", "buf_gate_up_0", "buf_gate_up_1", "buf_down", "tiles", "rows", "core_down",
    "q_in", "k_in", "v_in", "att", "context", "residual", "mid_in", "mid_turned", "result", "d_mid", "d_branch",
    "gather_send", "gather_recv", "small_send", "small_recv", "local_sem", "swap_send", "swap_recv", "out_sem",
    "core_free", "core_send", "core_recv",
    "out_out", "d_residual_out", "d_attended_out", "x_in_out", "q_flat_out", "k_flat_out",
)
FF_TILE = 768


def forward_kernel(*refs):
    r = dict(zip(FORWARD_IN + FORWARD_OUT + FORWARD_SCRATCH, refs))
    place = Place()
    me = place.seq
    buffers = [r["buf_qkv"], r["buf_output"], r["buf_gate_up_0"], r["buf_gate_up_1"], r["buf_down"]]
    tiles = r["tiles"]
    pairs = own_copies(place, [r[name] for name in FORWARD_IN[:7]], buffers)
    pairs += ((r["gains"], tiles.at[place.y_hi, place.z, place.core]),)
    copies = [
        pltpu.make_async_copy(shard, there, r["local_sem"].at[at]) for at, (shard, there) in enumerate(pairs)
    ]
    for copy in copies:
        copy.start()
    greet(
        place.torus()
        + tuple(
            (place.dp, (place.x + dx) % 4 * 2 + (place.y_lo + dy) % 2)
            for dx, dy in OFFSETS
            if (dx, dy) not in ((1, 0), (3, 0), (0, 1))
        )
    )
    for copy in copies:
        copy.wait()
    gather = Gather(place, [buffers[0]] + buffers, r["gather_send"], r["gather_recv"])
    little = GatherSmall(place, tiles, r["small_send"], r["small_recv"])
    swap = Exchange(place, r["swap_send"], r["swap_recv"])
    saved = []

    def save(name, src, dst=None):
        at = len(saved)
        copy = pltpu.make_async_copy(src, r[name] if dst is None else dst, r["out_sem"].at[at])
        copy.start()
        saved.append(copy)

    def phases(*steps):
        for number, g in steps:
            gather.phase(number, g)

    little.start(0)
    phases((0, 0), (0, 1))
    little.take(0)
    little.start(1)
    phases((1, 0))
    little.take(1)
    little.start(2)
    little.start(3)
    phases((2, 0), (8, 0))
    little.take(2)
    little.take(3)
    little.start(4)
    phases((3, 0), (0, 3), (1, 1), (4, 0), (5, 0))
    little.take(4)
    g_attn, g_query, g_key, g_ffn = gain_rows(tiles)
    x = r["hidden"][...].reshape(256, 1024).astype(f32)
    r["x_in_out"][...] = (x * inv_rms(x) * g_attn).astype(bf16)
    phases((6, 0), (1, 3), (0, 2), (7, 0), (2, 3), (2, 1), (0, 5))
    save("gain_tiles", tiles)

    cos, sin = r["cos"], r["sin"]

    def qkv_weights(first):
        return buffers[0][:, :, :, :, pl.ds(pl.multiple_of(first, 128), 512)].reshape(1024, 512)

    def head_tile(j, flat_ref, rows_ref, first, gain):
        flat = mm(r["x_in_out"][...], qkv_weights(first + j * 512))
        cols = pl.ds(pl.multiple_of(j * 512, 128), 512)
        flat_ref[:, cols] = flat
        done = []
        for h in range(4):
            v = flat[:, h * 128 : (h + 1) * 128]
            v = v * inv_rms(v) * gain
            done.append((v * cos[...] + pltpu.roll(v, 64, 1) * sin[...]).astype(bf16))
        rows_ref[...] = jnp.concatenate(done, axis=-1).reshape(2, 128, 512)

    def query_tile(j, carry):
        head_tile(j, r["q_flat_out"], r["rows"].at[0, :, :, pl.ds(pl.multiple_of(j * 512, 128), 512)], 0, g_query)
        return carry

    def key_tile(j, carry):
        head_tile(j, r["k_flat_out"], r["rows"].at[1, :, :, pl.ds(pl.multiple_of(j * 512, 128), 512)], 2048, g_key)
        return carry

    def value_tile(j, carry):
        cols = pl.ds(pl.multiple_of(1024 + j * 512, 128), 512)
        r["rows"][1, :, :, cols] = mm(r["x_in_out"][...], qkv_weights(3072 + j * 512)).astype(bf16).reshape(2, 128, 512)
        return carry

    def to_heads(kind, at, first, heads, width):
        def cols(seq):
            return pl.ds(pl.multiple_of(first + seq * width, 128), width)

        swap.send(
            kind,
            lambda partner: r["rows"].at[at, :, :, cols(partner)],
            lambda sender: r[heads].at[:, token_rows(sender), :],
        )
        r[heads][:, token_rows(me), :] = r["rows"][at, :, :, cols(me)]

    lax.fori_loop(0, 4, query_tile, 0)
    to_heads(0, 0, 0, "q_in", 256)
    phases(
        (8, 1), (3, 1), (8, 3), (0, 4), (3, 3), (1, 5), (1, 2), (4, 1), (5, 1), (1, 4), (4, 3), (6, 1), (8, 5),
        (2, 4), (2, 2), (5, 3), (7, 1), (2, 5),
    )
    save("weights_qkv", buffers[0])
    lax.fori_loop(0, 2, key_tile, 0)
    to_heads(1, 1, 0, "k_in", 128)
    lax.fori_loop(0, 2, value_tile, 0)
    to_heads(2, 1, 1024, "v_in", 128)
    phases((3, 5), (6, 3), (8, 2), (4, 5), (3, 2), (4, 2))
    save("x_in", r["x_in_out"])
    save("q_flat", r["q_flat_out"])
    save("k_flat", r["k_flat_out"])
    swap.take(0, lambda sender: r["q_in"].at[:, token_rows(sender), :])
    swap.take(1, lambda sender: r["k_in"].at[:, token_rows(sender), :])
    swap.take(2, lambda sender: r["v_in"].at[:, token_rows(sender), :])
    save("q_heads", r["q_in"])
    save("k_heads", r["k_in"])
    save("v_heads", r["v_in"])

    def attend(slot, head):
        cols = slice(head * 128, (head + 1) * 128)
        for block in range(4):
            rows, upto = slice(block * 256, (block + 1) * 256), (block + 1) * 256
            q = r["q_in"][slot, rows, cols]
            scores = causal_scores(q, r["k_in"][slot, :upto, :], block * 256)
            top = jnp.max(scores, axis=-1, keepdims=True)
            shifted = jnp.exp(scores - top)
            total = jnp.sum(shifted, axis=-1, keepdims=True)
            prob = (shifted * (1.0 / total)).astype(bf16)
            r["att"][slot, rows, cols] = mm(prob, r["v_in"][slot, :upto, :]).astype(bf16)

    for slot in range(2):
        attend(slot, 0)
        attend(slot, 1)
        swap.send(
            3 + slot,
            lambda partner: r["att"].at[slot, token_rows(partner), :],
            lambda sender: r["context"].at[slot, :, head_cols(sender, 256)],
        )
        r["context"][slot, :, head_cols(me, 256)] = r["att"][slot, token_rows(me), :]
    phases((5, 2), (6, 2), (5, 5), (8, 4), (3, 4), (6, 5), (4, 4), (7, 2), (7, 5), (5, 4))
    for slot in range(2):
        swap.take(3 + slot, lambda sender: r["context"].at[slot, :, head_cols(sender, 256)])

    for half in range(2):
        cols = slice(half * 512, (half + 1) * 512)
        weights = buffers[1][:, :, :, :, cols].reshape(2048, 512)
        x = r["hidden"][:, :, cols].reshape(256, 512).astype(f32)
        r["residual"][:, cols] = x + mm(r["context"][...].reshape(256, 2048), weights)
    residual = r["residual"][...]
    mid_in = residual * inv_rms(residual) * g_ffn
    r["mid_in"][...] = mid_in.astype(bf16)
    r["mid_turned"][...] = mid_in.T.astype(bf16)


    def masked(values):
        order = lax.broadcasted_iota(jnp.int32, (128, 1024), 0).astype(f32)
        parts = [
            jnp.where(order < r["valid"][slot, :1, :1], values[slot * 128 : (slot + 1) * 128], 0.0)
            for slot in range(2)
        ]
        return jnp.concatenate(parts, axis=0)

    d_result = masked(r["cot"][...].reshape(256, 1024).astype(f32))
    r["d_branch"][...] = d_result.astype(bf16)
    phases((7, 3), (6, 4))
    gather.finish(0, 1, 3, 5)
    little.finish()
    swap.finish()
    for copy in saved:
        copy.wait()
    saved.clear()
    pl.semaphore_signal(r["core_free"], inc=1, device_id=place.to_core, device_id_type=MESH)
    pl.semaphore_wait(r["core_free"], 1)
    core, other = place.core, 1 - place.core

    def to_core(src, dst, *at):
        return pltpu.make_async_remote_copy(
            src_ref=src,
            dst_ref=dst,
            send_sem=r["core_send"].at[at],
            recv_sem=r["core_recv"].at[at],
            device_id=place.to_core,
            device_id_type=MESH,
        )

    def ffn_places(f):
        here = pl.ds(pl.multiple_of(f % 2 * FF_TILE, 128), FF_TILE)
        up = pl.ds(pl.multiple_of(1536 + f % 2 * FF_TILE, 128), FF_TILE)
        there = pl.ds(pl.multiple_of(f * FF_TILE, 128), FF_TILE)
        return here, up, there, pl.ds(f % 2 * 2, 2)

    def ffn_copies(b, f):
        here, up, there, z = ffn_places(f)
        weights = buffers[2 + b]
        return (
            to_core(weights.at[:, :, other, :, here], buffers[0].at[:, :, 0, :, there], f, 0),
            to_core(weights.at[:, :, other, :, up], buffers[0].at[:, :, 1, :, there], f, 1),
            to_core(buffers[4].at[b, z, other], r["core_down"].at[b, z], f, 2),
        )

    def ffn_join(b, f):
        here, up, there, z = ffn_places(f)
        weights = buffers[2 + b]
        for copy in ffn_copies(b, f):
            copy.wait_recv()
        weights[:, :, core, :, here] = weights[:, :, core, :, here] + buffers[0][:, :, 0, :, there]
        weights[:, :, core, :, up] = weights[:, :, core, :, up] + buffers[0][:, :, 1, :, there]
        buffers[4][b, z, core] = buffers[4][b, z, core] + r["core_down"][b, z]

    r["result"][...] = residual
    r["d_mid"][...] = jnp.zeros((256, 1024), f32)

    def ffn_tile(b, f):
        gate_cols, up_cols, _, z = ffn_places(f)
        w_gate = buffers[2 + b][:, :, :, :, gate_cols].reshape(1024, FF_TILE)
        w_up = buffers[2 + b][:, :, :, :, up_cols].reshape(1024, FF_TILE)
        w_down = buffers[4][b, z].reshape(FF_TILE, 1024)
        mid, d_branch = r["mid_in"][...], r["d_branch"][...]
        gate, up = mm(mid, w_gate), mm(mid, w_up)
        sig = 1.0 / (1.0 + jnp.exp(-gate))
        silu = gate * sig
        unit = (silu * up).astype(bf16)
        d_unit = mm_nt(d_branch, w_down)
        d_gate = (d_unit * up * (sig * (1.0 + gate * (1.0 - sig)))).astype(bf16)
        d_up = (d_unit * silu).astype(bf16)
        r["result"][...] += mm(unit, w_down)
        r["d_mid"][...] += mm_nt(d_gate, w_gate) + mm_nt(d_up, w_up)
        shape = (4, 2, 64, FF_TILE)
        for part in range(2):
            mid_part = r["mid_turned"][part * 512 : (part + 1) * 512, :]
            buffers[2 + b][part, :, :, :, gate_cols] = mm(mid_part, d_gate).astype(bf16).reshape(shape)
            buffers[2 + b][part, :, :, :, up_cols] = mm(mid_part, d_up).astype(bf16).reshape(shape)
        buffers[4][b, z] = mm_tn(unit, d_branch).astype(bf16).reshape(2, 2, 192, 1024)
        for copy in ffn_copies(b, f):
            copy.start()

    def first_half(f, carry):
        ffn_tile(0, f)

        @pl.when(f > 0)
        def _():
            ffn_join(0, f - 1)

        return carry

    def last_half(f, carry):
        ffn_tile(1, f)

        @pl.when(f > 2)
        def _():
            ffn_join(1, f - 1)

        return carry

    lax.fori_loop(0, 2, first_half, 0)
    phases((7, 4))
    gather.finish(2, 4)
    ffn_join(0, 1)
    lax.fori_loop(2, 4, last_half, 0)
    r["out_out"][...] = masked(r["result"][...]).astype(bf16).reshape(2, 128, 1024)
    save("out", r["out_out"])

    residual, d_mid = r["residual"][...], r["d_mid"][...]
    scale = inv_rms(residual)
    weighed = g_ffn * d_mid
    d_norm = scale * weighed - residual * (scale * scale * scale) * jnp.mean(
        residual * weighed, axis=-1, keepdims=True
    )
    r["dg_ffn"][...] = jnp.sum(d_mid * residual * scale, axis=0, keepdims=True)
    d_result = masked(r["cot"][...].reshape(256, 1024).astype(f32))
    r["d_residual_out"][...] = d_result + d_norm
    r["d_branch"][...] = r["d_residual_out"][...].astype(bf16)

    def output_tile(j, carry):
        y, z = j // 2, j % 2 * 2
        cols = pl.ds(pl.multiple_of(j * 512, 128), 512)
        d_attn = r["d_branch"][...]
        weights = buffers[1][y, pl.ds(z, 2)].reshape(512, 1024)
        r["d_attended_out"][:, :, cols] = mm_nt(d_attn, weights).astype(bf16).reshape(2, 128, 512)
        context = r["context"][:, :, cols].reshape(256, 512)
        buffers[1][y, pl.ds(z, 2)] = mm_tn(context, d_attn).astype(bf16).reshape(2, 2, 128, 1024)
        for copy in output_copies(j):
            copy.start()
        return carry

    def output_copies(j):
        y, z = j // 2, j % 2
        return tuple(
            to_core(
                buffers[1].at[y, z * 2 + k, other],
                r["rows"].at[y, z, :, pl.ds(k * 1024, 1024)],
                4 + j,
                k,
            )
            for k in range(2)
        )

    lax.fori_loop(0, 4, output_tile, 0)
    save("d_residual", r["d_residual_out"])
    save("d_attended", r["d_attended_out"])
    ffn_join(1, 3)
    for half in range(2):
        for b in range(2):
            save(
                "total_gate_up",
                buffers[2 + b].at[:, :, core, :, pl.ds(half * 1536, 1536)],
                r["total_gate_up"].at[half, :, :, :, pl.ds(b * 1536, 1536)],
            )
        save("total_down", buffers[4].at[:, :, core, :, pl.ds(half * 512, 512)], r["total_down"].at[half])

    def output_join(j, carry):
        y, z = j // 2, j % 2
        for k, copy in enumerate(output_copies(j)):
            copy.wait_recv()
            cols = slice(k * 1024, (k + 1) * 1024)
            buffers[1][y, z * 2 + k, core] = buffers[1][y, z * 2 + k, core] + r["rows"][y, z, :, cols]
        return carry

    lax.fori_loop(0, 4, output_join, 0)
    for half in range(2):
        save("total_output", buffers[1].at[:, :, core, :, pl.ds(half * 512, 512)], r["total_output"].at[half])
    for at in range(4):
        for copy in ffn_copies(at // 2, at) + output_copies(at):
            copy.wait_send()
    for copy in saved:
        copy.wait()


def forward(shards, gains, hidden, cot, cos, sin, valid):
    def shape(*dims, dtype=bf16):
        return jax.ShapeDtypeStruct(dims, dtype)

    outs = {
        "out": shape(2, 128, 1024),
        "d_residual": shape(256, 1024, dtype=f32),
        "d_attended": shape(2, 128, 2048),
        "dg_ffn": shape(1, 1024, dtype=f32),
        "x_in": shape(256, 1024),
        "q_flat": shape(256, 2048, dtype=f32),
        "k_flat": shape(256, 1024, dtype=f32),
        "total_output": shape(2, 2, 4, 128, 512),
        "total_gate_up": shape(2, 2, 4, 64, 3072),
        "total_down": shape(2, 2, 4, 192, 512),
        "weights_qkv": shape(2, 4, 2, 64, 4096),
        "q_heads": shape(2, 1024, 256),
        "k_heads": shape(2, 1024, 128),
        "v_heads": shape(2, 1024, 128),
        "gain_tiles": shape(2, 4, 2, 16, 128),
    }
    vmem = pl.BlockSpec(memory_space=pltpu.VMEM)
    hbm = pl.BlockSpec(memory_space=pl.ANY)
    scratch = {
        "buf_qkv": (2, 4, 2, 64, 4096),
        "buf_output": (2, 4, 2, 128, 1024),
        "buf_gate_up_0": (2, 4, 2, 64, 3072),
        "buf_gate_up_1": (2, 4, 2, 64, 3072),
        "buf_down": (2, 4, 2, 192, 1024),
        "tiles": (2, 4, 2, 16, 128),
        "rows": (2, 2, 128, 2048),
        "core_down": (2, 4, 192, 1024),
        "q_in": (2, 1024, 256),
        "k_in": (2, 1024, 128),
        "v_in": (2, 1024, 128),
        "att": (2, 1024, 256),
        "context": (2, 128, 2048),
        "residual": ((256, 1024), f32),
        "mid_in": (256, 1024),
        "mid_turned": (1024, 256),
        "result": ((256, 1024), f32),
        "d_mid": ((256, 1024), f32),
        "d_branch": (256, 1024),
    }
    dma = pltpu.SemaphoreType.DMA
    sems = [dma((6, KINDS)), dma((6, KINDS)), dma((5,)), dma((5,)), dma((10,)), dma((5, 7)), dma((5, 7)), dma((11,))]
    sems += [pltpu.SemaphoreType.REGULAR, dma((8, 3)), dma((8, 3))]
    buffers = [
        pltpu.VMEM(*(dims if isinstance(dims[0], tuple) else (dims, bf16))) for dims in scratch.values()
    ]
    results = pl.pallas_call(
        functools.partial(forward_kernel),
        out_shape=list(outs.values()),
        in_specs=[hbm] * 8 + [vmem] * 5,
        out_specs=[vmem if name == "dg_ffn" else hbm for name in outs],
        scratch_shapes=buffers
        + sems
        + [
            pltpu.VMEM(outs[name].shape, outs[name].dtype)
            for name in ("out", "d_residual", "d_attended", "x_in", "q_flat", "k_flat")
        ],
        compiler_params=pltpu.CompilerParams(
            collective_id=1, has_side_effects=True, vmem_limit_bytes=63 * 1024 * 1024
        ),
        name="forward",
    )(*shards, gains, hidden, cot, cos, sin, valid)
    return dict(zip(outs, results))


BACKWARD_IN = (
    "total_output", "total_gate_up", "total_down", "weights_qkv", "d_attended", "q_heads", "k_heads", "v_heads",
    "q_flat", "k_flat", "x_in", "hidden", "d_residual", "cos", "sin", "gain_tiles", "dg_ffn",
)
BACKWARD_OUT = ("d_input", "gains_sum", "sum_qkv", "sum_output", "sum_gate_up", "sum_down")
BACKWARD_SCRATCH = (
    "buf_qkv", "q_in", "k_in", "v_in", "grad_in", "dq", "dk", "dv", "dk_sum", "dv_sum", "dq_rows", "dk_rows", "dv_rows",
    "q_flat_in", "k_flat_in", "x_in_in", "hidden_in", "d_residual_in", "cos_in", "sin_in", "tiles_in", "dg_ffn_in", "x_in_turned", "d_x", "dg_query", "dg_key", "slots",
    "reduce_send", "reduce_recv", "load_sem", "small_send", "small_recv", "out_sem", "swap_send", "swap_recv", "in_sem",
)
BACKWARD_ORDER = (
    (0, 2),
    ("attention", 0),
    ("attention", 1),
    (0, 3),
    (1, 2),
    ("rows",),
    ("keys_values",),
    ("queries",),
    (0, 1),
    (1, 3),
    ("join_cores",),
    ("input_grad",),
    (0, 0),
    (2, 2),
    ("small", 0),
    (1, 1),
    (2, 3),
    ("small", 1),
    (1, 0),
    (2, 1),
    ("small", 2),
    (3, 3),
    (3, 2),
    ("small", 3),
    (3, 1),
    (2, 0),
    ("small", 4),
    (4, 3),
    (4, 2),
    (4, 1),
    (5, 3),
    (3, 0),
    (6, 3),
    (5, 1),
    (5, 2),
    (4, 0),
    (7, 3),
    (6, 1),
    (6, 2),
    (5, 0),
    (7, 1),
    (8, 3),
    (7, 2),
    (8, 1),
    (6, 0),
    (7, 0),
    (9, 1),
    (8, 2),
    (8, 0),
    (9, 3),
    (9, 0),
    (9, 2),
)
LATE_LOADS = (
    "q_flat", "k_flat", "x_in", "weights_qkv", "hidden", "d_residual", "cos", "sin", "gain_tiles", "dg_ffn",
)


def backward_kernel(*refs):
    names = BACKWARD_IN + BACKWARD_OUT
    count = 4 * SCRATCH_PER_GROUP
    r = dict(zip(names, refs))
    scratch = refs[len(names) : len(names) + count]
    r.update(zip(BACKWARD_SCRATCH, refs[len(names) + count :]))
    place = Place()
    me = place.seq
    loads = {
        name: pltpu.make_async_copy(r[name], r[there], r["in_sem"].at[at])
        for at, (name, there) in enumerate(
            (
                ("q_heads", "q_in"),
                ("k_heads", "k_in"),
                ("v_heads", "v_in"),
                ("q_flat", "q_flat_in"),
                ("k_flat", "k_flat_in"),
                ("x_in", "x_in_in"),
                ("weights_qkv", "buf_qkv"),
                ("hidden", "hidden_in"),
                ("d_residual", "d_residual_in"),
                ("cos", "cos_in"),
                ("sin", "sin_in"),
                ("gain_tiles", "tiles_in"),
                ("dg_ffn", "dg_ffn_in"),
            )
        )
    }
    grads = (None, r["total_output"], r["total_gate_up"], r["total_down"])
    outs = (r["sum_qkv"], r["sum_output"], r["sum_gate_up"], r["sum_down"])
    reduce = Reduce(place, grads, scratch, r["reduce_send"], r["reduce_recv"], r["load_sem"])
    little = ReduceSmall(place, r["slots"], r["small_send"], r["small_recv"])
    swap = Exchange(place, r["swap_send"], r["swap_recv"])
    for name in ("q_heads", "k_heads", "v_heads"):
        loads[name].start()
    reduce.load(3).start()
    greet(
        place.torus()
        + tuple(
            (place.dp, (place.x + dx) % 4 * 2 + (place.y_lo + dy) % 2)
            for dx, dy in OFFSETS
            if (dx, dy) not in ((1, 0), (3, 0), (0, 1))
        )
        + ((place.y_hi * 8 + place.z_far * 2 + place.core, place.seq),)
    )
    own = []
    for slot in range(2):
        swap.send(
            slot,
            lambda partner: r["d_attended"].at[slot, :, head_cols(partner, 256)],
            lambda sender: r["grad_in"].at[slot, token_rows(sender), :],
        )
        copy = pltpu.make_async_copy(
            r["d_attended"].at[slot, :, head_cols(me, 256)], r["grad_in"].at[slot, token_rows(me), :], r["in_sem"].at[13 + slot]
        )
        copy.start()
        own.append(copy)
    reduce.load(2).start()
    reduce.load(1).start()
    for name in LATE_LOADS:
        loads[name].start()

    def stages(*steps):
        for number, g in steps:
            reduce.stage(number, g)
            if number == 9:
                pltpu.make_async_copy(reduce.result(g), outs[g], r["out_sem"].at[g]).start()

    for name in ("q_heads", "k_heads", "v_heads"):
        loads[name].wait()

    def attend_back(slot, head):
        cols = slice(head * 128, (head + 1) * 128)
        if head == 0:
            r["dk_sum"][...] = jnp.zeros((1024, 128), f32)
            r["dv_sum"][...] = jnp.zeros((1024, 128), f32)
        for block in range(4):
            rows, upto = slice(block * 256, (block + 1) * 256), (block + 1) * 256
            q, grad = r["q_in"][slot, rows, cols], r["grad_in"][slot, rows, cols]
            k, v = r["k_in"][slot, :upto, :], r["v_in"][slot, :upto, :]
            scores = mm_nt(k, q) * SCALE
            key = lax.broadcasted_iota(jnp.int32, scores.shape, 0)
            query = block * 256 + lax.broadcasted_iota(jnp.int32, scores.shape, 1)
            scores = jnp.where(key <= query, scores, -1e30)
            shifted = jnp.exp(scores - jnp.max(scores, axis=0, keepdims=True))
            prob = shifted * (1.0 / jnp.sum(shifted, axis=0, keepdims=True))
            d_prob = mm_nt(v, grad)
            dot = jnp.sum(prob * d_prob, axis=0, keepdims=True)
            d_score = (prob * (d_prob - dot) * SCALE).astype(bf16)
            r["dk_sum"][:upto, :] += mm(d_score, q)
            r["dv_sum"][:upto, :] += mm(prob.astype(bf16), grad)
            r["dq"][slot, rows, cols] = mm_tn(d_score, k).astype(bf16)

    def to_rows(kind, slot, heads, rows, width):
        swap.send(
            kind,
            lambda partner: r[heads].at[slot, token_rows(partner), :],
            lambda sender: r[rows].at[slot, :, head_cols(sender, width)],
        )
        r[rows][slot, :, head_cols(me, width)] = r[heads][slot, token_rows(me), :]

    def attention(slot):
        own[slot].wait()
        swap.take(slot, lambda sender: r["grad_in"].at[slot, token_rows(sender), :])
        attend_back(slot, 0)
        attend_back(slot, 1)
        r["dk"][slot] = r["dk_sum"][...].astype(bf16)
        r["dv"][slot] = r["dv_sum"][...].astype(bf16)
        to_rows(2 + 3 * slot, slot, "dq", "dq_rows", 256)
        to_rows(3 + 3 * slot, slot, "dk", "dk_rows", 128)
        to_rows(4 + 3 * slot, slot, "dv", "dv_rows", 128)

    gains = {}

    def rows():
        for name in LATE_LOADS:
            loads[name].wait()
        gains["attn"], gains["query"], gains["key"], _ = gain_rows(r["tiles_in"])
        r["x_in_turned"][...] = r["x_in_in"][...].astype(f32).T.astype(bf16)
        for slot in range(2):
            swap.take(2 + 3 * slot, lambda sender: r["dq_rows"].at[slot, :, head_cols(sender, 256)])
            swap.take(3 + 3 * slot, lambda sender: r["dk_rows"].at[slot, :, head_cols(sender, 128)])
            swap.take(4 + 3 * slot, lambda sender: r["dv_rows"].at[slot, :, head_cols(sender, 128)])
        r["d_x"][...] = jnp.zeros((256, 1024), f32)
        r["dg_query"][...] = jnp.zeros((1, 128), f32)
        r["dg_key"][...] = jnp.zeros((1, 128), f32)

    cos, sin = r["cos_in"], r["sin_in"]

    def project_back(d_flat, first):
        cols = pl.ds(pl.multiple_of(first, 128), 512)
        weights = r["buf_qkv"][:, :, :, :, :, cols].reshape(1024, 512)
        r["d_x"][...] += mm_nt(d_flat, weights)
        grad = mm(r["x_in_turned"][...], d_flat).astype(bf16)
        r["buf_qkv"][:, :, :, :, :, cols] = grad.reshape(2, 4, 2, 4, 16, 512)

    def head_tile(j, rows_ref, flat_ref, first, gain, dg_ref):
        cols = pl.ds(pl.multiple_of(j * 512, 128), 512)
        grads_in = rows_ref[:, :, cols].reshape(256, 512).astype(f32)
        flat = flat_ref[:, cols]
        done = []
        for h in range(4):
            e = grads_in[:, h * 128 : (h + 1) * 128]
            v = flat[:, h * 128 : (h + 1) * 128]
            e = e * cos[...] - pltpu.roll(e, 64, 1) * sin[...]
            scale = inv_rms(v)
            weighed = gain * e
            d = scale * weighed - v * (scale * scale * scale) * jnp.mean(v * weighed, axis=-1, keepdims=True)
            dg_ref[...] += jnp.sum(e * v * scale, axis=0, keepdims=True)
            done.append(d.astype(bf16))
        project_back(jnp.concatenate(done, axis=-1), first + j * 512)

    def query_tile(j, carry):
        head_tile(j, r["dq_rows"], r["q_flat_in"], 0, gains["query"], r["dg_query"])
        return carry

    def key_tile(j, carry):
        head_tile(j, r["dk_rows"], r["k_flat_in"], 2048, gains["key"], r["dg_key"])
        return carry

    def value_tile(j, carry):
        cols = pl.ds(pl.multiple_of(j * 512, 128), 512)
        project_back(r["dv_rows"][:, :, cols].reshape(256, 512), 3072 + j * 512)
        return carry

    def swap_cores(half):
        reduce.send(
            0, 36 + 6 * half,
            r["buf_qkv"].at[:, :, 1 - place.core, :, :, pl.ds(half * 2048, 2048)],
            reduce.total(0).at[half],
            place.to_core,
        )

    def queries():
        lax.fori_loop(0, 4, query_tile, 0)
        swap_cores(0)

    def keys_values():
        lax.fori_loop(0, 2, key_tile, 0)
        lax.fori_loop(0, 2, value_tile, 0)
        swap_cores(1)

    def join_cores():
        for half in range(2):
            reduce.take(0, 36 + 6 * half, reduce.total(0).at[half])
            accumulate(
                reduce.total(0).at[half],
                r["buf_qkv"].at[:, :, place.core, :, :, pl.ds(half * 2048, 2048)],
            )

    give = pltpu.make_async_copy(r["d_x"], r["d_input"], r["in_sem"].at[15])

    def input_grad():
        x, d_x = r["hidden_in"][...].reshape(256, 1024).astype(f32), r["d_x"][...]
        scale = inv_rms(x)
        weighed = gains["attn"] * d_x
        d_norm = scale * weighed - x * (scale * scale * scale) * jnp.mean(x * weighed, axis=-1, keepdims=True)
        dg_attn = jnp.sum(d_x * x * scale, axis=0, keepdims=True)
        r["d_x"][...] = r["d_residual_in"][...] + d_norm
        give.start()
        lines = [dg_attn[:, at * 128 : (at + 1) * 128] for at in range(8)]
        lines += [r["dg_query"][...], r["dg_key"][...]]
        lines += [r["dg_ffn_in"][:, at * 128 : (at + 1) * 128] for at in range(8)]
        lines += [jnp.zeros((6, 128), f32)]
        little.put(0, jnp.concatenate(lines, axis=0))

    def small(step):
        if step < 4:
            little.put(step + 1, little.sum(step))
        else:
            r["gains_sum"][...] = little.sum(4)

    for step in BACKWARD_ORDER:
        if step[0] == "attention":
            attention(step[1])
        elif step[0] == "rows":
            rows()
        elif step[0] == "queries":
            queries()
        elif step[0] == "keys_values":
            keys_values()
        elif step[0] == "join_cores":
            join_cores()
        elif step[0] == "input_grad":
            input_grad()
        elif step[0] == "small":
            small(step[1])
        else:
            stages(step)
    reduce.finish()
    swap.finish()
    give.wait()
    for g in range(4):
        pltpu.make_async_copy(reduce.result(g), outs[g], r["out_sem"].at[g]).wait()


def backward(inputs):
    def shape(*dims, dtype=bf16):
        return jax.ShapeDtypeStruct(dims, dtype)

    outs = [shape(256, 1024, dtype=f32), shape(24, 128, dtype=f32)] + [
        shape(2, 4, rows // 4, cols // 2) for rows, cols in zip(SHARD_ROWS, COLUMNS)
    ]
    vmem = pl.BlockSpec(memory_space=pltpu.VMEM)
    hbm = pl.BlockSpec(memory_space=pl.ANY)
    buffers = [
        pltpu.VMEM(dims, dtype)
        for dims, dtype in (
            ((2, 4, 2, 4, 16, 4096), bf16),
            ((2, 1024, 256), bf16),
            ((2, 1024, 128), bf16),
            ((2, 1024, 128), bf16),
            ((2, 1024, 256), bf16),
            ((2, 1024, 256), bf16),
            ((2, 1024, 128), bf16),
            ((2, 1024, 128), bf16),
            ((1024, 128), f32),
            ((1024, 128), f32),
            ((2, 128, 2048), bf16),
            ((2, 128, 1024), bf16),
            ((2, 128, 1024), bf16),
            ((256, 2048), f32),
            ((256, 1024), f32),
            ((256, 1024), bf16),
            ((2, 128, 1024), bf16),
            ((256, 1024), f32),
            ((256, 128), f32),
            ((256, 128), f32),
            ((2, 4, 2, 16, 128), bf16),
            ((1, 1024), f32),
            ((1024, 256), bf16),
            ((256, 1024), f32),
            ((1, 128), f32),
            ((1, 128), f32),
            ((5, 4, 24, 128), f32),
        )
    ]
    dma = pltpu.SemaphoreType.DMA
    sems = [
        dma((4, 44)),
        dma((4, 44)),
        dma((4,)),
        dma((5, 3)),
        dma((5, 3)),
        dma((4,)),
        dma((8, 7)),
        dma((8, 7)),
        dma((16,)),
    ]
    results = pl.pallas_call(
        functools.partial(backward_kernel),
        out_shape=outs,
        in_specs=[hbm] * len(BACKWARD_IN),
        out_specs=[hbm, vmem] + [hbm] * 4,
        scratch_shapes=reduce_scratch() + buffers + sems,
        compiler_params=pltpu.CompilerParams(
            collective_id=2, has_side_effects=True, vmem_limit_bytes=63 * 1024 * 1024
        ),
        name="backward",
    )(*[inputs[name] for name in BACKWARD_IN])
    return dict(zip(BACKWARD_OUT, results))


def finish_kernel(*refs):
    gq, gk, gv, go, gg, gu, gd, d_attn, d_query, d_key, d_ffn = refs[5:16]
    qkv, output, gate_up, down, gains, sem = refs[16:]
    copies = [pltpu.make_async_copy(refs[at], refs[16 + at], sem.at[at]) for at in range(5)]
    for copy in copies:
        copy.start()
    for copy in copies:
        copy.wait()
    gq[...] = qkv[0].astype(f32)
    gk[...] = qkv[1, :, :1024].astype(f32)
    gv[...] = qkv[1, :, 1024:].astype(f32)
    for half in range(2):
        cols = slice(half * 512, (half + 1) * 512)
        go[:, cols] = output[half].astype(f32)
        gd[:, cols] = down[half].astype(f32)
    gg[...] = gate_up[0].astype(f32)
    gu[...] = gate_up[1].astype(f32)
    dp = lax.axis_index("dp")
    row, lane = dp // 2, dp % 2 * 64
    for ref, at in ((d_attn, row), (d_ffn, 10 + row)):
        ref[...] = pltpu.roll(gains[pl.ds(at, 1), :], lane, 1)[:, :64]
    for ref, at in ((d_query, 8), (d_key, 9)):
        ref[...] = pltpu.roll(gains[at : at + 1, :], (128 - dp * 8) % 128, 1)[:, :8]


def finish(sums, gains):
    def shape(*dims):
        return jax.ShapeDtypeStruct(dims, f32)

    outs = [
        shape(64, 2048),
        shape(64, 1024),
        shape(64, 1024),
        shape(128, 1024),
        shape(64, 3072),
        shape(64, 3072),
        shape(192, 1024),
        shape(1, 64),
        shape(1, 8),
        shape(1, 8),
        shape(1, 64),
    ]
    vmem = pl.BlockSpec(memory_space=pltpu.VMEM)
    sums = [part.reshape(2, rows, cols // 2) for part, rows, cols in zip(sums, SHARD_ROWS, COLUMNS)]
    return pl.pallas_call(
        functools.partial(finish_kernel),
        out_shape=outs,
        in_specs=[pl.BlockSpec(memory_space=pl.ANY)] * 5,
        out_specs=[vmem] * 11,
        scratch_shapes=[pltpu.VMEM(part.shape, part.dtype) for part in (*sums, gains)]
        + [pltpu.SemaphoreType.DMA((5,))],
        compiler_params=pltpu.CompilerParams(vmem_limit_bytes=60 * 1024 * 1024),
        name="finish",
    )(*sums, gains)


def rotary_tables(positions):
    frequency = jnp.exp(jnp.arange(64, dtype=f32) * (-2.0 * math.log(rope_base) / 128))
    angles = positions.astype(f32)[:, None] * frequency[None, :]
    cos_half, sin_half = jnp.cos(angles), jnp.sin(angles)
    return (
        jnp.concatenate([cos_half, cos_half], axis=-1),
        jnp.concatenate([-sin_half, sin_half], axis=-1),
    )


def per_device(
    hidden_in,
    out_cotangent,
    slot_lengths,
    position_ids,
    attn_gain,
    w_query,
    key_weight,
    value_weight,
    query_gain,
    key_gain,
    w_output,
    ffn_gain,
    w_gate,
    w_up,
    w_down,
):
    dp = lax.axis_index("dp")
    lane = jnp.arange(128, dtype=jnp.int32)[None, :]
    wide = jnp.stack([attn_gain, ffn_gain])
    wide = jnp.where(lane // 64 == dp % 2, jnp.concatenate([wide, wide], axis=1), 0)
    narrow = jnp.where(lane // 8 == dp, jnp.tile(jnp.stack([query_gain, key_gain]), (1, 16)), 0)
    tile = jnp.concatenate([wide[:1], narrow, wide[1:], jnp.zeros((12, 128), bf16)], axis=0)
    valid = jnp.broadcast_to((slot_lengths - lax.axis_index("seq") * 128).astype(f32)[:, None, None], (2, 8, 128))
    cos, sin = rotary_tables(position_ids.reshape(256))
    shards = (w_query, key_weight, value_weight, w_output, w_gate, w_up, w_down)
    done = forward(shards, tile, hidden_in, out_cotangent, cos, sin, valid)
    done.update(hidden=hidden_in, cos=cos, sin=sin)
    for name, rows, cols in (("total_output", 32, 512), ("total_gate_up", 16, 3072), ("total_down", 48, 512)):
        done[name] = done[name].reshape(2, 2, 4, 4, rows, cols)
    done["weights_qkv"] = done["weights_qkv"].reshape(2, 4, 2, 4, 16, 4096)
    last = backward(done)
    sums = [last[name] for name in ("sum_qkv", "sum_output", "sum_gate_up", "sum_down")]
    d_input = last["d_input"].reshape(2, 128, 1024)
    gq, gk, gv, go, gg, gu, gd, *gains = finish(sums, last["gains_sum"])
    dg_attn, dg_query, dg_key, dg_ffn = [gain.reshape(-1) for gain in gains]
    return (done["out"], d_input, dg_attn, gq, gk, gv, dg_query, dg_key, go, dg_ffn, gg, gu, gd)


def solution(mesh):
    slots, rows, vector, matrix = P("dp", "seq", None), P("dp", "seq"), P("dp"), P("dp", None)
    in_specs = (
        slots,
        slots,
        vector,
        rows,
        vector,
        matrix,
        matrix,
        matrix,
        vector,
        vector,
        matrix,
        vector,
        matrix,
        matrix,
        matrix,
    )
    out_specs = (
        slots,
        slots,
        vector,
        matrix,
        matrix,
        matrix,
        vector,
        vector,
        matrix,
        vector,
        matrix,
        matrix,
        matrix,
    )
    return jax.shard_map(
        per_device, mesh=mesh, in_specs=in_specs, out_specs=out_specs, check_vma=False
    )
```

```python
import functools
import math

import jax
import jax.numpy as jnp
from jax import lax
from jax.experimental import pallas as pl
from jax.experimental.pallas import tpu as pltpu
from jax.sharding import PartitionSpec as P

epsilon = 1e-06
rope_base = 1000000.0
bf16 = jnp.bfloat16
f32 = jnp.float32


MESH = pl.DeviceIdType.MESH
SHARD_ROWS = (64, 128, 64, 192)
COLUMNS = (4096, 1024, 6144, 1024)
THIRDS = ((512, 512, 1024), (128, 128, 256), (768, 768, 1536), (128, 128, 256))


GATHER_ROWS = (64, 64, 128, 64, 64, 192)
GATHER_COLUMNS = (2048, 2048, 1024, 3072, 3072, 1024)
GATHER_FIRST = (0, 2048, 0, 0, 0, 0)
SHARED = (640, 640, 384, 1024, 1024, 384)
SHARES = (
    (256, 256, 128),
    (128, 256, 256),
    (128, 128, 128),
    (384, 256, 384),
    (256, 384, 384),
    (128, 128, 128),
)


class Place:
    def __init__(self):
        dp, seq = lax.axis_index("dp"), lax.axis_index("seq")
        x, y_lo = seq // 2, seq % 2
        y_hi, z, core = dp // 8, (dp // 2) % 4, dp % 2
        self.dp, self.seq, self.x, self.y_lo = dp, seq, x, y_lo
        self.y_hi, self.z, self.core = y_hi, z, core
        self.z_up, self.z_down, self.z_far = (z + 1) % 4, (z + 3) % 4, (z + 2) % 4
        self.color = (x + y_lo + y_hi) % 2
        self.to_z_up = (y_hi * 8 + self.z_up * 2 + core, seq)
        self.to_z_down = (y_hi * 8 + self.z_down * 2 + core, seq)
        self.to_x_up = (dp, ((x + 1) % 4) * 2 + y_lo)
        self.to_x_down = (dp, ((x + 3) % 4) * 2 + y_lo)
        self.to_pair = (dp, x * 2 + 1 - y_lo)
        self.to_cross = ((1 - y_hi) * 8 + z * 2 + core, x * 2 + 1 - y_lo)
        self.to_core = (y_hi * 8 + z * 2 + 1 - core, seq)

    def torus(self):
        return (
            self.to_z_up,
            self.to_z_down,
            self.to_x_up,
            self.to_x_down,
            self.to_pair,
            self.to_cross,
            self.to_core,
        )


def greet(peers):
    barrier = pltpu.get_barrier_semaphore()
    for peer in peers:
        pl.semaphore_signal(barrier, inc=1, device_id=peer, device_id_type=MESH)
    pl.semaphore_wait(barrier, len(peers))


GATHER_KINDS = (
    "own_up",
    "own_down",
    "on_up",
    "on_down",
    "cross_own",
    "cross_up",
    "cross_down",
    "cross_far",
    "other_up",
    "other_down",
    "other_on_up",
    "other_on_down",
) + tuple(f"share_{n}_{s}" for n in range(3) for s in ("up", "down", "far", "other"))
GATHER_KINDS += tuple(f"core_{s}" for s in ("own", "up", "down", "far", "other"))
KIND_AT = {kind: at for at, kind in enumerate(GATHER_KINDS)}
KINDS = len(GATHER_KINDS)


class Gather:
    def __init__(self, place, buffers, send_sem, recv_sem):
        self.place, self.buffers, self.send_sem, self.recv_sem = place, buffers, send_sem, recv_sem
        self.sent = []

    def region(self, g, kind, receiving):
        p = self.place
        rows, cols = GATHER_ROWS[g], GATHER_COLUMNS[g]
        shared = SHARED[g]
        here, there = p.y_hi, 1 - p.y_hi
        whole, top, low = pl.ds(0, rows), pl.ds(0, rows // 2), pl.ds(rows // 2, rows // 2)
        low_first = pl.ds(rows // 2, rows // 4)
        low_last = pl.ds(rows // 2 + rows // 4, rows // 4)
        color = p.color
        if kind.startswith("share") and receiving:
            color = 1 - color
        begin = GATHER_FIRST[g]
        mine = pl.ds(pl.multiple_of(begin + color * shared, 128), cols - shared)
        below, above = p.z_down, p.z_up
        z, far = p.z, p.z_far
        buf = self.buffers[g]

        def at(y, zz, r, c):
            return buf.at[y, zz, p.core, r, c]

        def at_core(y, zz, core):
            return buf.at[y, zz, core, :, pl.ds(begin, cols)]

        if kind == "own_up":
            return at(here, below if receiving else z, whole, mine), p.to_z_up
        if kind == "own_down":
            return at(here, above if receiving else z, whole, mine), p.to_z_down
        if kind == "on_up":
            return at(here, far if receiving else below, top, mine), p.to_z_up
        if kind == "on_down":
            return at(here, far if receiving else above, low, mine), p.to_z_down
        if kind.startswith("cross"):
            y = there if receiving else here
            which = kind[6:]
            if which == "own":
                return at(y, z, whole, mine), p.to_cross
            return at(y, {"up": above, "down": below, "far": far}[which], top, mine), p.to_cross
        if kind == "other_up":
            return at(there, below if receiving else z, low, mine), p.to_z_up
        if kind == "other_down":
            return at(there, above if receiving else z, low, mine), p.to_z_down
        if kind == "other_on_up":
            return at(there, far if receiving else below, low_first, mine), p.to_z_up
        if kind == "other_on_down":
            return at(there, far if receiving else above, low_last, mine), p.to_z_down
        if kind.startswith("share"):
            _, n, which = kind.split("_")
            n = int(n)
            start = begin + color * (cols - shared) + sum(SHARES[g][:n])
            part = pl.ds(pl.multiple_of(start, 128), SHARES[g][n])
            to = (p.to_x_up, p.to_x_down, p.to_pair)[n]
            if which == "other":
                return buf.at[there, :, p.core, :, part], to
            return at(here, {"up": above, "down": below, "far": far}[which], whole, part), to
        which = kind[5:]
        core = 1 - p.core if receiving else p.core
        if which == "other":
            return buf.at[there, :, core, :, pl.ds(begin, cols)], p.to_core
        return at_core(here, {"own": z, "up": above, "down": below, "far": far}[which], core), p.to_core

    def copy(self, g, kind, receiving=False):
        region, to = self.region(g, kind, receiving)
        at = KIND_AT[kind]
        return pltpu.make_async_remote_copy(
            src_ref=region,
            dst_ref=region,
            send_sem=self.send_sem.at[g, at],
            recv_sem=self.recv_sem.at[g, at],
            device_id=to,
            device_id_type=MESH,
        )

    def send(self, g, *kinds):
        for kind in kinds:
            self.copy(g, kind).start()
            self.sent.append((g, kind))

    def take(self, g, *kinds):
        for kind in kinds:
            self.copy(g, kind, True).wait_recv()

    def share(self, g, which):
        self.send(g, *(f"share_{n}_{which}" for n in range(3)))

    def taken(self, g, which):
        self.take(g, *(f"share_{n}_{which}" for n in range(3)))

    def phase(self, number, g):
        if number == 0:
            self.send(g, "own_up", "own_down", "cross_own", "core_own")
        elif number == 1:
            self.take(g, "own_up", "own_down")
            self.send(g, "on_up", "on_down", "cross_up", "cross_down")
            self.share(g, "up")
            self.share(g, "down")
        elif number == 2:
            self.take(g, "cross_own")
            self.send(g, "other_up", "other_down")
        elif number == 8:
            self.take(g, "on_up", "on_down")
            self.send(g, "cross_far")
            self.share(g, "far")
        elif number == 3:
            self.take(g, "other_up", "other_down")
            self.send(g, "other_on_up", "other_on_down")
        elif number == 4:
            self.take(g, "cross_up", "cross_down", "cross_far", "other_on_up", "other_on_down")
            self.share(g, "other")
        elif number == 5:
            for which in ("up", "down", "far"):
                self.taken(g, which)
                self.send(g, f"core_{which}")
        elif number == 6:
            self.taken(g, "other")
            self.send(g, "core_other")
        else:
            self.take(g, "core_own", "core_up", "core_down", "core_far", "core_other")

    def finish(self, *groups):
        for g, kind in self.sent:
            if g in groups:
                self.copy(g, kind).wait_send()
        self.sent = [one for one in self.sent if one[0] not in groups]


def own_copies(place, shards, buffers):
    mine = [buf.at[place.y_hi, place.z, place.core] for buf in buffers]
    query, key, value, output, gate, up, down = shards
    first, last = pl.ds(0, 1536), pl.ds(1536, 1536)
    return (
        (query, mine[0].at[:, pl.ds(0, 2048)]),
        (key, mine[0].at[:, pl.ds(2048, 1024)]),
        (value, mine[0].at[:, pl.ds(3072, 1024)]),
        (output, mine[1]),
        (gate.at[:, first], mine[2].at[:, first]),
        (up.at[:, first], mine[2].at[:, last]),
        (gate.at[:, last], mine[3].at[:, first]),
        (up.at[:, last], mine[3].at[:, last]),
        (down, mine[4]),
    )


class GatherSmall:
    def __init__(self, place, buffer, send_sem, recv_sem):
        self.place, self.buffer, self.send_sem, self.recv_sem = place, buffer, send_sem, recv_sem

    def copy(self, step, receiving=False):
        p, buf = self.place, self.buffer
        if step == 0:
            region, to = buf.at[p.y_hi, p.z, 1 - p.core if receiving else p.core], p.to_core
        elif step == 1:
            region, to = buf.at[1 - p.y_hi if receiving else p.y_hi, p.z], p.to_cross
        elif step == 2:
            region, to = buf.at[:, p.z_down if receiving else p.z], p.to_z_up
        elif step == 3:
            region, to = buf.at[:, p.z_up if receiving else p.z], p.to_z_down
        else:
            region, to = buf.at[:, p.z_far if receiving else p.z_down], p.to_z_up
        return pltpu.make_async_remote_copy(
            src_ref=region,
            dst_ref=region,
            send_sem=self.send_sem.at[step],
            recv_sem=self.recv_sem.at[step],
            device_id=to,
            device_id_type=MESH,
        )

    def start(self, step):
        self.copy(step).start()

    def take(self, step):
        self.copy(step, True).wait_recv()

    def finish(self):
        for step in range(5):
            self.copy(step).wait_send()


PART_ORDER = ("xyz", "yzx", "zxy")
FREE = ((("yl", "yh", "z"), ("z",), ()), (("z", "x"), ("x",), ()), (("yl", "yh", "x"), ("yl", "yh"), ()))
EXTENT = {"yl": 2, "yh": 2, "z": 4, "x": 4}


def half_shape(part, step):
    free = FREE[part][step]
    first = EXTENT[free[0]] // 2
    return ((first,) if first > 1 else ()) + tuple(EXTENT[d] for d in free[1:])


def near_shape(part, step):
    return tuple(EXTENT[d] for d in FREE[part][step])


def reduce_scratch():
    shapes = []
    for g in range(4):
        rows, half = SHARD_ROWS[g] // 4, COLUMNS[g] // 2
        shapes.append(pltpu.VMEM((2, 2, 4, 4, rows, half), bf16))
        shapes.append(pltpu.VMEM((2, 4, rows, half), bf16))
        for part in range(3):
            tail = (rows, THIRDS[g][part])
            for step in range(3):
                if step < 2:
                    shapes.append(pltpu.VMEM((2,) + half_shape(part, step) + tail, bf16))
                else:
                    shapes.append(pltpu.VMEM((1,) + tail, bf16))
                shapes.append(pltpu.VMEM((2,) + near_shape(part, step) + tail, bf16))
    return shapes


SCRATCH_PER_GROUP = 2 + 18


def accumulate(dst, src):
    lead = dst.shape[:-2]
    count = 1
    for n in lead:
        count *= n
    if not lead:
        dst[...] = dst[...] + src[...]
        return

    def body(i, carry):
        at, rest = [], i
        for n in reversed(lead):
            at.append(rest % n)
            rest = rest // n
        at = tuple(reversed(at))
        dst.at[at][...] = dst.at[at][...] + src.at[at][...]
        return carry

    lax.fori_loop(0, count, body, 0)


class Reduce:
    def __init__(self, place, grads, scratch, send_sem, recv_sem, load_sem):
        self.place, self.grads = place, grads
        self.send_sem, self.recv_sem, self.load_sem = send_sem, recv_sem, load_sem
        self.sent = []
        self.groups = [scratch[g * SCRATCH_PER_GROUP : (g + 1) * SCRATCH_PER_GROUP] for g in range(4)]

    def total(self, g):
        return self.groups[g][0]

    def result(self, g):
        return self.groups[g][1]

    def halves(self, g, part, step):
        return self.groups[g][2 + (part * 3 + step) * 2]

    def nears(self, g, part, step):
        return self.groups[g][3 + (part * 3 + step) * 2]

    def cols(self, g, part):
        return pl.ds(sum(THIRDS[g][:part]), THIRDS[g][part])

    def moved(self, dim, by):
        p = self.place
        if dim == "x":
            x = (p.x + by) % 4
            return {"x": x}, (p.dp, x * 2 + p.y_lo)
        if dim == "z":
            z = (p.z + by) % 4
            return {"z": z}, (p.y_hi * 8 + z * 2 + p.core, p.seq)
        y = (p.y_hi * 2 + p.y_lo + by) % 4
        return {"yl": y % 2, "yh": y // 2}, ((y // 2) * 8 + p.z * 2 + p.core, p.x * 2 + y % 2)

    def chunk(self, g, part, step, by, half=None):
        at = {}
        for earlier in range(step):
            at.update(self.moved(PART_ORDER[part][earlier], 0)[0])
        at.update(self.moved(PART_ORDER[part][step], by)[0])
        if half is not None:
            cut = FREE[part][step][0]
            size = EXTENT[cut] // 2
            at[cut] = half if size == 1 else pl.ds(half * size, size)
        index = tuple(at.get(name, slice(None)) for name in ("yl", "yh", "z", "x"))
        return self.total(g).at[index + (slice(None), self.cols(g, part))]

    def remote(self, g, sem, src, dst, to):
        return pltpu.make_async_remote_copy(
            src_ref=src,
            dst_ref=dst,
            send_sem=self.send_sem.at[g, sem],
            recv_sem=self.recv_sem.at[g, sem],
            device_id=to,
            device_id_type=MESH,
        )

    def send(self, g, sem, src, dst, to):
        copy = self.remote(g, sem, src, dst, to)
        copy.start()
        self.sent.append(copy)

    def take(self, g, sem, dst):
        self.remote(g, sem, dst, dst, self.place.to_core).wait_recv()

    def load(self, g):
        return pltpu.make_async_copy(self.grads[g], self.total(g), self.load_sem.at[g])

    def send_far(self, g, step):
        for part in range(3):
            sem, dim = part * 12 + step * 4, PART_ORDER[part][step]
            buf = self.halves(g, part, step)
            up, down = self.moved(dim, 1)[1], self.moved(dim, 3)[1]
            if step < 2:
                self.send(g, sem, self.chunk(g, part, step, 2, 0), buf.at[0], up)
                self.send(g, sem + 1, self.chunk(g, part, step, 2, 1), buf.at[1], down)
            else:
                self.send(g, sem, self.chunk(g, part, step, 2), buf.at[0], up)

    def send_near(self, g, step):
        for part in range(3):
            sem, dim = part * 12 + step * 4, PART_ORDER[part][step]
            buf, near = self.halves(g, part, step), self.nears(g, part, step)
            up, down = self.moved(dim, 1)[1], self.moved(dim, 3)[1]
            self.take(g, sem, buf.at[0])
            accumulate(self.chunk(g, part, step, 1, 0 if step < 2 else None), buf.at[0])
            self.send(g, sem + 2, self.chunk(g, part, step, 1), near.at[0], up)
            if step < 2:
                self.take(g, sem + 1, buf.at[1])
                accumulate(self.chunk(g, part, step, 3, 1), buf.at[1])
            self.send(g, sem + 3, self.chunk(g, part, step, 3), near.at[1], down)

    def join_near(self, g, step):
        for part in range(3):
            sem, near = part * 12 + step * 4, self.nears(g, part, step)
            for way in range(2):
                self.take(g, sem + 2 + way, near.at[way])
                accumulate(self.chunk(g, part, step, 0), near.at[way])

    def stage(self, number, g):
        p = self.place
        result = self.result(g)
        if number == 0:
            if self.grads[g] is not None:
                self.load(g).wait()
            self.send_far(g, 0)
        elif number in (1, 3, 5):
            self.send_near(g, number // 2)
        elif number in (2, 4):
            self.join_near(g, number // 2 - 1)
            self.send_far(g, number // 2)
        elif number == 6:
            self.join_near(g, 2)
            result.at[p.y_lo, p.x][...] = self.total(g).at[p.y_lo, p.y_hi, p.z, p.x][...]
            mine = result.at[p.y_lo, p.x]
            self.send(g, 37, mine, mine, p.to_pair)
        elif number == 7:
            self.take(g, 37, result.at[1 - p.y_lo, p.x])
            mine = result.at[:, p.x]
            self.send(g, 38, mine, mine, p.to_x_up)
            self.send(g, 39, mine, mine, p.to_x_down)
        elif number == 8:
            below, above = (p.x + 3) % 4, (p.x + 1) % 4
            self.take(g, 38, result.at[:, below])
            self.send(g, 40, result.at[0, below], result.at[0, below], p.to_x_up)
            self.take(g, 39, result.at[:, above])
            self.send(g, 41, result.at[1, above], result.at[1, above], p.to_x_down)
        else:
            far = (p.x + 2) % 4
            self.take(g, 40, result.at[0, far])
            self.take(g, 41, result.at[1, far])

    def finish(self):
        for copy in self.sent:
            copy.wait_send()
        self.sent = []


class ReduceSmall:
    STEPS = (("core", 2), ("pair", 2), ("cross", 2), ("x", 4), ("z", 4))

    def __init__(self, place, slots, send_sem, recv_sem):
        self.place, self.slots, self.send_sem, self.recv_sem = place, slots, send_sem, recv_sem

    def peers(self, step):
        p = self.place
        name, count = self.STEPS[step]
        if count == 2:
            mine, to = {
                "core": (p.core, p.to_core),
                "pair": (p.y_lo, p.to_pair),
                "cross": (p.y_hi, p.to_cross),
            }[name]
            return mine, [(1 - mine, to)]
        if name == "x":
            return p.x, [((p.x + by) % 4, (p.dp, (p.x + by) % 4 * 2 + p.y_lo)) for by in (1, 2, 3)]
        return p.z, [
            ((p.z + by) % 4, (p.y_hi * 8 + (p.z + by) % 4 * 2 + p.core, p.seq)) for by in (1, 2, 3)
        ]

    def copies(self, step, receiving):
        mine, peers = self.peers(step)
        if receiving:
            peers = peers[::-1]
        for at, (place, to) in enumerate(peers):
            slot = self.slots.at[step, place if receiving else mine]
            yield pltpu.make_async_remote_copy(
                src_ref=slot,
                dst_ref=slot,
                send_sem=self.send_sem.at[step, at],
                recv_sem=self.recv_sem.at[step, at],
                device_id=to,
                device_id_type=MESH,
            )

    def put(self, step, values):
        mine, _ = self.peers(step)
        self.slots.at[step, mine][...] = values
        for copy in self.copies(step, False):
            copy.start()

    def sum(self, step):
        for copy in self.copies(step, True):
            copy.wait_recv()
        for copy in self.copies(step, False):
            copy.wait_send()
        total = self.slots[step, 0]
        for at in range(1, self.STEPS[step][1]):
            total = total + self.slots[step, at]
        return total


SCALE = 128 ** (-0.5)
OFFSETS = tuple((dx, dy) for dx in range(4) for dy in range(2) if (dx, dy) != (0, 0))


def mm(left, right):
    return jnp.dot(left, right, preferred_element_type=f32)


def mm_nt(left, right):
    return lax.dot_general(left, right, (((1,), (1,)), ((), ())), preferred_element_type=f32)


def mm_tn(left, right):
    return lax.dot_general(left, right, (((0,), (0,)), ((), ())), preferred_element_type=f32)


def inv_rms(v):
    return lax.rsqrt(jnp.mean(v * v, axis=-1, keepdims=True) + epsilon)


class Exchange:
    def __init__(self, place, send_sem, recv_sem):
        self.place, self.send_sem, self.recv_sem, self.sent = place, send_sem, recv_sem, []

    def partner(self, at, back=False):
        dx, dy = OFFSETS[at]
        x = (self.place.x + (4 - dx if back else dx)) % 4
        return x * 2 + (self.place.y_lo + dy) % 2

    def send(self, kind, src, dst):
        for at in range(7):
            partner = self.partner(at)
            copy = pltpu.make_async_remote_copy(
                src_ref=src(partner),
                dst_ref=dst(self.place.seq),
                send_sem=self.send_sem.at[kind, at],
                recv_sem=self.recv_sem.at[kind, at],
                device_id=(self.place.dp, partner),
                device_id_type=MESH,
            )
            copy.start()
            self.sent.append(copy)

    def take(self, kind, dst):
        for at in range(7):
            partner = self.partner(at, back=True)
            pltpu.make_async_remote_copy(
                src_ref=dst(partner),
                dst_ref=dst(partner),
                send_sem=self.send_sem.at[kind, at],
                recv_sem=self.recv_sem.at[kind, at],
                device_id=(self.place.dp, partner),
                device_id_type=MESH,
            ).wait_recv()

    def finish(self):
        for copy in self.sent:
            copy.wait_send()
        self.sent = []


def token_rows(seq):
    return pl.ds(pl.multiple_of(seq * 128, 128), 128)


def head_cols(seq, width):
    return pl.ds(pl.multiple_of(seq * width, 128), width)


def gain_rows(tile_ref):
    tiles = tile_ref[...].astype(f32).reshape(8, 2, 16, 128)
    pairs = tiles[:, 0] + tiles[:, 1]
    total = pairs[0]
    for at in range(1, 8):
        total = total + pairs[at]

    def wide(row):
        return jnp.concatenate([pairs[at, row : row + 1, :] for at in range(8)], axis=-1)

    return wide(0), total[1:2, :], total[2:3, :], wide(3)


def causal_scores(q, k, first):
    scores = mm_nt(q, k) * SCALE
    row = first + lax.broadcasted_iota(jnp.int32, scores.shape, 0)
    col = lax.broadcasted_iota(jnp.int32, scores.shape, 1)
    return jnp.where(col <= row, scores, -1e30)


FORWARD_IN = (
    "w_query", "w_key", "w_value", "w_output", "w_gate", "w_up", "w_down", "gains",
    "hidden", "cot", "cos", "sin", "valid",
)
FORWARD_OUT = (
    "out", "d_residual", "d_attended", "dg_ffn", "x_in", "q_flat", "k_flat",
    "total_output", "total_gate_up", "total_down", "weights_qkv", "q_heads", "k_heads", "v_heads", "gain_tiles",
)
FORWARD_SCRATCH = (
    "buf_qkv", "buf_output", "buf_gate_up_0", "buf_gate_up_1", "buf_down", "tiles", "rows", "core_down",
    "q_in", "k_in", "v_in", "att", "context", "residual", "mid_in", "mid_turned", "result", "d_mid", "d_branch",
    "gather_send", "gather_recv", "small_send", "small_recv", "local_sem", "swap_send", "swap_recv", "out_sem",
    "core_free", "core_send", "core_recv",
    "out_out", "d_residual_out", "d_attended_out", "x_in_out", "q_flat_out", "k_flat_out",
    "hidden_in", "cot_in", "cos_in", "sin_in", "valid_in",
)
FF_TILE = 768


def forward_kernel(*refs):
    r = dict(zip(FORWARD_IN + FORWARD_OUT + FORWARD_SCRATCH, refs))
    place = Place()
    me = place.seq
    buffers = [r["buf_qkv"], r["buf_output"], r["buf_gate_up_0"], r["buf_gate_up_1"], r["buf_down"]]
    tiles = r["tiles"]
    pairs = own_copies(place, [r[name] for name in FORWARD_IN[:7]], buffers)
    pairs += ((r["gains"], tiles.at[place.y_hi, place.z, place.core]),)
    copies = [
        pltpu.make_async_copy(shard, there, r["local_sem"].at[at]) for at, (shard, there) in enumerate(pairs)
    ]
    for copy in copies:
        copy.start()
    inputs = [
        pltpu.make_async_copy(r[name], r[name + "_in"], r["local_sem"].at[10 + at])
        for at, name in enumerate(FORWARD_IN[8:])
    ]
    for copy in inputs:
        copy.start()
    greet(
        place.torus()
        + tuple(
            (place.dp, (place.x + dx) % 4 * 2 + (place.y_lo + dy) % 2)
            for dx, dy in OFFSETS
            if (dx, dy) not in ((1, 0), (3, 0), (0, 1))
        )
    )
    for copy in copies:
        copy.wait()
    gather = Gather(place, [buffers[0]] + buffers, r["gather_send"], r["gather_recv"])
    little = GatherSmall(place, tiles, r["small_send"], r["small_recv"])
    swap = Exchange(place, r["swap_send"], r["swap_recv"])
    saved = []

    def save(name, src, dst=None):
        at = len(saved)
        copy = pltpu.make_async_copy(src, r[name] if dst is None else dst, r["out_sem"].at[at])
        copy.start()
        saved.append(copy)

    def phases(*steps):
        for number, g in steps:
            gather.phase(number, g)

    little.start(0)
    phases((0, 0), (0, 1))
    little.take(0)
    little.start(1)
    phases((1, 0))
    little.take(1)
    little.start(2)
    little.start(3)
    phases((2, 0), (8, 0))
    little.take(2)
    little.take(3)
    little.start(4)
    phases((3, 0), (0, 3), (1, 1), (4, 0), (5, 0))
    little.take(4)
    for copy in inputs:
        copy.wait()
    g_attn, g_query, g_key, g_ffn = gain_rows(tiles)
    x = r["hidden_in"][...].reshape(256, 1024).astype(f32)
    r["x_in_out"][...] = (x * inv_rms(x) * g_attn).astype(bf16)
    phases((6, 0), (1, 3), (0, 2), (7, 0), (2, 3), (2, 1), (0, 5))
    save("gain_tiles", tiles)

    cos, sin = r["cos_in"], r["sin_in"]

    def qkv_weights(first):
        return buffers[0][:, :, :, :, pl.ds(pl.multiple_of(first, 128), 512)].reshape(1024, 512)

    def head_tile(j, flat_ref, rows_ref, first, gain):
        flat = mm(r["x_in_out"][...], qkv_weights(first + j * 512))
        cols = pl.ds(pl.multiple_of(j * 512, 128), 512)
        flat_ref[:, cols] = flat
        done = []
        for h in range(4):
            v = flat[:, h * 128 : (h + 1) * 128]
            v = v * inv_rms(v) * gain
            done.append((v * cos[...] + pltpu.roll(v, 64, 1) * sin[...]).astype(bf16))
        rows_ref[...] = jnp.concatenate(done, axis=-1).reshape(2, 128, 512)

    def query_tile(j, carry):
        head_tile(j, r["q_flat_out"], r["rows"].at[0, :, :, pl.ds(pl.multiple_of(j * 512, 128), 512)], 0, g_query)
        return carry

    def key_tile(j, carry):
        head_tile(j, r["k_flat_out"], r["rows"].at[1, :, :, pl.ds(pl.multiple_of(j * 512, 128), 512)], 2048, g_key)
        return carry

    def value_tile(j, carry):
        cols = pl.ds(pl.multiple_of(1024 + j * 512, 128), 512)
        r["rows"][1, :, :, cols] = mm(r["x_in_out"][...], qkv_weights(3072 + j * 512)).astype(bf16).reshape(2, 128, 512)
        return carry

    def to_heads(kind, at, first, heads, width):
        def cols(seq):
            return pl.ds(pl.multiple_of(first + seq * width, 128), width)

        swap.send(
            kind,
            lambda partner: r["rows"].at[at, :, :, cols(partner)],
            lambda sender: r[heads].at[:, token_rows(sender), :],
        )
        r[heads][:, token_rows(me), :] = r["rows"][at, :, :, cols(me)]

    lax.fori_loop(0, 4, query_tile, 0)
    to_heads(0, 0, 0, "q_in", 256)
    phases(
        (8, 1), (3, 1), (8, 3), (0, 4), (3, 3), (1, 5), (1, 2), (4, 1), (5, 1), (1, 4), (4, 3), (6, 1), (8, 5),
        (2, 4), (2, 2), (5, 3), (7, 1), (2, 5),
    )
    save("weights_qkv", buffers[0])
    lax.fori_loop(0, 2, key_tile, 0)
    to_heads(1, 1, 0, "k_in", 128)
    lax.fori_loop(0, 2, value_tile, 0)
    to_heads(2, 1, 1024, "v_in", 128)
    phases((3, 5), (6, 3), (8, 2), (4, 5), (3, 2), (4, 2))
    save("x_in", r["x_in_out"])
    save("q_flat", r["q_flat_out"])
    save("k_flat", r["k_flat_out"])
    swap.take(0, lambda sender: r["q_in"].at[:, token_rows(sender), :])
    swap.take(1, lambda sender: r["k_in"].at[:, token_rows(sender), :])
    swap.take(2, lambda sender: r["v_in"].at[:, token_rows(sender), :])
    save("q_heads", r["q_in"])
    save("k_heads", r["k_in"])
    save("v_heads", r["v_in"])

    def attend(slot, head):
        cols = slice(head * 128, (head + 1) * 128)
        for block in range(4):
            rows, upto = slice(block * 256, (block + 1) * 256), (block + 1) * 256
            q = r["q_in"][slot, rows, cols]
            scores = causal_scores(q, r["k_in"][slot, :upto, :], block * 256)
            top = jnp.max(scores, axis=-1, keepdims=True)
            shifted = jnp.exp(scores - top)
            total = jnp.sum(shifted, axis=-1, keepdims=True)
            prob = (shifted * (1.0 / total)).astype(bf16)
            r["att"][slot, rows, cols] = mm(prob, r["v_in"][slot, :upto, :]).astype(bf16)

    for slot in range(2):
        attend(slot, 0)
        attend(slot, 1)
        swap.send(
            3 + slot,
            lambda partner: r["att"].at[slot, token_rows(partner), :],
            lambda sender: r["context"].at[slot, :, head_cols(sender, 256)],
        )
        r["context"][slot, :, head_cols(me, 256)] = r["att"][slot, token_rows(me), :]
    phases((5, 2), (6, 2), (5, 5), (8, 4), (3, 4), (6, 5), (4, 4), (7, 2), (7, 5), (5, 4))
    for slot in range(2):
        swap.take(3 + slot, lambda sender: r["context"].at[slot, :, head_cols(sender, 256)])

    for half in range(2):
        cols = slice(half * 512, (half + 1) * 512)
        weights = buffers[1][:, :, :, :, cols].reshape(2048, 512)
        x = r["hidden_in"][:, :, cols].reshape(256, 512).astype(f32)
        r["residual"][:, cols] = x + mm(r["context"][...].reshape(256, 2048), weights)
    residual = r["residual"][...]
    mid_in = residual * inv_rms(residual) * g_ffn
    r["mid_in"][...] = mid_in.astype(bf16)
    r["mid_turned"][...] = mid_in.T.astype(bf16)


    def masked(values):
        order = lax.broadcasted_iota(jnp.int32, (128, 1024), 0).astype(f32)
        parts = [
            jnp.where(order < r["valid_in"][slot, :1, :1], values[slot * 128 : (slot + 1) * 128], 0.0)
            for slot in range(2)
        ]
        return jnp.concatenate(parts, axis=0)

    d_result = masked(r["cot_in"][...].reshape(256, 1024).astype(f32))
    r["d_branch"][...] = d_result.astype(bf16)
    phases((7, 3), (6, 4))
    gather.finish(0, 1, 3, 5)
    little.finish()
    swap.finish()
    for copy in saved:
        copy.wait()
    saved.clear()
    pl.semaphore_signal(r["core_free"], inc=1, device_id=place.to_core, device_id_type=MESH)
    pl.semaphore_wait(r["core_free"], 1)
    core, other = place.core, 1 - place.core

    def to_core(src, dst, *at):
        return pltpu.make_async_remote_copy(
            src_ref=src,
            dst_ref=dst,
            send_sem=r["core_send"].at[at],
            recv_sem=r["core_recv"].at[at],
            device_id=place.to_core,
            device_id_type=MESH,
        )

    def ffn_places(f):
        here = pl.ds(pl.multiple_of(f % 2 * FF_TILE, 128), FF_TILE)
        up = pl.ds(pl.multiple_of(1536 + f % 2 * FF_TILE, 128), FF_TILE)
        there = pl.ds(pl.multiple_of(f * FF_TILE, 128), FF_TILE)
        return here, up, there, pl.ds(f % 2 * 2, 2)

    def ffn_copies(b, f):
        here, up, there, z = ffn_places(f)
        weights = buffers[2 + b]
        return (
            to_core(weights.at[:, :, other, :, here], buffers[0].at[:, :, 0, :, there], f, 0),
            to_core(weights.at[:, :, other, :, up], buffers[0].at[:, :, 1, :, there], f, 1),
            to_core(buffers[4].at[b, z, other], r["core_down"].at[b, z], f, 2),
        )

    def ffn_join(b, f):
        here, up, there, z = ffn_places(f)
        weights = buffers[2 + b]
        for copy in ffn_copies(b, f):
            copy.wait_recv()
        weights[:, :, core, :, here] = weights[:, :, core, :, here] + buffers[0][:, :, 0, :, there]
        weights[:, :, core, :, up] = weights[:, :, core, :, up] + buffers[0][:, :, 1, :, there]
        buffers[4][b, z, core] = buffers[4][b, z, core] + r["core_down"][b, z]

    r["result"][...] = residual
    r["d_mid"][...] = jnp.zeros((256, 1024), f32)

    def ffn_tile(b, f):
        gate_cols, up_cols, _, z = ffn_places(f)
        w_gate = buffers[2 + b][:, :, :, :, gate_cols].reshape(1024, FF_TILE)
        w_up = buffers[2 + b][:, :, :, :, up_cols].reshape(1024, FF_TILE)
        w_down = buffers[4][b, z].reshape(FF_TILE, 1024)
        mid, d_branch = r["mid_in"][...], r["d_branch"][...]
        gate, up = mm(mid, w_gate), mm(mid, w_up)
        sig = 1.0 / (1.0 + jnp.exp(-gate))
        silu = gate * sig
        unit = (silu * up).astype(bf16)
        d_unit = mm_nt(d_branch, w_down)
        d_gate = (d_unit * up * (sig * (1.0 + gate * (1.0 - sig)))).astype(bf16)
        d_up = (d_unit * silu).astype(bf16)
        r["result"][...] += mm(unit, w_down)
        r["d_mid"][...] += mm_nt(d_gate, w_gate) + mm_nt(d_up, w_up)
        shape = (4, 2, 64, FF_TILE)
        for part in range(2):
            mid_part = r["mid_turned"][part * 512 : (part + 1) * 512, :]
            buffers[2 + b][part, :, :, :, gate_cols] = mm(mid_part, d_gate).astype(bf16).reshape(shape)
            buffers[2 + b][part, :, :, :, up_cols] = mm(mid_part, d_up).astype(bf16).reshape(shape)
        buffers[4][b, z] = mm_tn(unit, d_branch).astype(bf16).reshape(2, 2, 192, 1024)
        for copy in ffn_copies(b, f):
            copy.start()

    def first_half(f, carry):
        ffn_tile(0, f)

        @pl.when(f > 0)
        def _():
            ffn_join(0, f - 1)

        return carry

    def last_half(f, carry):
        ffn_tile(1, f)

        @pl.when(f > 2)
        def _():
            ffn_join(1, f - 1)

        return carry

    lax.fori_loop(0, 2, first_half, 0)
    phases((7, 4))
    gather.finish(2, 4)
    ffn_join(0, 1)
    lax.fori_loop(2, 4, last_half, 0)
    r["out_out"][...] = masked(r["result"][...]).astype(bf16).reshape(2, 128, 1024)
    save("out", r["out_out"])

    residual, d_mid = r["residual"][...], r["d_mid"][...]
    scale = inv_rms(residual)
    weighed = g_ffn * d_mid
    d_norm = scale * weighed - residual * (scale * scale * scale) * jnp.mean(
        residual * weighed, axis=-1, keepdims=True
    )
    r["dg_ffn"][...] = jnp.sum(d_mid * residual * scale, axis=0, keepdims=True)
    d_result = masked(r["cot_in"][...].reshape(256, 1024).astype(f32))
    r["d_residual_out"][...] = d_result + d_norm
    r["d_branch"][...] = r["d_residual_out"][...].astype(bf16)

    def output_tile(j, carry):
        y, z = j // 2, j % 2 * 2
        cols = pl.ds(pl.multiple_of(j * 512, 128), 512)
        d_attn = r["d_branch"][...]
        weights = buffers[1][y, pl.ds(z, 2)].reshape(512, 1024)
        r["d_attended_out"][:, :, cols] = mm_nt(d_attn, weights).astype(bf16).reshape(2, 128, 512)
        context = r["context"][:, :, cols].reshape(256, 512)
        buffers[1][y, pl.ds(z, 2)] = mm_tn(context, d_attn).astype(bf16).reshape(2, 2, 128, 1024)
        for copy in output_copies(j):
            copy.start()
        return carry

    def output_copies(j):
        y, z = j // 2, j % 2
        return tuple(
            to_core(
                buffers[1].at[y, z * 2 + k, other],
                r["rows"].at[y, z, :, pl.ds(k * 1024, 1024)],
                4 + j,
                k,
            )
            for k in range(2)
        )

    lax.fori_loop(0, 4, output_tile, 0)
    save("d_residual", r["d_residual_out"])
    save("d_attended", r["d_attended_out"])
    ffn_join(1, 3)
    for half in range(2):
        for b in range(2):
            save(
                "total_gate_up",
                buffers[2 + b].at[:, :, core, :, pl.ds(half * 1536, 1536)],
                r["total_gate_up"].at[half, :, :, :, pl.ds(b * 1536, 1536)],
            )
        save("total_down", buffers[4].at[:, :, core, :, pl.ds(half * 512, 512)], r["total_down"].at[half])

    def output_join(j, carry):
        y, z = j // 2, j % 2
        for k, copy in enumerate(output_copies(j)):
            copy.wait_recv()
            cols = slice(k * 1024, (k + 1) * 1024)
            buffers[1][y, z * 2 + k, core] = buffers[1][y, z * 2 + k, core] + r["rows"][y, z, :, cols]
        return carry

    lax.fori_loop(0, 4, output_join, 0)
    for half in range(2):
        save("total_output", buffers[1].at[:, :, core, :, pl.ds(half * 512, 512)], r["total_output"].at[half])
    for at in range(4):
        for copy in ffn_copies(at // 2, at) + output_copies(at):
            copy.wait_send()
    for copy in saved:
        copy.wait()


def forward(shards, gains, hidden, cot, cos, sin, valid):
    def shape(*dims, dtype=bf16):
        return jax.ShapeDtypeStruct(dims, dtype)

    outs = {
        "out": shape(2, 128, 1024),
        "d_residual": shape(256, 1024, dtype=f32),
        "d_attended": shape(2, 128, 2048),
        "dg_ffn": shape(1, 1024, dtype=f32),
        "x_in": shape(256, 1024),
        "q_flat": shape(256, 2048, dtype=f32),
        "k_flat": shape(256, 1024, dtype=f32),
        "total_output": shape(2, 2, 4, 128, 512),
        "total_gate_up": shape(2, 2, 4, 64, 3072),
        "total_down": shape(2, 2, 4, 192, 512),
        "weights_qkv": shape(2, 4, 2, 64, 4096),
        "q_heads": shape(2, 1024, 256),
        "k_heads": shape(2, 1024, 128),
        "v_heads": shape(2, 1024, 128),
        "gain_tiles": shape(2, 4, 2, 16, 128),
    }
    vmem = pl.BlockSpec(memory_space=pltpu.VMEM)
    hbm = pl.BlockSpec(memory_space=pl.ANY)
    scratch = {
        "buf_qkv": (2, 4, 2, 64, 4096),
        "buf_output": (2, 4, 2, 128, 1024),
        "buf_gate_up_0": (2, 4, 2, 64, 3072),
        "buf_gate_up_1": (2, 4, 2, 64, 3072),
        "buf_down": (2, 4, 2, 192, 1024),
        "tiles": (2, 4, 2, 16, 128),
        "rows": (2, 2, 128, 2048),
        "core_down": (2, 4, 192, 1024),
        "q_in": (2, 1024, 256),
        "k_in": (2, 1024, 128),
        "v_in": (2, 1024, 128),
        "att": (2, 1024, 256),
        "context": (2, 128, 2048),
        "residual": ((256, 1024), f32),
        "mid_in": (256, 1024),
        "mid_turned": (1024, 256),
        "result": ((256, 1024), f32),
        "d_mid": ((256, 1024), f32),
        "d_branch": (256, 1024),
    }
    dma = pltpu.SemaphoreType.DMA
    sems = [dma((6, KINDS)), dma((6, KINDS)), dma((5,)), dma((5,)), dma((15,)), dma((5, 7)), dma((5, 7)), dma((11,))]
    sems += [pltpu.SemaphoreType.REGULAR, dma((8, 3)), dma((8, 3))]
    buffers = [
        pltpu.VMEM(*(dims if isinstance(dims[0], tuple) else (dims, bf16))) for dims in scratch.values()
    ]
    results = pl.pallas_call(
        functools.partial(forward_kernel),
        out_shape=list(outs.values()),
        in_specs=[hbm] * 13,
        out_specs=[vmem if name == "dg_ffn" else hbm for name in outs],
        scratch_shapes=buffers
        + sems
        + [
            pltpu.VMEM(outs[name].shape, outs[name].dtype)
            for name in ("out", "d_residual", "d_attended", "x_in", "q_flat", "k_flat")
        ]
        + [pltpu.VMEM(array.shape, array.dtype) for array in (hidden, cot, cos, sin, valid)],
        compiler_params=pltpu.CompilerParams(
            collective_id=1, has_side_effects=True, vmem_limit_bytes=63 * 1024 * 1024
        ),
        name="forward",
    )(*shards, gains, hidden, cot, cos, sin, valid)
    return dict(zip(outs, results))


BACKWARD_IN = (
    "total_output", "total_gate_up", "total_down", "weights_qkv", "d_attended", "q_heads", "k_heads", "v_heads",
    "q_flat", "k_flat", "x_in", "hidden", "d_residual", "cos", "sin", "gain_tiles", "dg_ffn",
)
BACKWARD_OUT = ("d_input", "gains_sum", "sum_qkv", "sum_output", "sum_gate_up", "sum_down")
BACKWARD_SCRATCH = (
    "buf_qkv", "q_in", "k_in", "v_in", "grad_in", "dq", "dk", "dv", "dk_sum", "dv_sum", "dq_rows", "dk_rows", "dv_rows",
    "q_flat_in", "k_flat_in", "x_in_in", "hidden_in", "d_residual_in", "cos_in", "sin_in", "tiles_in", "dg_ffn_in", "x_in_turned", "d_x", "dg_query", "dg_key", "slots",
    "reduce_send", "reduce_recv", "load_sem", "small_send", "small_recv", "out_sem", "swap_send", "swap_recv", "in_sem",
)
BACKWARD_ORDER = (
    (0, 2),
    ("attention", 0),
    ("attention", 1),
    (0, 3),
    (0, 1),
    (1, 2),
    ("rows",),
    ("queries",),
    (1, 3),
    ("keys_values",),
    (1, 1),
    (2, 2),
    (2, 3),
    ("join_cores",),
    (0, 0),
    (3, 2),
    (3, 3),
    (2, 1),
    (1, 0),
    (4, 3),
    (4, 2),
    (3, 1),
    (2, 0),
    (5, 3),
    (5, 2),
    (4, 1),
    (3, 0),
    (6, 3),
    (5, 1),
    ("input_grad",),
    (6, 2),
    (4, 0),
    ("small", 0),
    (7, 3),
    (6, 1),
    ("small", 1),
    (5, 0),
    (7, 2),
    ("small", 2),
    (7, 1),
    (6, 0),
    ("small", 3),
    (8, 3),
    (7, 0),
    ("small", 4),
    (8, 2),
    (8, 0),
    (8, 1),
    (9, 2),
    (9, 1),
    (9, 3),
    (9, 0),
)
LATE_LOADS = (
    "q_flat", "k_flat", "x_in", "weights_qkv", "hidden", "d_residual", "cos", "sin", "gain_tiles", "dg_ffn",
)


def backward_kernel(*refs):
    names = BACKWARD_IN + BACKWARD_OUT
    count = 4 * SCRATCH_PER_GROUP
    r = dict(zip(names, refs))
    scratch = refs[len(names) : len(names) + count]
    r.update(zip(BACKWARD_SCRATCH, refs[len(names) + count :]))
    place = Place()
    me = place.seq
    loads = {
        name: pltpu.make_async_copy(r[name], r[there], r["in_sem"].at[at])
        for at, (name, there) in enumerate(
            (
                ("q_heads", "q_in"),
                ("k_heads", "k_in"),
                ("v_heads", "v_in"),
                ("q_flat", "q_flat_in"),
                ("k_flat", "k_flat_in"),
                ("x_in", "x_in_in"),
                ("weights_qkv", "buf_qkv"),
                ("hidden", "hidden_in"),
                ("d_residual", "d_residual_in"),
                ("cos", "cos_in"),
                ("sin", "sin_in"),
                ("gain_tiles", "tiles_in"),
                ("dg_ffn", "dg_ffn_in"),
            )
        )
    }
    grads = (None, r["total_output"], r["total_gate_up"], r["total_down"])
    outs = (r["sum_qkv"], r["sum_output"], r["sum_gate_up"], r["sum_down"])
    reduce = Reduce(place, grads, scratch, r["reduce_send"], r["reduce_recv"], r["load_sem"])
    little = ReduceSmall(place, r["slots"], r["small_send"], r["small_recv"])
    swap = Exchange(place, r["swap_send"], r["swap_recv"])
    for name in ("q_heads", "k_heads", "v_heads"):
        loads[name].start()
    reduce.load(3).start()
    greet(
        place.torus()
        + tuple(
            (place.dp, (place.x + dx) % 4 * 2 + (place.y_lo + dy) % 2)
            for dx, dy in OFFSETS
            if (dx, dy) not in ((1, 0), (3, 0), (0, 1))
        )
        + ((place.y_hi * 8 + place.z_far * 2 + place.core, place.seq),)
    )
    own = []
    for slot in range(2):
        swap.send(
            slot,
            lambda partner: r["d_attended"].at[slot, :, head_cols(partner, 256)],
            lambda sender: r["grad_in"].at[slot, token_rows(sender), :],
        )
        copy = pltpu.make_async_copy(
            r["d_attended"].at[slot, :, head_cols(me, 256)], r["grad_in"].at[slot, token_rows(me), :], r["in_sem"].at[13 + slot]
        )
        copy.start()
        own.append(copy)
    reduce.load(2).start()
    reduce.load(1).start()
    for name in LATE_LOADS:
        loads[name].start()

    def stages(*steps):
        for number, g in steps:
            reduce.stage(number, g)
            if number == 9:
                pltpu.make_async_copy(reduce.result(g), outs[g], r["out_sem"].at[g]).start()

    for name in ("q_heads", "k_heads", "v_heads"):
        loads[name].wait()

    def attend_back(slot, head):
        cols = slice(head * 128, (head + 1) * 128)
        if head == 0:
            r["dk_sum"][...] = jnp.zeros((1024, 128), f32)
            r["dv_sum"][...] = jnp.zeros((1024, 128), f32)
        for block in range(4):
            rows, upto = slice(block * 256, (block + 1) * 256), (block + 1) * 256
            q, grad = r["q_in"][slot, rows, cols], r["grad_in"][slot, rows, cols]
            k, v = r["k_in"][slot, :upto, :], r["v_in"][slot, :upto, :]
            scores = mm_nt(k, q) * SCALE
            key = lax.broadcasted_iota(jnp.int32, scores.shape, 0)
            query = block * 256 + lax.broadcasted_iota(jnp.int32, scores.shape, 1)
            scores = jnp.where(key <= query, scores, -1e30)
            shifted = jnp.exp(scores - jnp.max(scores, axis=0, keepdims=True))
            prob = shifted * (1.0 / jnp.sum(shifted, axis=0, keepdims=True))
            d_prob = mm_nt(v, grad)
            dot = jnp.sum(prob * d_prob, axis=0, keepdims=True)
            d_score = (prob * (d_prob - dot) * SCALE).astype(bf16)
            r["dk_sum"][:upto, :] += mm(d_score, q)
            r["dv_sum"][:upto, :] += mm(prob.astype(bf16), grad)
            r["dq"][slot, rows, cols] = mm_tn(d_score, k).astype(bf16)

    def to_rows(kind, slot, heads, rows, width):
        swap.send(
            kind,
            lambda partner: r[heads].at[slot, token_rows(partner), :],
            lambda sender: r[rows].at[slot, :, head_cols(sender, width)],
        )
        r[rows][slot, :, head_cols(me, width)] = r[heads][slot, token_rows(me), :]

    def attention(slot):
        own[slot].wait()
        swap.take(slot, lambda sender: r["grad_in"].at[slot, token_rows(sender), :])
        attend_back(slot, 0)
        attend_back(slot, 1)
        r["dk"][slot] = r["dk_sum"][...].astype(bf16)
        r["dv"][slot] = r["dv_sum"][...].astype(bf16)
        to_rows(2 + 3 * slot, slot, "dq", "dq_rows", 256)
        to_rows(3 + 3 * slot, slot, "dk", "dk_rows", 128)
        to_rows(4 + 3 * slot, slot, "dv", "dv_rows", 128)

    gains = {}

    def rows():
        for name in LATE_LOADS:
            loads[name].wait()
        gains["attn"], gains["query"], gains["key"], _ = gain_rows(r["tiles_in"])
        r["x_in_turned"][...] = r["x_in_in"][...].astype(f32).T.astype(bf16)
        for slot in range(2):
            swap.take(2 + 3 * slot, lambda sender: r["dq_rows"].at[slot, :, head_cols(sender, 256)])
            swap.take(3 + 3 * slot, lambda sender: r["dk_rows"].at[slot, :, head_cols(sender, 128)])
            swap.take(4 + 3 * slot, lambda sender: r["dv_rows"].at[slot, :, head_cols(sender, 128)])
        r["d_x"][...] = jnp.zeros((256, 1024), f32)
        r["dg_query"][...] = jnp.zeros((1, 128), f32)
        r["dg_key"][...] = jnp.zeros((1, 128), f32)

    cos, sin = r["cos_in"], r["sin_in"]

    def project_back(d_flat, first):
        cols = pl.ds(pl.multiple_of(first, 128), 512)
        weights = r["buf_qkv"][:, :, :, :, :, cols].reshape(1024, 512)
        r["d_x"][...] += mm_nt(d_flat, weights)
        grad = mm(r["x_in_turned"][...], d_flat).astype(bf16)
        r["buf_qkv"][:, :, :, :, :, cols] = grad.reshape(2, 4, 2, 4, 16, 512)

    def head_tile(j, rows_ref, flat_ref, first, gain, dg_ref):
        cols = pl.ds(pl.multiple_of(j * 512, 128), 512)
        grads_in = rows_ref[:, :, cols].reshape(256, 512).astype(f32)
        flat = flat_ref[:, cols]
        done = []
        for h in range(4):
            e = grads_in[:, h * 128 : (h + 1) * 128]
            v = flat[:, h * 128 : (h + 1) * 128]
            e = e * cos[...] - pltpu.roll(e, 64, 1) * sin[...]
            scale = inv_rms(v)
            weighed = gain * e
            d = scale * weighed - v * (scale * scale * scale) * jnp.mean(v * weighed, axis=-1, keepdims=True)
            dg_ref[...] += jnp.sum(e * v * scale, axis=0, keepdims=True)
            done.append(d.astype(bf16))
        project_back(jnp.concatenate(done, axis=-1), first + j * 512)

    def query_tile(j, carry):
        head_tile(j, r["dq_rows"], r["q_flat_in"], 0, gains["query"], r["dg_query"])
        return carry

    def key_tile(j, carry):
        head_tile(j, r["dk_rows"], r["k_flat_in"], 2048, gains["key"], r["dg_key"])
        return carry

    def value_tile(j, carry):
        cols = pl.ds(pl.multiple_of(j * 512, 128), 512)
        project_back(r["dv_rows"][:, :, cols].reshape(256, 512), 3072 + j * 512)
        return carry

    def swap_cores(half):
        reduce.send(
            0, 36 + 6 * half,
            r["buf_qkv"].at[:, :, 1 - place.core, :, :, pl.ds(half * 2048, 2048)],
            reduce.total(0).at[half],
            place.to_core,
        )

    def queries():
        lax.fori_loop(0, 4, query_tile, 0)
        swap_cores(0)

    def keys_values():
        lax.fori_loop(0, 2, key_tile, 0)
        lax.fori_loop(0, 2, value_tile, 0)
        swap_cores(1)

    def join_cores():
        for half in range(2):
            reduce.take(0, 36 + 6 * half, reduce.total(0).at[half])
            accumulate(
                reduce.total(0).at[half],
                r["buf_qkv"].at[:, :, place.core, :, :, pl.ds(half * 2048, 2048)],
            )

    give = pltpu.make_async_copy(r["d_x"], r["d_input"], r["in_sem"].at[15])

    def input_grad():
        x, d_x = r["hidden_in"][...].reshape(256, 1024).astype(f32), r["d_x"][...]
        scale = inv_rms(x)
        weighed = gains["attn"] * d_x
        d_norm = scale * weighed - x * (scale * scale * scale) * jnp.mean(x * weighed, axis=-1, keepdims=True)
        dg_attn = jnp.sum(d_x * x * scale, axis=0, keepdims=True)
        r["d_x"][...] = r["d_residual_in"][...] + d_norm
        give.start()
        lines = [dg_attn[:, at * 128 : (at + 1) * 128] for at in range(8)]
        lines += [r["dg_query"][...], r["dg_key"][...]]
        lines += [r["dg_ffn_in"][:, at * 128 : (at + 1) * 128] for at in range(8)]
        lines += [jnp.zeros((6, 128), f32)]
        little.put(0, jnp.concatenate(lines, axis=0))

    def small(step):
        if step < 4:
            little.put(step + 1, little.sum(step))
        else:
            r["gains_sum"][...] = little.sum(4)

    for step in BACKWARD_ORDER:
        if step[0] == "attention":
            attention(step[1])
        elif step[0] == "rows":
            rows()
        elif step[0] == "queries":
            queries()
        elif step[0] == "keys_values":
            keys_values()
        elif step[0] == "join_cores":
            join_cores()
        elif step[0] == "input_grad":
            input_grad()
        elif step[0] == "small":
            small(step[1])
        else:
            stages(step)
    reduce.finish()
    swap.finish()
    give.wait()
    for g in range(4):
        pltpu.make_async_copy(reduce.result(g), outs[g], r["out_sem"].at[g]).wait()


def backward(inputs):
    def shape(*dims, dtype=bf16):
        return jax.ShapeDtypeStruct(dims, dtype)

    outs = [shape(256, 1024, dtype=f32), shape(24, 128, dtype=f32)] + [
        shape(2, 4, rows // 4, cols // 2) for rows, cols in zip(SHARD_ROWS, COLUMNS)
    ]
    vmem = pl.BlockSpec(memory_space=pltpu.VMEM)
    hbm = pl.BlockSpec(memory_space=pl.ANY)
    buffers = [
        pltpu.VMEM(dims, dtype)
        for dims, dtype in (
            ((2, 4, 2, 4, 16, 4096), bf16),
            ((2, 1024, 256), bf16),
            ((2, 1024, 128), bf16),
            ((2, 1024, 128), bf16),
            ((2, 1024, 256), bf16),
            ((2, 1024, 256), bf16),
            ((2, 1024, 128), bf16),
            ((2, 1024, 128), bf16),
            ((1024, 128), f32),
            ((1024, 128), f32),
            ((2, 128, 2048), bf16),
            ((2, 128, 1024), bf16),
            ((2, 128, 1024), bf16),
            ((256, 2048), f32),
            ((256, 1024), f32),
            ((256, 1024), bf16),
            ((2, 128, 1024), bf16),
            ((256, 1024), f32),
            ((256, 128), f32),
            ((256, 128), f32),
            ((2, 4, 2, 16, 128), bf16),
            ((1, 1024), f32),
            ((1024, 256), bf16),
            ((256, 1024), f32),
            ((1, 128), f32),
            ((1, 128), f32),
            ((5, 4, 24, 128), f32),
        )
    ]
    dma = pltpu.SemaphoreType.DMA
    sems = [
        dma((4, 44)),
        dma((4, 44)),
        dma((4,)),
        dma((5, 3)),
        dma((5, 3)),
        dma((4,)),
        dma((8, 7)),
        dma((8, 7)),
        dma((16,)),
    ]
    results = pl.pallas_call(
        functools.partial(backward_kernel),
        out_shape=outs,
        in_specs=[hbm] * len(BACKWARD_IN),
        out_specs=[hbm, vmem] + [hbm] * 4,
        scratch_shapes=reduce_scratch() + buffers + sems,
        compiler_params=pltpu.CompilerParams(
            collective_id=2, has_side_effects=True, vmem_limit_bytes=63 * 1024 * 1024
        ),
        name="backward",
    )(*[inputs[name] for name in BACKWARD_IN])
    return dict(zip(BACKWARD_OUT, results))


def finish_kernel(*refs):
    gq, gk, gv, go, gg, gu, gd, d_attn, d_query, d_key, d_ffn = refs[5:16]
    qkv, output, gate_up, down, gains, sem = refs[16:]
    copies = [pltpu.make_async_copy(refs[at], refs[16 + at], sem.at[at]) for at in range(5)]
    for copy in copies:
        copy.start()
    for copy in copies:
        copy.wait()
    gq[...] = qkv[0].astype(f32)
    gk[...] = qkv[1, :, :1024].astype(f32)
    gv[...] = qkv[1, :, 1024:].astype(f32)
    for half in range(2):
        cols = slice(half * 512, (half + 1) * 512)
        go[:, cols] = output[half].astype(f32)
        gd[:, cols] = down[half].astype(f32)
    gg[...] = gate_up[0].astype(f32)
    gu[...] = gate_up[1].astype(f32)
    dp = lax.axis_index("dp")
    row, lane = dp // 2, dp % 2 * 64
    for ref, at in ((d_attn, row), (d_ffn, 10 + row)):
        ref[...] = pltpu.roll(gains[pl.ds(at, 1), :], lane, 1)[:, :64]
    for ref, at in ((d_query, 8), (d_key, 9)):
        ref[...] = pltpu.roll(gains[at : at + 1, :], (128 - dp * 8) % 128, 1)[:, :8]


def finish(sums, gains):
    def shape(*dims):
        return jax.ShapeDtypeStruct(dims, f32)

    outs = [
        shape(64, 2048),
        shape(64, 1024),
        shape(64, 1024),
        shape(128, 1024),
        shape(64, 3072),
        shape(64, 3072),
        shape(192, 1024),
        shape(1, 64),
        shape(1, 8),
        shape(1, 8),
        shape(1, 64),
    ]
    vmem = pl.BlockSpec(memory_space=pltpu.VMEM)
    sums = [part.reshape(2, rows, cols // 2) for part, rows, cols in zip(sums, SHARD_ROWS, COLUMNS)]
    return pl.pallas_call(
        functools.partial(finish_kernel),
        out_shape=outs,
        in_specs=[pl.BlockSpec(memory_space=pl.ANY)] * 5,
        out_specs=[vmem] * 11,
        scratch_shapes=[pltpu.VMEM(part.shape, part.dtype) for part in (*sums, gains)]
        + [pltpu.SemaphoreType.DMA((5,))],
        compiler_params=pltpu.CompilerParams(vmem_limit_bytes=60 * 1024 * 1024),
        name="finish",
    )(*sums, gains)


def rotary_tables(positions):
    frequency = jnp.exp(jnp.arange(64, dtype=f32) * (-2.0 * math.log(rope_base) / 128))
    angles = positions.astype(f32)[:, None] * frequency[None, :]
    cos_half, sin_half = jnp.cos(angles), jnp.sin(angles)
    return (
        jnp.concatenate([cos_half, cos_half], axis=-1),
        jnp.concatenate([-sin_half, sin_half], axis=-1),
    )


def per_device(
    hidden_in,
    out_cotangent,
    slot_lengths,
    position_ids,
    attn_gain,
    w_query,
    key_weight,
    value_weight,
    query_gain,
    key_gain,
    w_output,
    ffn_gain,
    w_gate,
    w_up,
    w_down,
):
    dp = lax.axis_index("dp")
    lane = jnp.arange(128, dtype=jnp.int32)[None, :]
    wide = jnp.stack([attn_gain, ffn_gain])
    wide = jnp.where(lane // 64 == dp % 2, jnp.concatenate([wide, wide], axis=1), 0)
    narrow = jnp.where(lane // 8 == dp, jnp.tile(jnp.stack([query_gain, key_gain]), (1, 16)), 0)
    tile = jnp.concatenate([wide[:1], narrow, wide[1:], jnp.zeros((12, 128), bf16)], axis=0)
    valid = jnp.broadcast_to((slot_lengths - lax.axis_index("seq") * 128).astype(f32)[:, None, None], (2, 8, 128))
    cos, sin = rotary_tables(position_ids.reshape(256))
    shards = (w_query, key_weight, value_weight, w_output, w_gate, w_up, w_down)
    done = forward(shards, tile, hidden_in, out_cotangent, cos, sin, valid)
    done.update(hidden=hidden_in, cos=cos, sin=sin)
    for name, rows, cols in (("total_output", 32, 512), ("total_gate_up", 16, 3072), ("total_down", 48, 512)):
        done[name] = done[name].reshape(2, 2, 4, 4, rows, cols)
    done["weights_qkv"] = done["weights_qkv"].reshape(2, 4, 2, 4, 16, 4096)
    last = backward(done)
    sums = [last[name] for name in ("sum_qkv", "sum_output", "sum_gate_up", "sum_down")]
    d_input = last["d_input"].reshape(2, 128, 1024)
    gq, gk, gv, go, gg, gu, gd, *gains = finish(sums, last["gains_sum"])
    dg_attn, dg_query, dg_key, dg_ffn = [gain.reshape(-1) for gain in gains]
    return (done["out"], d_input, dg_attn, gq, gk, gv, dg_query, dg_key, go, dg_ffn, gg, gu, gd)


def solution(mesh):
    slots, rows, vector, matrix = P("dp", "seq", None), P("dp", "seq"), P("dp"), P("dp", None)
    in_specs = (
        slots,
        slots,
        vector,
        rows,
        vector,
        matrix,
        matrix,
        matrix,
        vector,
        vector,
        matrix,
        vector,
        matrix,
        matrix,
        matrix,
    )
    out_specs = (
        slots,
        slots,
        vector,
        matrix,
        matrix,
        matrix,
        vector,
        vector,
        matrix,
        vector,
        matrix,
        matrix,
        matrix,
    )
    return jax.shard_map(
        per_device, mesh=mesh, in_specs=in_specs, out_specs=out_specs, check_vma=False
    )
```
